32 devices in a mesh: groups: 2 (over x), gz: 16 (over z, y, core).
Axes of the slice: x: 2, y: 2, z: 4, core: 2. Of those that a mesh axis runs over, the one named last changes fastest.
Arguments:
- e_field: float32 [3, 32, 384, 256], P(None, 'gz', 'groups'), parts along dimension 2, may hold values from -6 to 6
- h_field: float32 [3, 32, 384, 256], P(None, 'gz', 'groups'), parts along dimension 2, may hold values from -6 to 6
- forward_field: float32 [3, 32, 384, 256], P(None, 'gz', 'groups'), parts along dimension 2, may hold values from -6 to 6
- permittivity: float32 [32, 384, 256], P('gz', 'groups'), parts along dimension 1, may hold values from 1 to 4
- conductivity: float32 [32, 384, 256], P('gz', 'groups'), parts along dimension 1, may hold values from 0.05 to 1
- owners: int32 [4096, 2], P('gz', 'groups'), parts along dimension 1, may hold values from 0 to 15; in each aligned block of 256 rows (0 to 255, 256 to 511, ...) at most 32 rows name the same one
- cells: int32 [4096, 2], P('gz', 'groups'), parts along dimension 1, may hold values from 0 to 98303
- amplitude: float32 [6, 4096], P('groups', 'gz'), parts along dimension 0, may hold values from -24 to 24
- timing: float32 [4, 2], P('groups'), parts along dimension 0, may hold values from 0.5 to 1.5
- bounds: int32 [6, 2], P('groups'), parts along dimension 0, may hold values from 0 to 256, as said below
Outputs:
- e_out: float32 [3, 32, 384, 256], P(None, 'gz', 'groups'), parts along dimension 2
- h_out: float32 [3, 32, 384, 256], P(None, 'gz', 'groups'), parts along dimension 2
- gradient: float32 [32, 384, 256], P('gz', 'groups'), parts along dimension 1
The draws below stay inside these ranges and needn't reach their ends.
There are 2 independent parts, one for each index of `groups`. The reference program is written for one: setup_inputs(seed, part) draws one part's arguments, and reference() takes and returns one part's arrays. A program takes and returns all parts, laid end to end along the dimension named above; each array names one. Nothing has to cross between parts.
Inputs may be any that keep to these rules, and one draw needn't show every extreme that they name: `owners`: in the rows of one device no slab is named by more than 32 entries, a bound that some block reaches. `cells`: entries may name the same cell; they add. `bounds`: along each dimension of n cells the lower bound lies in 0 .. n // 4 and the upper in n - n // 4 .. n.
All inputs are finite; a program needn't handle non-finite values.
Results may differ from the reference program's by a relative error of at most 0.0001.
Values sent between devices are 32-bit elements; how exact they have to be, the bound alone decides.
No kernel may reach another device: no remote copies, remote signals or barrier semaphores. Data moves between devices by JAX's collectives and lax.ppermute only.
A program may use at most 256 MiB of HBM per device.

```python
import math
import jax
import jax.numpy as jnp
import numpy as np
from jax import lax

NX = 192
NY = 256
S_DEV = 256
STEPS = 2
NZ = 32
CELLS_DEV = 98304
SOURCES = 4096
MOST = 32
N_GZ = 16


def draw_bounds(key, part):
    key = jax.random.fold_in(key, 5)
    first, second = jax.random.split(key)
    extent = jnp.array([NZ, NX, NY], dtype=jnp.int32)
    lower = jax.random.randint(first, (3,), 0, extent // 4 + 1)
    upper = extent - jax.random.randint(second, (3,), 0, extent // 4 + 1)
    return jnp.stack([lower, upper], axis=1).astype(jnp.int32)


def touch_ends(drawn, rng, smallest, top_value):
    index_at = [jax.random.randint(jax.random.fold_in(rng, axis), (), 0, length) for axis, length in enumerate(drawn.shape)]
    longest = drawn.shape.index(max(drawn.shape))
    next_to = index_at[:longest] + [(index_at[longest] + 1) % drawn.shape[longest]] + index_at[longest + 1:]
    return drawn.at[tuple(index_at)].set(smallest).at[tuple(next_to)].set(top_value)


def level_of(key, shape, pieces, least, high):
    gain, own = 1.0, jax.random.fold_in(key, 6)
    for position, shards_of in pieces:
        steps = jnp.exp(jax.random.uniform(jax.random.fold_in(own, position), (shards_of,), jnp.float32, least / len(pieces), high / len(pieces)))
        gain = gain * jnp.repeat(steps, shape[position] // shards_of).reshape([-1 if axis == position else 1 for axis in range(len(shape))])
    return gain


def deal_out(key, own, number, rows, number_of, top, reach, lean):
    sequence = jax.random.permutation(key, number_of)
    crowded, ordinary = load_shares(number_of, rows * top, reach, lean, True), load_shares(number_of, rows * top, reach, lean, False)
    places = jnp.arange(number_of)

    def named(sizes, turn):
        used = int((sizes > 0).sum())
        fixed = max(1, used // 4)
        moved = fixed + (places - fixed + turn * (used - fixed)) % max(1, number_of - fixed)
        return jnp.zeros((number_of,), jnp.int32).at[sequence[jnp.where(places < fixed, places, moved)]].set(jnp.asarray(sizes, jnp.int32))

    sizes = jnp.where(number % 4 == 0, named(crowded, number // 4), named(ordinary, number - number // 4 - 1))
    mixed = jax.random.permutation(jax.random.fold_in(own, 3), number_of)
    donor, sink = mixed[0:number_of // 2 * 2:2], mixed[1:number_of // 2 * 2:2]
    margin = jnp.minimum(sizes[donor] - 1, reach - sizes[sink]) // 2
    margin = jnp.where((donor == sequence[0]) | (sink == sequence[0]) | (sizes[sink] == 0), 0, jnp.maximum(margin, 0))
    moved = jax.random.randint(jax.random.fold_in(own, 4), (number_of // 2,), 0, 1 << 20) % (margin + 1)
    sizes = sizes.at[donor].add(-moved).at[sink].add(moved)
    members = jnp.searchsorted(jnp.cumsum(sizes), jnp.arange(rows * top), side="right").astype(jnp.int32)
    listing = members.reshape(top, rows).T
    listing = listing[jax.random.permutation(jax.random.fold_in(own, 1), rows)]
    turn = jax.random.randint(jax.random.fold_in(own, 2), (rows, 1), 0, top)
    return jnp.take_along_axis(listing, (jnp.arange(top)[None, :] + turn) % top, axis=1)


def load_shares(count, total, bound, skew, full):
    portions = [(1 << 20) // math.isqrt(grade ** skew) + 1 for grade in range(1, count + 1)]
    largest = bound if full else min(bound, max(-(-total // count), total * portions[0] // sum(portions)))
    least = 1 if total - largest >= count - 1 else 0
    given, surplus = [largest] + [least] * (count - 1), total - largest - least * (count - 1)
    while surplus > 0:
        candidates = [i for i in range(1, count) if given[i] < largest] or [i for i in range(1, count) if given[i] < bound]
        whole, remaining = sum([portions[i] for i in candidates]), surplus
        for i in candidates:
            more = min(bound - given[i], max(1, remaining * portions[i] // whole), surplus)
            given[i] = given[i] + more
            surplus = surplus - more
    return np.array(given)


def bell_draw(rng, shape, deviation, reach, cuts=(), held_as=jnp.bfloat16):
    values = jax.random.normal(rng, shape, jnp.float32) * deviation
    if len(cuts) > 0:
        values = level_of(rng, shape, cuts, -0.22, 0.18) * values
    return jnp.clip(values, min=-reach, max=reach).astype(held_as)


def setup_inputs(seed: int = 0, part: int = 0) -> dict:
    seeds = jax.random.split(jax.random.key(seed), 11)
    part_splits = jax.random.split(jax.random.fold_in(seeds[10], part), 11)
    e_field = bell_draw(part_splits[0], (3, NZ, NX, NY), 1.0, 6.0, ((1, 16),), jnp.float32)
    h_field = bell_draw(part_splits[1], (3, NZ, NX, NY), 1.0, 6.0, ((1, 16),), jnp.float32)
    forward_field = bell_draw(part_splits[2], (3, NZ, NX, NY), 1.0, 6.0, ((1, 16),), jnp.float32)
    permittivity = jnp.clip(jnp.exp(math.log(4.0) - 1.3862944 * jax.random.uniform(part_splits[3], (NZ, NX, NY), jnp.float32) ** level_of(part_splits[3], (NZ, NX, NY), ((0, 16),), -0.2, 0.2)), 1.0, 4.0)
    conductivity = jnp.clip(jnp.exp(math.log(1.0) - 2.9957323 * jax.random.uniform(part_splits[4], (NZ, NX, NY), jnp.float32) ** level_of(part_splits[4], (NZ, NX, NY), ((0, 16),), -0.2, 0.2)), 0.05, 1.0)
    owners_keys = jax.random.split(jax.random.fold_in(part_splits[5], 1), SOURCES // S_DEV)
    owners_turns = jax.random.permutation(jax.random.fold_in(part_splits[5], 3), SOURCES // S_DEV)
    owners = jax.vmap(lambda own, number: deal_out(jax.random.fold_in(part_splits[5], 2), own, number, S_DEV, N_GZ, 1, MOST, 2))(owners_keys, owners_turns).reshape((SOURCES, 1))
    cells = touch_ends(jax.random.randint(part_splits[6], (SOURCES, 1), 0, CELLS_DEV), jax.random.fold_in(part_splits[6], 1), 0, CELLS_DEV - 1).astype(jnp.int32)
    amplitude = bell_draw(part_splits[7], (3, SOURCES), 4.0, 24.0, ((1, 16),), jnp.float32)
    timing = jnp.clip(jax.random.uniform(part_splits[8], (2, STEPS), jnp.float32, 0.5, 1.5), 0.5, 1.5)
    bounds = draw_bounds(jax.random.fold_in(jax.random.fold_in(seeds[10], part), 71), part)
    return dict(e_field=e_field, h_field=h_field, forward_field=forward_field, permittivity=permittivity, conductivity=conductivity, owners=owners, cells=cells, amplitude=amplitude, timing=timing, bounds=bounds)


def ahead(field, axis, top):
    upper = lax.slice_in_dim(field, 1, field.shape[axis], axis=axis)
    return jnp.concatenate([upper, top], axis=axis) - field


def behind(field, axis, bottom):
    lower = lax.slice_in_dim(field, 0, field.shape[axis] - 1, axis=axis)
    return field - jnp.concatenate([bottom, lower], axis=axis)


def zero_layer(field, axis):
    return jnp.zeros_like(lax.slice_in_dim(field, 0, 1, axis=axis))


def curl_ahead(efield, top_x, top_y):
    ex, ey, ez = efield[0], efield[1], efield[2]
    cx = ahead(ez, 2, zero_layer(ez, 2)) - ahead(ey, 0, top_y)
    cy = ahead(ex, 0, top_x) - ahead(ez, 1, zero_layer(ez, 1))
    cz = ahead(ey, 1, zero_layer(ey, 1)) - ahead(ex, 2, zero_layer(ex, 2))
    return jnp.stack([cx, cy, cz])


def curl_behind(hfield, bottom_x, bottom_y):
    hx, hy, hz = hfield[0], hfield[1], hfield[2]
    cx = behind(hz, 2, zero_layer(hz, 2)) - behind(hy, 0, bottom_y)
    cy = behind(hx, 0, bottom_x) - behind(hz, 1, zero_layer(hz, 1))
    cz = behind(hy, 1, zero_layer(hy, 1)) - behind(hx, 2, zero_layer(hx, 2))
    return jnp.stack([cx, cy, cz])


def reference(e_field, h_field, forward_field, permittivity, conductivity, owners, cells, amplitude, timing, bounds):
    flat_index = (owners[:, 0] * CELLS_DEV + cells[:, 0]).astype(jnp.int32)
    source = jnp.zeros((3, NZ * NX * NY), jnp.float32).at[:, flat_index].add(amplitude)
    source = source.reshape(3, NZ, NX, NY)
    loss = conductivity / (2.0 * permittivity)
    coef_a = (1.0 - loss) / (1.0 + loss)
    coef_b = 0.5 / (permittivity * (1.0 + loss))
    zpos = jnp.arange(NZ, dtype=jnp.int32)[:, None, None]
    xpos = jnp.arange(NX, dtype=jnp.int32)[None, :, None]
    ypos = jnp.arange(NY, dtype=jnp.int32)[None, None, :]
    inside = (zpos >= bounds[0, 0]) & (zpos < bounds[0, 1]) & (xpos >= bounds[1, 0]) & (xpos < bounds[1, 1]) & (ypos >= bounds[2, 0]) & (ypos < bounds[2, 1])
    mask = inside.astype(jnp.float32)
    gradient = jnp.zeros((NZ, NX, NY), jnp.float32)
    efield, hfield = e_field, h_field
    empty = jnp.zeros((1, NX, NY), jnp.float32)
    for step in range(STEPS):
        hfield = hfield - 0.5 * curl_ahead(efield, empty, empty)
        efield = coef_a * efield + coef_b * (curl_behind(hfield, empty, empty) - timing[0, step] * source)
        gradient = gradient + timing[1, step] * mask * jnp.sum(efield * forward_field, axis=0)
    return efield, hfield, gradient
```

```python
import functools

import jax
import jax.numpy as jnp
from jax import lax
from jax.experimental import pallas as pl
from jax.experimental.pallas import tpu as pltpu
from jax.sharding import PartitionSpec as P

STEPS = 2
ROWS = 24
LANES = 128
HALF = 0.5
F32 = jnp.float32
BF16 = jnp.bfloat16
VMEM = pltpu.VMEM
SMEM = pltpu.SMEM


def lanes_of(v):
    return lax.broadcasted_iota(jnp.int32, v.shape, 1)


def ahead_y(v):
    last = v.shape[1] - 1
    return jnp.where(lanes_of(v) < last, pltpu.roll(v, last, axis=1), 0.0) - v


def behind_y(v):
    return v - jnp.where(lanes_of(v) > 0, pltpu.roll(v, 1, axis=1), 0.0)


class Chunk:
    def __init__(self, at, size, width_x):
        self.at, self.size, self.width = at, size, width_x

    def get(self, ref, *index):
        return ref[(*index, pl.ds(self.at, self.size), slice(None))]

    def put(self, ref, *index_and_value):
        *index, value = index_and_value
        ref[(*index, pl.ds(self.at, self.size), slice(None))] = value

    def ahead_x(self, ref, *index):
        here = self.get(ref, *index)
        after = pl.multiple_of(jnp.minimum(self.at + self.size, self.width - 8), 8)
        more = ref[(*index, pl.ds(after, 8), slice(None))]
        more = jnp.where(self.at + self.size < self.width, more, 0.0)
        both = jnp.concatenate([here, more], axis=0)
        return pltpu.roll(both, self.size + 7, axis=0)[: self.size] - here

    def behind_x(self, ref, *index):
        here = self.get(ref, *index)
        before = pl.multiple_of(jnp.maximum(self.at - 8, 0), 8)
        more = ref[(*index, pl.ds(before, 8), slice(None))]
        more = jnp.where(self.at > 0, more, 0.0)
        both = jnp.concatenate([more, here], axis=0)
        return here - pltpu.roll(both, 1, axis=0)[8:]


def over_rows(width_x, body):
    size = ROWS if width_x % ROWS == 0 else 8

    def step(i, carry):
        body(Chunk(pl.multiple_of(i * size, 8), size, width_x))
        return carry

    lax.fori_loop(0, width_x // size, step, 0)


def coefficient(c, eps_ref, sigma_ref, z):
    eps, sigma = c.get(eps_ref, z), c.get(sigma_ref, z)
    return 1.0 / (2.0 * eps + sigma), eps, sigma


def odd_device():
    return lax.rem(lax.axis_index("gz"), 2) == 1


def halves_first(e_ref, h_ref, eps_ref, sigma_ref, chip_ref, far_ref):
    top, width_x = e_ref.shape[1] - 1, e_ref.shape[2]
    odd = odd_device()

    def body(c):
        ez = c.get(e_ref, 2, top)
        hx = c.get(h_ref, 0, top) - HALF * (ahead_y(ez) + c.get(e_ref, 1, top))
        hy = c.get(h_ref, 1, top) + HALF * (c.get(e_ref, 0, top) + c.ahead_x(e_ref, 2, top))
        cb_top = coefficient(c, eps_ref, sigma_ref, top)[0]
        cb_low = coefficient(c, eps_ref, sigma_ref, 0)[0]
        upward = (hx, hy, cb_top)
        downward = (c.get(e_ref, 0, 0), c.get(e_ref, 1, 0), cb_low)
        for k in range(3):
            c.put(chip_ref, k, jnp.where(odd, downward[k], upward[k]))
            c.put(far_ref, k, jnp.where(odd, upward[k], downward[k]))

    over_rows(width_x, body)


def split3(v):
    one = v.astype(BF16)
    rest = v - one.astype(F32)
    two = rest.astype(BF16)
    three = (rest - two.astype(F32)).astype(BF16)
    return one, two, three


def pack_entries(owners_ref, cells_ref, amplitude_ref, packed_ref, slab, top, width_x, width_y, cap):
    peers, _, lanes = packed_ref.shape
    owner, cell, amp = owners_ref[...], cells_ref[...], amplitude_ref[...]
    entries = owner.shape[1]
    named = lax.broadcasted_iota(jnp.int32, (peers, entries), 0) == owner
    hot = named.astype(F32).astype(BF16)
    first = lax.broadcasted_iota(jnp.int32, (entries, entries), 0)
    second = lax.broadcasted_iota(jnp.int32, (entries, entries), 1)
    ahead = (first < second).astype(F32).astype(BF16)
    before = jnp.dot(hot, ahead, preferred_element_type=F32)
    rank = jnp.sum(jnp.where(named, before, 0.0), axis=0, keepdims=True).astype(jnp.int32)
    layer = width_x * width_y
    own = owner * lanes + rank
    above = jnp.where((cell >= top * layer) & (owner + 1 < peers), own + (lanes + cap), -1)
    below = jnp.where((cell < layer) & (owner > 0), own + (2 * cap - lanes), -1)
    line = cell // width_y
    column = cell - line * width_y
    rows = jnp.concatenate(
        [amp, line.astype(F32), column.astype(F32), jnp.zeros((3, entries), F32)], axis=0
    )
    one, two, three = split3(rows)
    values = jnp.concatenate(
        [one.astype(F32), two.astype(F32), three.astype(F32), jnp.zeros((8, entries), F32)], axis=0
    ).astype(BF16)
    slot = lax.broadcasted_iota(jnp.int32, (lanes, entries), 0)

    def body(d, carry):
        want = slot + d * lanes
        hit = (want == own) | (want == above) | (want == below)
        place = hit.astype(F32).astype(BF16)
        out = lax.dot_general(values, place, (((1,), (1,)), ((), ())), preferred_element_type=F32)
        packed_ref[d] = out[0:8] + out[8:16] + out[16:24]
        return carry

    lax.fori_loop(0, peers, body, 0)


def halves_second(
    cap,
    e_ref,
    h_ref,
    eps_ref,
    sigma_ref,
    owners_ref,
    cells_ref,
    amplitude_ref,
    chip_ref,
    far_ref,
    packed_ref,
    h1_ref,
    e1_ref,
    ca_ref,
    cb_ref,
):
    slab, width_x, width_y = e_ref.shape[1], e_ref.shape[2], e_ref.shape[3]
    top = slab - 1
    odd = odd_device()
    pack_entries(
        owners_ref, cells_ref, amplitude_ref, packed_ref, slab, top, width_x, width_y, cap
    )

    def magnetic(c):
        for z in range(slab):
            ex, ey, ez = (c.get(e_ref, k, z) for k in range(3))
            up_x = c.get(e_ref, 0, z + 1) - ex if z < top else -ex
            up_y = c.get(e_ref, 1, z + 1) - ey if z < top else -ey
            c.put(h1_ref, 0, z, c.get(h_ref, 0, z) - HALF * (ahead_y(ez) - up_y))
            c.put(h1_ref, 1, z, c.get(h_ref, 1, z) - HALF * (up_x - c.ahead_x(e_ref, 2, z)))
            c.put(h1_ref, 2, z, c.get(h_ref, 2, z) - HALF * (c.ahead_x(e_ref, 1, z) - ahead_y(ex)))

    over_rows(width_x, magnetic)

    def electric(c):
        for z in range(slab):
            cb, eps, sigma = coefficient(c, eps_ref, sigma_ref, z)
            ca = (2.0 * eps - sigma) * cb
            c.put(ca_ref, z, ca)
            c.put(cb_ref, z, cb)
            hx, hy, hz = (c.get(h1_ref, k, z) for k in range(3))
            by_x, by_y = behind_y(hx), behind_y(hz)
            if z > 0:
                down_x, down_y = hx - c.get(h1_ref, 0, z - 1), hy - c.get(h1_ref, 1, z - 1)
            else:
                down_x, down_y = hx, hy
            ex = ca * c.get(e_ref, 0, z) + cb * (by_y - down_y)
            ey = ca * c.get(e_ref, 1, z) + cb * (down_x - c.behind_x(h1_ref, 2, z))
            ez = ca * c.get(e_ref, 2, z) + cb * (c.behind_x(h1_ref, 1, z) - by_x)
            c.put(e1_ref, 0, z, ex)
            c.put(e1_ref, 1, z, ey)
            c.put(e1_ref, 2, z, ez)

    over_rows(width_x, electric)

    def boundary(c):
        ex, ey, ez = (c.get(e1_ref, k, top) for k in range(3))
        hx = c.get(h1_ref, 0, top) - HALF * (ahead_y(ez) + ey)
        hy = c.get(h1_ref, 1, top) + HALF * (ex + c.ahead_x(e1_ref, 2, top))
        upward = (hx, hy)
        downward = (c.get(e1_ref, 0, 0), c.get(e1_ref, 1, 0))
        for k in range(2):
            c.put(chip_ref, k, jnp.where(odd, downward[k], upward[k]))
            c.put(far_ref, k, jnp.where(odd, upward[k], downward[k]))

    over_rows(width_x, boundary)


def place_entries(cap, slab, got_ref, own_ref, below_ref, above_ref):
    peers, _, lanes = got_ref.shape
    width_x, width_y = own_ref.shape[2], own_ref.shape[3]
    group = LANES // cap
    part = lax.broadcasted_iota(jnp.int32, (8, LANES), 1) // cap

    def row_of(segment):
        blocks = []
        for g in range(0, peers, group):
            block = jnp.zeros((8, LANES), F32)
            for p in range(min(group, peers - g)):
                shift = ((p - segment) * cap) % LANES
                there = got_ref[g + p]
                there = pltpu.roll(there, shift, axis=1) if shift else there
                block = jnp.where(part == p, there, block)
            blocks.append(block)
        return jnp.concatenate(blocks, axis=1)

    def fill(segment, first_line, lines, comps, store):
        row = row_of(segment)
        count = row.shape[1]
        line = row[3:4].astype(jnp.int32) - first_line
        column = row[4:5].astype(jnp.int32)
        where_line = lax.broadcasted_iota(jnp.int32, (lines, count), 0) == line
        left = where_line.astype(F32).astype(BF16)
        where_column = lax.broadcasted_iota(jnp.int32, (width_y, count), 0) == column
        for k in range(comps):
            total = None
            for term in split3(row[k : k + 1]):
                right = jnp.where(where_column, term.astype(F32), 0.0).astype(BF16)
                out = lax.dot_general(
                    left, right, (((1,), (1,)), ((), ())), preferred_element_type=F32
                )
                total = out if total is None else total + out
            store(k, total)

    def store_own(k, total):
        for z in range(slab):
            own_ref[k, z] = total[z * width_x : (z + 1) * width_x]

    def store_below(k, total):
        below_ref[k] = total

    def store_above(k, total):
        above_ref[k] = total

    fill(0, 0, slab * width_x, 3, store_own)
    fill(1, (slab - 1) * width_x, width_x, 3, store_below)
    fill(2, 0, width_x, 2, store_above)


def inside(c, bounds_ref, z, slab, shape):
    deep = lax.axis_index("gz") * slab + z
    in_z = (deep >= bounds_ref[0, 0]) & (deep < bounds_ref[0, 1])
    line = lax.broadcasted_iota(jnp.int32, shape, 0) + c.at
    column = lax.broadcasted_iota(jnp.int32, shape, 1)
    keep = (line >= bounds_ref[1, 0]) & (line < bounds_ref[1, 1])
    keep = keep & (column >= bounds_ref[2, 0]) & (column < bounds_ref[2, 1])
    return jnp.where(keep & in_z, 1.0, 0.0)


def middle(
    e_ref,
    forward_ref,
    h1_ref,
    e1_ref,
    ca_ref,
    cb_ref,
    own_ref,
    sbelow_ref,
    sabove_ref,
    chip_ref,
    far_ref,
    timing_ref,
    bounds_ref,
    h2_ref,
    e2_ref,
    grad_ref,
    e1s,
    h1s,
    fs,
    h2a,
    dza,
):
    slab, width_x = e_ref.shape[1], e_ref.shape[2]
    top = slab - 1
    odd = odd_device()
    has_below = jnp.where(lax.axis_index("gz") > 0, 1.0, 0.0).astype(F32)
    wave0, wave1 = timing_ref[0, 0], timing_ref[0, 1]
    weight0, weight1 = timing_ref[1, 0], timing_ref[1, 1]

    def first(c):
        chip = [c.get(chip_ref, k) for k in range(3)]
        far = [c.get(far_ref, k) for k in range(3)]
        low = [jnp.where(odd, a, b) for a, b in zip(chip, far)]
        high = [jnp.where(odd, b, a) for a, b in zip(chip, far)]
        ex, ey = c.get(e_ref, 0, 0), c.get(e_ref, 1, 0)
        hax = has_below * (low[0] + HALF * ey)
        hay = has_below * (low[1] - HALF * ex)
        cb_a, cb_b = low[2], high[2]
        cb = [c.get(cb_ref, z) for z in range(slab)]
        e1 = [
            [c.get(e1_ref, k, z) - wave0 * cb[z] * c.get(own_ref, k, z) for k in range(3)]
            for z in range(slab)
        ]
        e1[0][0] = e1[0][0] + cb[0] * hay
        e1[0][1] = e1[0][1] - cb[0] * hax
        hx = c.get(h1_ref, 0, top) + HALF * high[1]
        hy = c.get(h1_ref, 1, top) - HALF * high[0]
        c.put(h1s, 0, hx)
        c.put(h1s, 1, hy)
        bx_far, bx_chip = c.behind_x(far_ref, 0), c.behind_x(chip_ref, 0)
        bx = jnp.where(odd, bx_far, bx_chip)
        e1[top][0] = e1[top][0] + HALF * cb[top] * high[0]
        e1[top][1] = e1[top][1] + HALF * cb[top] * high[1]
        e1[top][2] = e1[top][2] - HALF * cb[top] * (bx + behind_y(high[1]))
        c.put(fs, 0, cb_b * (hy - wave0 * c.get(sabove_ref, 0)))
        c.put(fs, 1, -cb_b * (hx + wave0 * c.get(sabove_ref, 1)))
        for z in range(slab):
            for k in range(3):
                c.put(e1s, k, z, e1[z][k])
        dx = cb_a * (HALF * ex - wave0 * c.get(sbelow_ref, 0))
        dy = cb_a * (HALF * ey - wave0 * c.get(sbelow_ref, 1))
        dz = -cb_a * (
            HALF * (c.behind_x(e_ref, 0, 0) + behind_y(ey)) + wave0 * c.get(sbelow_ref, 2)
        )
        c.put(dza, dz)
        c.put(h2a, 0, has_below * HALF * (ey - dy + e1[0][1] - ahead_y(dz)))
        c.put(h2a, 1, has_below * HALF * (dx - ex - e1[0][0]))

    over_rows(width_x, first)

    def second(c):
        c.put(h2a, 1, c.get(h2a, 1) + has_below * HALF * c.ahead_x(dza))
        for z in range(slab):
            ex, ey, ez = (c.get(e1s, k, z) for k in range(3))
            if z < top:
                up_x, up_y = c.get(e1s, 0, z + 1) - ex, c.get(e1s, 1, z + 1) - ey
                hx, hy = c.get(h1_ref, 0, z), c.get(h1_ref, 1, z)
            else:
                up_x, up_y = c.get(fs, 0) - ex, c.get(fs, 1) - ey
                hx, hy = c.get(h1s, 0), c.get(h1s, 1)
            c.put(h2_ref, 0, z, hx - HALF * (ahead_y(ez) - up_y))
            c.put(h2_ref, 1, z, hy - HALF * (up_x - c.ahead_x(e1s, 2, z)))
            hz = c.get(h1_ref, 2, z)
            c.put(h2_ref, 2, z, hz - HALF * (c.ahead_x(e1s, 1, z) - ahead_y(ex)))

    over_rows(width_x, second)

    def third(c):
        for z in range(slab):
            ca, cb = c.get(ca_ref, z), c.get(cb_ref, z)
            hx, hy, hz = (c.get(h2_ref, k, z) for k in range(3))
            if z > 0:
                down_x, down_y = hx - c.get(h2_ref, 0, z - 1), hy - c.get(h2_ref, 1, z - 1)
            else:
                down_x, down_y = hx - c.get(h2a, 0), hy - c.get(h2a, 1)
            curl = (
                behind_y(hz) - down_y,
                down_x - c.behind_x(h2_ref, 2, z),
                c.behind_x(h2_ref, 1, z) - behind_y(hx),
            )
            dot1, dot2 = 0.0, 0.0
            for k in range(3):
                e1 = c.get(e1s, k, z)
                e2 = ca * e1 + cb * (curl[k] - wave1 * c.get(own_ref, k, z))
                c.put(e2_ref, k, z, e2)
                fwd = c.get(forward_ref, k, z)
                dot1 = dot1 + e1 * fwd
                dot2 = dot2 + e2 * fwd
            mask = inside(c, bounds_ref, z, slab, ca.shape)
            c.put(grad_ref, z, mask * (weight0 * dot1 + weight1 * dot2))

    over_rows(width_x, third)


def last(
    forward_ref,
    h2_ref,
    e2_ref,
    gradp_ref,
    cb_ref,
    chip_ref,
    far_ref,
    timing_ref,
    bounds_ref,
    eout_ref,
    hout_ref,
    grad_ref,
):
    slab, width_x = e2_ref.shape[1], e2_ref.shape[2]
    top = slab - 1
    odd = odd_device()
    weight1 = timing_ref[1, 1]

    def body(c):
        chip = [c.get(chip_ref, k) for k in range(2)]
        far = [c.get(far_ref, k) for k in range(2)]
        low = [jnp.where(odd, a, b) for a, b in zip(chip, far)]
        high = [jnp.where(odd, b, a) for a, b in zip(chip, far)]
        bx = jnp.where(odd, c.behind_x(far_ref, 0), c.behind_x(chip_ref, 0))
        more = [[None] * 3 for _ in range(slab)]
        cb_low, cb_top = c.get(cb_ref, 0), HALF * c.get(cb_ref, top)
        more[0][0] = cb_low * low[1]
        more[0][1] = -cb_low * low[0]
        more[top][0] = cb_top * high[0]
        more[top][1] = cb_top * high[1]
        more[top][2] = -cb_top * (bx + behind_y(high[1]))
        for z in range(slab):
            dot = 0.0
            for k in range(3):
                e2 = c.get(e2_ref, k, z)
                if more[z][k] is not None:
                    e2 = e2 + more[z][k]
                    dot = dot + more[z][k] * c.get(forward_ref, k, z)
                c.put(eout_ref, k, z, e2)
            mask = inside(c, bounds_ref, z, slab, cb_low.shape)
            c.put(grad_ref, z, c.get(gradp_ref, z) + (weight1 * mask) * dot)
            hx, hy = c.get(h2_ref, 0, z), c.get(h2_ref, 1, z)
            if z == top:
                hx, hy = hx + HALF * high[1], hy - HALF * high[0]
            c.put(hout_ref, 0, z, hx)
            c.put(hout_ref, 1, z, hy)
            c.put(hout_ref, 2, z, c.get(h2_ref, 2, z))

    over_rows(width_x, body)


def shape(*dims):
    return jax.ShapeDtypeStruct(dims, F32)


def call(body, outs, ins, flops, scratch=()):
    total = sum(8 * x.size for x in jax.tree.leaves((outs, list(ins))))
    return pl.pallas_call(
        body,
        out_shape=outs,
        in_specs=[
            pl.BlockSpec(memory_space=SMEM if x.size < 16 else VMEM) for x in ins
        ],
        out_specs=jax.tree.map(lambda _: pl.BlockSpec(memory_space=VMEM), outs),
        scratch_shapes=list(scratch),
        compiler_params=pltpu.CompilerParams(vmem_limit_bytes=40 * 1024 * 1024),
        cost_estimate=pl.CostEstimate(flops=flops, bytes_accessed=total, transcendentals=0),
    )(*ins)


def local(
    e_field,
    h_field,
    forward_field,
    permittivity,
    conductivity,
    owners,
    cells,
    amplitude,
    timing,
    bounds,
):
    slab, wx, wy = permittivity.shape
    peers = lax.axis_size("gz")
    rows = owners.shape[0]
    cap = 2 * rows // peers
    lanes = -(-3 * cap // LANES) * LANES
    cells_all = slab * wx * wy
    chip_pairs = [p for i in range(0, peers - 1, 2) for p in ((i, i + 1), (i + 1, i))]
    far_pairs = [p for i in range(1, peers - 1, 2) for p in ((i, i + 1), (i + 1, i))]

    chip1, far1 = call(
        halves_first,
        (shape(3, wx, wy), shape(3, wx, wy)),
        (e_field, h_field, permittivity, conductivity),
        cells_all * 20,
    )
    far1 = lax.ppermute(far1, "gz", far_pairs)
    chip1 = lax.ppermute(chip1, "gz", chip_pairs)
    chip2, far2, packed, h1, e1, ca, cb = call(
        functools.partial(halves_second, cap),
        (
            shape(2, wx, wy),
            shape(2, wx, wy),
            shape(peers, 8, lanes),
            shape(3, slab, wx, wy),
            shape(3, slab, wx, wy),
            shape(slab, wx, wy),
            shape(slab, wx, wy),
        ),
        (
            e_field,
            h_field,
            permittivity,
            conductivity,
            owners.reshape(1, rows),
            cells.reshape(1, rows),
            amplitude,
        ),
        cells_all * 60,
    )
    got = lax.all_to_all(packed, "gz", 0, 0, tiled=True)
    far2 = lax.ppermute(far2, "gz", far_pairs)
    chip2 = lax.ppermute(chip2, "gz", chip_pairs)
    own, sbelow, sabove = call(
        functools.partial(place_entries, cap, slab),
        (shape(3, slab, wx, wy), shape(3, wx, wy), shape(2, wx, wy)),
        (got,),
        cells_all * 60,
    )
    h2, e2, grad = call(
        middle,
        (shape(3, slab, wx, wy), shape(3, slab, wx, wy), shape(slab, wx, wy)),
        (
            e_field,
            forward_field,
            h1,
            e1,
            ca,
            cb,
            own,
            sbelow,
            sabove,
            chip1,
            far1,
            timing,
            bounds,
        ),
        cells_all * 100,
        scratch=(
            VMEM((3, slab, wx, wy), F32),
            VMEM((2, wx, wy), F32),
            VMEM((2, wx, wy), F32),
            VMEM((2, wx, wy), F32),
            VMEM((wx, wy), F32),
        ),
    )
    return call(
        last,
        (shape(3, slab, wx, wy), shape(3, slab, wx, wy), shape(slab, wx, wy)),
        (forward_field, h2, e2, grad, cb, chip2, far2, timing, bounds),
        cells_all * 20,
    )


def solution(mesh):
    placed = (
        P(None, "gz", "groups", None),
        P(None, "gz", "groups", None),
        P(None, "gz", "groups", None),
        P("gz", "groups", None),
        P("gz", "groups", None),
        P("gz", "groups"),
        P("gz", "groups"),
        P("groups", "gz"),
        P("groups", None),
        P("groups", None),
    )
    return jax.shard_map(
        local,
        mesh=mesh,
        in_specs=placed,
        out_specs=(
            P(None, "gz", "groups", None),
            P(None, "gz", "groups", None),
            P("gz", "groups", None),
        ),
        check_vma=False,
    )
```

```python
import functools
import math

import jax
import jax.numpy as jnp
from jax import lax
from jax.experimental import pallas as pl
from jax.experimental.pallas import tpu as pltpu
from jax.sharding import PartitionSpec as P

STEPS = 2
ROWS = 24
PARTS = 4
LANES = 128
HALF = 0.5
F32 = jnp.float32
BF16 = jnp.bfloat16
VMEM = pltpu.VMEM
SMEM = pltpu.SMEM


def lanes_of(v):
    return lax.broadcasted_iota(jnp.int32, v.shape, 1)


def ahead_y(v):
    last = v.shape[1] - 1
    return jnp.where(lanes_of(v) < last, pltpu.roll(v, last, axis=1), 0.0) - v


def behind_y(v):
    return v - jnp.where(lanes_of(v) > 0, pltpu.roll(v, 1, axis=1), 0.0)


class Chunk:
    def __init__(self, at, size, width_x):
        self.at, self.size, self.width = at, size, width_x

    def get(self, ref, *index):
        return ref[(*index, pl.ds(self.at, self.size), slice(None))]

    def put(self, ref, *index_and_value):
        *index, value = index_and_value
        ref[(*index, pl.ds(self.at, self.size), slice(None))] = value

    def ahead_x(self, ref, *index):
        here = self.get(ref, *index)
        after = pl.multiple_of(jnp.minimum(self.at + self.size, self.width - 8), 8)
        more = ref[(*index, pl.ds(after, 8), slice(None))]
        more = jnp.where(self.at + self.size < self.width, more, 0.0)
        both = jnp.concatenate([here, more], axis=0)
        return pltpu.roll(both, self.size + 7, axis=0)[: self.size] - here

    def behind_x(self, ref, *index):
        here = self.get(ref, *index)
        before = pl.multiple_of(jnp.maximum(self.at - 8, 0), 8)
        more = ref[(*index, pl.ds(before, 8), slice(None))]
        more = jnp.where(self.at > 0, more, 0.0)
        both = jnp.concatenate([more, here], axis=0)
        return here - pltpu.roll(both, 1, axis=0)[8:]


def over_rows(width_x, body, begin=0, end=None):
    end = width_x if end is None else end
    size = ROWS if (end - begin) % ROWS == 0 else 8

    def step(i, carry):
        body(Chunk(pl.multiple_of(begin + i * size, 8), size, width_x))
        return carry

    lax.fori_loop(0, (end - begin) // size, step, 0)


def odd_device():
    return lax.rem(lax.axis_index("gz"), 2) == 1


def send_rows(g, part, chip_ref, far_ref, chip_hbm, far_hbm, sems):
    rows = pl.ds(g * part, part)
    far = pltpu.make_async_copy(far_ref.at[:, rows], far_hbm.at[:, rows], sems.at[g, 0])
    chip = pltpu.make_async_copy(chip_ref.at[:, rows], chip_hbm.at[:, rows], sems.at[g, 1])
    far.start()
    chip.start()
    return [far, chip]


def halves_first(
    e_hbm,
    h_hbm,
    eps_hbm,
    sigma_hbm,
    chip_hbm,
    far_hbm,
    e_ref,
    h_ref,
    low_ref,
    mat_ref,
    chip_ref,
    far_ref,
    sems,
    out_sems,
):
    slab, width_x = e_hbm.shape[1], e_hbm.shape[2]
    top = slab - 1
    odd = odd_device()
    part = width_x // PARTS
    copies = []
    for g in range(PARTS):
        rows = pl.ds(g * part, part)
        pairs = (
            (e_hbm.at[:, top, rows], e_ref.at[:, rows]),
            (h_hbm.at[0:2, top, rows], h_ref.at[:, rows]),
            (eps_hbm.at[:, rows], mat_ref.at[0, :, rows]),
            (sigma_hbm.at[:, rows], mat_ref.at[1, :, rows]),
            (e_hbm.at[0:2, 0, rows], low_ref.at[:, rows]),
        )
        copies.append(
            [pltpu.make_async_copy(a, b, sems.at[g, i]) for i, (a, b) in enumerate(pairs)]
        )
        for copy in copies[-1]:
            copy.start()

    def body(c):
        ez = c.get(e_ref, 2)
        hx = c.get(h_ref, 0) - HALF * (ahead_y(ez) + c.get(e_ref, 1))
        hy = c.get(h_ref, 1) + HALF * (c.get(e_ref, 0) + c.ahead_x(e_ref, 2))
        cb_top = 1.0 / (2.0 * c.get(mat_ref, 0, top) + c.get(mat_ref, 1, top))
        cb_low = 1.0 / (2.0 * c.get(mat_ref, 0, 0) + c.get(mat_ref, 1, 0))
        upward = (hx, hy, cb_top)
        downward = (c.get(low_ref, 0), c.get(low_ref, 1), cb_low)
        for k in range(3):
            c.put(chip_ref, k, jnp.where(odd, downward[k], upward[k]))
            c.put(far_ref, k, jnp.where(odd, upward[k], downward[k]))

    for copy in copies[0]:
        copy.wait()
    out = []
    for g in range(PARTS):
        if g + 1 < PARTS:
            for copy in copies[g + 1]:
                copy.wait()
        over_rows(width_x, body, g * part, (g + 1) * part)
        out = out + send_rows(g, part, chip_ref, far_ref, chip_hbm, far_hbm, out_sems)
    for copy in out:
        copy.wait()


def split3(v):
    one = v.astype(BF16)
    rest = v - one.astype(F32)
    two = rest.astype(BF16)
    three = (rest - two.astype(F32)).astype(BF16)
    return one, two, three


def pack_entries(cap, top, width_x, width_y, owners_ref, cells_ref, amplitude_ref, packed_ref):
    peers, _, lanes = packed_ref.shape
    owner, cell, amp = owners_ref[...], cells_ref[...], amplitude_ref[...]
    entries = owner.shape[1]
    named = lax.broadcasted_iota(jnp.int32, (peers, entries), 0) == owner
    hot = named.astype(F32).astype(BF16)
    first = lax.broadcasted_iota(jnp.int32, (entries, entries), 0)
    second = lax.broadcasted_iota(jnp.int32, (entries, entries), 1)
    ahead = (first < second).astype(F32).astype(BF16)
    before = jnp.dot(hot, ahead, preferred_element_type=F32)
    rank = jnp.sum(jnp.where(named, before, 0.0), axis=0, keepdims=True).astype(jnp.int32)
    layer = width_x * width_y
    own = owner * lanes + rank
    above = jnp.where((cell >= top * layer) & (owner + 1 < peers), own + (lanes + cap), -1)
    below = jnp.where((cell < layer) & (owner > 0), own + (2 * cap - lanes), -1)
    line = cell // width_y
    column = cell - line * width_y
    rows = jnp.concatenate(
        [amp, line.astype(F32), column.astype(F32), jnp.zeros((3, entries), F32)], axis=0
    )
    one, two, three = split3(rows)
    values = jnp.concatenate(
        [one.astype(F32), two.astype(F32), three.astype(F32), jnp.zeros((8, entries), F32)], axis=0
    ).astype(BF16)
    slot = lax.broadcasted_iota(jnp.int32, (lanes, entries), 0)

    def body(d, carry):
        want = slot + d * lanes
        hit = (want == own) | (want == above) | (want == below)
        place = hit.astype(F32).astype(BF16)
        out = lax.dot_general(values, place, (((1,), (1,)), ((), ())), preferred_element_type=F32)
        packed_ref[d] = out[0:8] + out[8:16] + out[16:24]
        return carry

    lax.fori_loop(0, peers, body, 0)


def magnetic_step(c, e_ref, h_ref, h1_ref):
    slab = e_ref.shape[1]
    for z in range(slab):
        ex, ey, ez = (c.get(e_ref, k, z) for k in range(3))
        up_x = c.get(e_ref, 0, z + 1) - ex if z + 1 < slab else -ex
        up_y = c.get(e_ref, 1, z + 1) - ey if z + 1 < slab else -ey
        c.put(h1_ref, 0, z, c.get(h_ref, 0, z) - HALF * (ahead_y(ez) - up_y))
        c.put(h1_ref, 1, z, c.get(h_ref, 1, z) - HALF * (up_x - c.ahead_x(e_ref, 2, z)))
        c.put(h1_ref, 2, z, c.get(h_ref, 2, z) - HALF * (c.ahead_x(e_ref, 1, z) - ahead_y(ex)))


def electric_step(c, z, comps, e_ref, h1_ref, ca, cb):
    hx, hy, hz = (c.get(h1_ref, k, z) for k in range(3))
    down_x = hx - c.get(h1_ref, 0, z - 1) if z > 0 else hx
    down_y = hy - c.get(h1_ref, 1, z - 1) if z > 0 else hy
    ex = ca * c.get(e_ref, 0, z) + cb * (behind_y(hz) - down_y)
    ey = ca * c.get(e_ref, 1, z) + cb * (down_x - c.behind_x(h1_ref, 2, z))
    if comps == 2:
        return ex, ey
    ez = ca * c.get(e_ref, 2, z) + cb * (c.behind_x(h1_ref, 1, z) - behind_y(hx))
    return ex, ey, ez


def coefficients(c, eps_ref, sigma_ref, z):
    eps, sigma = c.get(eps_ref, z), c.get(sigma_ref, z)
    cb = 1.0 / (2.0 * eps + sigma)
    return (2.0 * eps - sigma) * cb, cb


def halves_second(
    e_ref,
    h_ref,
    eps_ref,
    sigma_ref,
    packed_hbm,
    chip_hbm,
    far_hbm,
    h1_ref,
    e1_ref,
    low_ref,
    chip_ref,
    far_ref,
    out_sems,
):
    slab, width_x = e_ref.shape[1], e_ref.shape[2]
    top = slab - 1
    odd = odd_device()
    over_rows(width_x, lambda c: magnetic_step(c, e_ref, h_ref, h1_ref))

    def electric(c):
        for z, ref, comps in ((0, low_ref, 2), (top, e1_ref, 3)):
            ca, cb = coefficients(c, eps_ref, sigma_ref, z)
            for k, v in enumerate(electric_step(c, z, comps, e_ref, h1_ref, ca, cb)):
                c.put(ref, k, v)

    over_rows(width_x, electric)

    def boundary(c):
        ex, ey, ez = (c.get(e1_ref, k) for k in range(3))
        hx = c.get(h1_ref, 0, top) - HALF * (ahead_y(ez) + ey)
        hy = c.get(h1_ref, 1, top) + HALF * (ex + c.ahead_x(e1_ref, 2))
        upward = (hx, hy)
        downward = (c.get(low_ref, 0), c.get(low_ref, 1))
        for k in range(2):
            c.put(chip_ref, k, jnp.where(odd, downward[k], upward[k]))
            c.put(far_ref, k, jnp.where(odd, upward[k], downward[k]))

    part = width_x // PARTS
    out = []
    for g in range(PARTS):
        over_rows(width_x, boundary, g * part, (g + 1) * part)
        out = out + send_rows(g, part, chip_ref, far_ref, chip_hbm, far_hbm, out_sems)
    for copy in out:
        copy.wait()


def place_entries(
    cap,
    got_hbm,
    e_ref,
    h_ref,
    eps_ref,
    sigma_ref,
    timing_ref,
    own_ref,
    below_ref,
    above_ref,
    h1_ref,
    e1_ref,
    ca_ref,
    cb_ref,
    got_ref,
    sem,
):
    arrive = pltpu.make_async_copy(got_hbm, got_ref, sem)
    arrive.start()
    over_rows(e_ref.shape[2], lambda c: magnetic_step(c, e_ref, h_ref, h1_ref))
    arrive.wait()
    peers, _, lanes = got_ref.shape
    slab, width_x, width_y = own_ref.shape[1:]
    group = LANES // cap
    part = lax.broadcasted_iota(jnp.int32, (8, LANES), 1) // cap

    def row_of(segment):
        blocks = []
        for g in range(0, peers, group):
            block = jnp.zeros((8, LANES), F32)
            for p in range(min(group, peers - g)):
                shift = ((p - segment) * cap) % LANES
                there = got_ref[g + p]
                there = pltpu.roll(there, shift, axis=1) if shift else there
                block = jnp.where(part == p, there, block)
            blocks.append(block)
        return jnp.concatenate(blocks, axis=1)

    def fill(segment, first_line, lines, comps, store):
        row = row_of(segment)
        count = row.shape[1]
        line = row[3:4].astype(jnp.int32) - first_line
        column = row[4:5].astype(jnp.int32)
        where_line = lax.broadcasted_iota(jnp.int32, (lines, count), 0) == line
        left = where_line.astype(F32).astype(BF16)
        where_column = lax.broadcasted_iota(jnp.int32, (width_y, count), 0) == column
        for k in range(comps):
            total = None
            for term in split3(row[k : k + 1]):
                right = jnp.where(where_column, term.astype(F32), 0.0).astype(BF16)
                out = lax.dot_general(
                    left, right, (((1,), (1,)), ((), ())), preferred_element_type=F32
                )
                total = out if total is None else total + out
            store(k, total)

    def store_own(k, total):
        for z in range(slab):
            own_ref[k, z] = total[z * width_x : (z + 1) * width_x]

    def store_below(k, total):
        below_ref[k] = total

    def store_above(k, total):
        above_ref[k] = total

    fill(0, 0, slab * width_x, 3, store_own)
    fill(1, (slab - 1) * width_x, width_x, 3, store_below)
    fill(2, 0, width_x, 2, store_above)

    wave0 = timing_ref[0, 0]

    def electric(c):
        for z in range(slab):
            ca, cb = coefficients(c, eps_ref, sigma_ref, z)
            c.put(ca_ref, z, ca)
            c.put(cb_ref, z, cb)
            for k, v in enumerate(electric_step(c, z, 3, e_ref, h1_ref, ca, cb)):
                c.put(e1_ref, k, z, v - wave0 * cb * c.get(own_ref, k, z))

    over_rows(width_x, electric)


def inside(c, bounds_ref, z, slab, shape):
    deep = lax.axis_index("gz") * slab + z
    in_z = (deep >= bounds_ref[0, 0]) & (deep < bounds_ref[0, 1])
    line = lax.broadcasted_iota(jnp.int32, shape, 0) + c.at
    column = lax.broadcasted_iota(jnp.int32, shape, 1)
    keep = (line >= bounds_ref[1, 0]) & (line < bounds_ref[1, 1])
    keep = keep & (column >= bounds_ref[2, 0]) & (column < bounds_ref[2, 1])
    return jnp.where(keep & in_z, 1.0, 0.0)


def middle(
    e_ref,
    forward_ref,
    h1_ref,
    e1_ref,
    ca_ref,
    cb_ref,
    own_ref,
    sbelow_ref,
    sabove_ref,
    chip_ref,
    far_ref,
    timing_ref,
    bounds_ref,
    h2_ref,
    e2_ref,
    grad_ref,
    e1s,
    h1s,
    fs,
    h2a,
    dza,
):
    slab, width_x = e_ref.shape[1], e_ref.shape[2]
    top = slab - 1
    odd = odd_device()
    has_below = jnp.where(lax.axis_index("gz") > 0, 1.0, 0.0).astype(F32)
    wave0, wave1 = timing_ref[0, 0], timing_ref[0, 1]
    weight0, weight1 = timing_ref[1, 0], timing_ref[1, 1]

    def first(c):
        chip = [c.get(chip_ref, k) for k in range(3)]
        far = [c.get(far_ref, k) for k in range(3)]
        low = [jnp.where(odd, a, b) for a, b in zip(chip, far)]
        high = [jnp.where(odd, b, a) for a, b in zip(chip, far)]
        ex, ey = c.get(e_ref, 0, 0), c.get(e_ref, 1, 0)
        hax = has_below * (low[0] + HALF * ey)
        hay = has_below * (low[1] - HALF * ex)
        cb_a, cb_b = low[2], high[2]
        cb = [c.get(cb_ref, z) for z in range(slab)]
        e1 = [[c.get(e1_ref, k, z) for k in range(3)] for z in range(slab)]
        e1[0][0] = e1[0][0] + cb[0] * hay
        e1[0][1] = e1[0][1] - cb[0] * hax
        hx = c.get(h1_ref, 0, top) + HALF * high[1]
        hy = c.get(h1_ref, 1, top) - HALF * high[0]
        c.put(h1s, 0, hx)
        c.put(h1s, 1, hy)
        bx_far, bx_chip = c.behind_x(far_ref, 0), c.behind_x(chip_ref, 0)
        bx = jnp.where(odd, bx_far, bx_chip)
        e1[top][0] = e1[top][0] + HALF * cb[top] * high[0]
        e1[top][1] = e1[top][1] + HALF * cb[top] * high[1]
        e1[top][2] = e1[top][2] - HALF * cb[top] * (bx + behind_y(high[1]))
        c.put(fs, 0, cb_b * (hy - wave0 * c.get(sabove_ref, 0)))
        c.put(fs, 1, -cb_b * (hx + wave0 * c.get(sabove_ref, 1)))
        for z in range(slab):
            for k in range(3):
                c.put(e1s, k, z, e1[z][k])
        dx = cb_a * (HALF * ex - wave0 * c.get(sbelow_ref, 0))
        dy = cb_a * (HALF * ey - wave0 * c.get(sbelow_ref, 1))
        dz = -cb_a * (
            HALF * (c.behind_x(e_ref, 0, 0) + behind_y(ey)) + wave0 * c.get(sbelow_ref, 2)
        )
        c.put(dza, dz)
        c.put(h2a, 0, has_below * HALF * (ey - dy + e1[0][1] - ahead_y(dz)))
        c.put(h2a, 1, has_below * HALF * (dx - ex - e1[0][0]))

    over_rows(width_x, first)

    def second(c):
        c.put(h2a, 1, c.get(h2a, 1) + has_below * HALF * c.ahead_x(dza))
        for z in range(slab):
            ex, ey, ez = (c.get(e1s, k, z) for k in range(3))
            if z < top:
                up_x, up_y = c.get(e1s, 0, z + 1) - ex, c.get(e1s, 1, z + 1) - ey
                hx, hy = c.get(h1_ref, 0, z), c.get(h1_ref, 1, z)
            else:
                up_x, up_y = c.get(fs, 0) - ex, c.get(fs, 1) - ey
                hx, hy = c.get(h1s, 0), c.get(h1s, 1)
            c.put(h2_ref, 0, z, hx - HALF * (ahead_y(ez) - up_y))
            c.put(h2_ref, 1, z, hy - HALF * (up_x - c.ahead_x(e1s, 2, z)))
            hz = c.get(h1_ref, 2, z)
            c.put(h2_ref, 2, z, hz - HALF * (c.ahead_x(e1s, 1, z) - ahead_y(ex)))

    over_rows(width_x, second)

    def third(c):
        for z in range(slab):
            ca, cb = c.get(ca_ref, z), c.get(cb_ref, z)
            hx, hy, hz = (c.get(h2_ref, k, z) for k in range(3))
            if z > 0:
                down_x, down_y = hx - c.get(h2_ref, 0, z - 1), hy - c.get(h2_ref, 1, z - 1)
            else:
                down_x, down_y = hx - c.get(h2a, 0), hy - c.get(h2a, 1)
            curl = (
                behind_y(hz) - down_y,
                down_x - c.behind_x(h2_ref, 2, z),
                c.behind_x(h2_ref, 1, z) - behind_y(hx),
            )
            dot1, dot2 = 0.0, 0.0
            for k in range(3):
                e1 = c.get(e1s, k, z)
                e2 = ca * e1 + cb * (curl[k] - wave1 * c.get(own_ref, k, z))
                c.put(e2_ref, k, z, e2)
                fwd = c.get(forward_ref, k, z)
                dot1 = dot1 + e1 * fwd
                dot2 = dot2 + e2 * fwd
            mask = inside(c, bounds_ref, z, slab, ca.shape)
            c.put(grad_ref, z, mask * (weight0 * dot1 + weight1 * dot2))

    over_rows(width_x, third)


def last(
    forward_ref,
    h2_ref,
    e2_ref,
    gradp_ref,
    cb_ref,
    chip_ref,
    far_ref,
    timing_ref,
    bounds_ref,
    eout_hbm,
    hout_hbm,
    grad_hbm,
    e_ref,
    h_ref,
    grad_ref,
    sems,
    rest_sems,
):
    slab, width_x = e2_ref.shape[1], e2_ref.shape[2]
    top = slab - 1
    odd = odd_device()
    weight1 = timing_ref[1, 1]
    rest = [
        (h2_ref.at[0:2, 0:top], hout_hbm.at[0:2, 0:top]),
        (h2_ref.at[2], hout_hbm.at[2]),
        (e2_ref.at[2, 0:top], eout_hbm.at[2, 0:top]),
    ]
    rest = [pltpu.make_async_copy(a, b, rest_sems.at[i]) for i, (a, b) in enumerate(rest)]
    for copy in rest:
        copy.start()

    def body(c):
        chip = [c.get(chip_ref, k) for k in range(2)]
        far = [c.get(far_ref, k) for k in range(2)]
        low = [jnp.where(odd, a, b) for a, b in zip(chip, far)]
        high = [jnp.where(odd, b, a) for a, b in zip(chip, far)]
        bx = jnp.where(odd, c.behind_x(far_ref, 0), c.behind_x(chip_ref, 0))
        cb_low, cb_top = c.get(cb_ref, 0), HALF * c.get(cb_ref, top)
        more = [[0.0] * 3 for _ in range(slab)]
        more[0][0] = cb_low * low[1]
        more[0][1] = -cb_low * low[0]
        more[top][0] = more[top][0] + cb_top * high[0]
        more[top][1] = more[top][1] + cb_top * high[1]
        more[top][2] = -cb_top * (bx + behind_y(high[1]))
        for z in range(slab):
            dot = 0.0
            for k in range(3 if z == top else 2):
                delta = more[z][k]
                dot = dot + delta * c.get(forward_ref, k, z)
                c.put(e_ref, k, z, c.get(e2_ref, k, z) + delta)
            mask = inside(c, bounds_ref, z, slab, cb_low.shape)
            c.put(grad_ref, z, c.get(gradp_ref, z) + (weight1 * mask) * dot)
        c.put(h_ref, 0, c.get(h2_ref, 0, top) + HALF * high[1])
        c.put(h_ref, 1, c.get(h2_ref, 1, top) - HALF * high[0])

    part = width_x // PARTS
    copies = []
    for g in range(PARTS):
        over_rows(width_x, body, g * part, (g + 1) * part)
        rows = pl.ds(g * part, part)
        pairs = (
            (e_ref.at[0:2, :, rows], eout_hbm.at[0:2, :, rows]),
            (e_ref.at[2, top, rows], eout_hbm.at[2, top, rows]),
            (h_ref.at[:, rows], hout_hbm.at[0:2, top, rows]),
            (grad_ref.at[:, rows], grad_hbm.at[:, rows]),
        )
        for i, (a, b) in enumerate(pairs):
            copy = pltpu.make_async_copy(a, b, sems.at[g, i])
            copy.start()
            copies.append(copy)
    for copy in rest + copies:
        copy.wait()


def shape(*dims):
    return jax.ShapeDtypeStruct(dims, F32)


def kept(*dims):
    return VMEM(dims, F32)


def sent(*dims):
    return pltpu.HBM(dims, F32)


def call(body, outs, ins, flops, limit, scratch=(), in_hbm=(), anywhere=(), out_hbm=False):
    total = sum(
        4 * math.prod(x.shape) for x in jax.tree.leaves(outs) + list(ins)
    )

    def place(i, x):
        if i in in_hbm:
            return pl.BlockSpec(memory_space=pltpu.HBM)
        if i in anywhere:
            return pl.BlockSpec(memory_space=pl.ANY)
        return pl.BlockSpec(memory_space=SMEM if x.size < 16 else VMEM)

    ins = [
        pltpu.with_memory_space_constraint(x, pltpu.HBM) if i in in_hbm else x
        for i, x in enumerate(ins)
    ]
    return pl.pallas_call(
        body,
        out_shape=outs,
        in_specs=[place(i, x) for i, x in enumerate(ins)],
        out_specs=jax.tree.map(
            lambda _: pl.BlockSpec(memory_space=pltpu.HBM if out_hbm else VMEM), outs
        ),
        scratch_shapes=list(scratch),
        compiler_params=pltpu.CompilerParams(vmem_limit_bytes=limit << 20),
        cost_estimate=pl.CostEstimate(flops=flops, bytes_accessed=total, transcendentals=0),
    )(*ins)


def local(
    e_field,
    h_field,
    forward_field,
    permittivity,
    conductivity,
    owners,
    cells,
    amplitude,
    timing,
    bounds,
):
    slab, wx, wy = permittivity.shape
    peers = lax.axis_size("gz")
    rows = owners.shape[0]
    cap = 2 * rows // peers
    lanes = -(-3 * cap // LANES) * LANES
    cells_all = slab * wx * wy
    chip_pairs = [p for i in range(0, peers - 1, 2) for p in ((i, i + 1), (i + 1, i))]
    far_pairs = [p for i in range(1, peers - 1, 2) for p in ((i, i + 1), (i + 1, i))]

    chip1, far1 = call(
        halves_first,
        (sent(3, wx, wy), sent(3, wx, wy)),
        (e_field, h_field, permittivity, conductivity),
        cells_all * 20,
        8,
        scratch=(
            VMEM((3, wx, wy), F32),
            VMEM((2, wx, wy), F32),
            VMEM((2, wx, wy), F32),
            VMEM((2, slab, wx, wy), F32),
            VMEM((3, wx, wy), F32),
            VMEM((3, wx, wy), F32),
            pltpu.SemaphoreType.DMA((PARTS, 5)),
            pltpu.SemaphoreType.DMA((PARTS, 2)),
        ),
        in_hbm=(0, 1, 2, 3),
        out_hbm=True,
    )
    far1 = lax.ppermute(far1, "gz", far_pairs)
    chip1 = lax.ppermute(chip1, "gz", chip_pairs)
    packed = call(
        functools.partial(pack_entries, cap, slab - 1, wx, wy),
        shape(peers, 8, lanes),
        (owners.reshape(1, rows), cells.reshape(1, rows), amplitude),
        cells_all * 10,
        8,
    )
    got = lax.all_to_all(packed, "gz", 0, 0, tiled=True)
    chip2, far2 = call(
        halves_second,
        (sent(2, wx, wy), sent(2, wx, wy)),
        (e_field, h_field, permittivity, conductivity, packed),
        cells_all * 60,
        16,
        scratch=(
            VMEM((3, slab, wx, wy), F32),
            VMEM((3, wx, wy), F32),
            VMEM((2, wx, wy), F32),
            VMEM((2, wx, wy), F32),
            VMEM((2, wx, wy), F32),
            pltpu.SemaphoreType.DMA((PARTS, 2)),
        ),
        in_hbm=(4,),
        out_hbm=True,
    )
    _, far2, chip2 = lax.optimization_barrier((got, far2, chip2))
    far2 = lax.ppermute(far2, "gz", far_pairs)
    chip2 = lax.ppermute(chip2, "gz", chip_pairs)
    own, sbelow, sabove, h1, e1, ca, cb = call(
        functools.partial(place_entries, cap),
        (
            kept(3, slab, wx, wy),
            kept(3, wx, wy),
            kept(2, wx, wy),
            kept(3, slab, wx, wy),
            kept(3, slab, wx, wy),
            kept(slab, wx, wy),
            kept(slab, wx, wy),
        ),
        (got, e_field, h_field, permittivity, conductivity, timing),
        cells_all * 60,
        16,
        scratch=(VMEM((peers, 8, lanes), F32), pltpu.SemaphoreType.DMA),
        anywhere=(0,),
    )
    h2, e2, grad = call(
        middle,
        (kept(3, slab, wx, wy), kept(3, slab, wx, wy), kept(slab, wx, wy)),
        (
            e_field,
            forward_field,
            h1,
            e1,
            ca,
            cb,
            own,
            sbelow,
            sabove,
            chip1,
            far1,
            timing,
            bounds,
        ),
        cells_all * 100,
        24,
        scratch=(
            VMEM((3, slab, wx, wy), F32),
            VMEM((2, wx, wy), F32),
            VMEM((2, wx, wy), F32),
            VMEM((2, wx, wy), F32),
            VMEM((wx, wy), F32),
        ),
    )
    return call(
        last,
        (shape(3, slab, wx, wy), shape(3, slab, wx, wy), shape(slab, wx, wy)),
        (forward_field, h2, e2, grad, cb, chip2, far2, timing, bounds),
        cells_all * 20,
        16,
        scratch=(
            VMEM((3, slab, wx, wy), F32),
            VMEM((2, wx, wy), F32),
            VMEM((slab, wx, wy), F32),
            pltpu.SemaphoreType.DMA((PARTS, 4)),
            pltpu.SemaphoreType.DMA((3,)),
        ),
        out_hbm=True,
    )


def solution(mesh):
    placed = (
        P(None, "gz", "groups", None),
        P(None, "gz", "groups", None),
        P(None, "gz", "groups", None),
        P("gz", "groups", None),
        P("gz", "groups", None),
        P("gz", "groups"),
        P("gz", "groups"),
        P("groups", "gz"),
        P("groups", None),
        P("groups", None),
    )
    return jax.shard_map(
        local,
        mesh=mesh,
        in_specs=placed,
        out_specs=(
            P(None, "gz", "groups", None),
            P(None, "gz", "groups", None),
            P("gz", "groups", None),
        ),
        check_vma=False,
    )
```

```python
import functools

import jax
import jax.numpy as jnp
from jax import lax
from jax.experimental import pallas as pl
from jax.experimental.pallas import tpu as pltpu
from jax.sharding import PartitionSpec as P

STEPS = 2
ROWS = 24
PARTS = 4
FLOPS_US = 1.15e9
LANES = 128
HALF = 0.5
F32 = jnp.float32
BF16 = jnp.bfloat16
VMEM = pltpu.VMEM
SMEM = pltpu.SMEM


def lanes_of(v):
    return lax.broadcasted_iota(jnp.int32, v.shape, 1)


def ahead_y(v):
    last = v.shape[1] - 1
    return jnp.where(lanes_of(v) < last, pltpu.roll(v, last, axis=1), 0.0) - v


def behind_y(v):
    return v - jnp.where(lanes_of(v) > 0, pltpu.roll(v, 1, axis=1), 0.0)


class Chunk:
    def __init__(self, at, size, width_x):
        self.at, self.size, self.width = at, size, width_x

    def get(self, ref, *index):
        return ref[(*index, pl.ds(self.at, self.size), slice(None))]

    def put(self, ref, *index_and_value):
        *index, value = index_and_value
        ref[(*index, pl.ds(self.at, self.size), slice(None))] = value

    def ahead_x(self, ref, *index):
        here = self.get(ref, *index)
        after = pl.multiple_of(jnp.minimum(self.at + self.size, self.width - 8), 8)
        more = ref[(*index, pl.ds(after, 8), slice(None))]
        more = jnp.where(self.at + self.size < self.width, more, 0.0)
        both = jnp.concatenate([here, more], axis=0)
        return pltpu.roll(both, self.size + 7, axis=0)[: self.size] - here

    def behind_x(self, ref, *index):
        here = self.get(ref, *index)
        before = pl.multiple_of(jnp.maximum(self.at - 8, 0), 8)
        more = ref[(*index, pl.ds(before, 8), slice(None))]
        more = jnp.where(self.at > 0, more, 0.0)
        both = jnp.concatenate([more, here], axis=0)
        return here - pltpu.roll(both, 1, axis=0)[8:]


def over_rows(width_x, body, begin=0, end=None):
    end = width_x if end is None else end
    size = ROWS if (end - begin) % ROWS == 0 else 8

    def step(i, carry):
        body(Chunk(pl.multiple_of(begin + i * size, 8), size, width_x))
        return carry

    lax.fori_loop(0, (end - begin) // size, step, 0)


def odd_device():
    return lax.rem(lax.axis_index("gz"), 2) == 1


def send_rows(g, part, chip_ref, far_ref, chip_hbm, far_hbm, sems):
    rows = pl.ds(g * part, part)
    far = pltpu.make_async_copy(far_ref.at[:, rows], far_hbm.at[:, rows], sems.at[g, 0])
    chip = pltpu.make_async_copy(chip_ref.at[:, rows], chip_hbm.at[:, rows], sems.at[g, 1])
    far.start()
    chip.start()
    return [far, chip]


def halves_first(
    e_hbm,
    h_hbm,
    eps_hbm,
    sigma_hbm,
    chip_hbm,
    far_hbm,
    e_ref,
    h_ref,
    low_ref,
    mat_ref,
    chip_ref,
    far_ref,
    sems,
    out_sems,
):
    slab, width_x = e_hbm.shape[1], e_hbm.shape[2]
    top = slab - 1
    odd = odd_device()
    part = width_x // PARTS
    copies = []
    for g in range(PARTS):
        rows = pl.ds(g * part, part)
        pairs = (
            (e_hbm.at[:, top, rows], e_ref.at[:, rows]),
            (h_hbm.at[0:2, top, rows], h_ref.at[:, rows]),
            (eps_hbm.at[:, rows], mat_ref.at[0, :, rows]),
            (sigma_hbm.at[:, rows], mat_ref.at[1, :, rows]),
            (e_hbm.at[0:2, 0, rows], low_ref.at[:, rows]),
        )
        copies.append(
            [pltpu.make_async_copy(a, b, sems.at[g, i]) for i, (a, b) in enumerate(pairs)]
        )
        for copy in copies[-1]:
            copy.start()

    def body(c):
        ez = c.get(e_ref, 2)
        hx = c.get(h_ref, 0) - HALF * (ahead_y(ez) + c.get(e_ref, 1))
        hy = c.get(h_ref, 1) + HALF * (c.get(e_ref, 0) + c.ahead_x(e_ref, 2))
        cb_top = 1.0 / (2.0 * c.get(mat_ref, 0, top) + c.get(mat_ref, 1, top))
        cb_low = 1.0 / (2.0 * c.get(mat_ref, 0, 0) + c.get(mat_ref, 1, 0))
        upward = (hx, hy, cb_top)
        downward = (c.get(low_ref, 0), c.get(low_ref, 1), cb_low)
        for k in range(3):
            c.put(chip_ref, k, jnp.where(odd, downward[k], upward[k]))
            c.put(far_ref, k, jnp.where(odd, upward[k], downward[k]))

    for copy in copies[0]:
        copy.wait()
    out = []
    for g in range(PARTS):
        if g + 1 < PARTS:
            for copy in copies[g + 1]:
                copy.wait()
        over_rows(width_x, body, g * part, (g + 1) * part)
        out = out + send_rows(g, part, chip_ref, far_ref, chip_hbm, far_hbm, out_sems)
    for copy in out:
        copy.wait()


def split3(v):
    one = v.astype(BF16)
    rest = v - one.astype(F32)
    two = rest.astype(BF16)
    three = (rest - two.astype(F32)).astype(BF16)
    return one, two, three


def pack_entries(cap, top, width_x, width_y, owners_ref, cells_ref, amplitude_ref, after_hbm, packed_ref):
    peers, _, lanes = packed_ref.shape
    owner, cell, amp = owners_ref[...], cells_ref[...], amplitude_ref[...]
    entries = owner.shape[1]
    named = lax.broadcasted_iota(jnp.int32, (peers, entries), 0) == owner
    hot = named.astype(F32).astype(BF16)
    first = lax.broadcasted_iota(jnp.int32, (entries, entries), 0)
    second = lax.broadcasted_iota(jnp.int32, (entries, entries), 1)
    ahead = (first < second).astype(F32).astype(BF16)
    before = jnp.dot(hot, ahead, preferred_element_type=F32)
    rank = jnp.sum(jnp.where(named, before, 0.0), axis=0, keepdims=True).astype(jnp.int32)
    layer = width_x * width_y
    spread = lambda v: jnp.broadcast_to(v, (8, entries))
    names = (
        spread(owner),
        spread(jnp.where(cell >= top * layer, owner + 1, -1)),
        spread(jnp.where(cell < layer, owner - 1, -1)),
    )
    line = cell // width_y
    column = cell - line * width_y
    rows = jnp.concatenate(
        [amp, line.astype(F32), column.astype(F32), jnp.zeros((3, entries), F32)], axis=0
    )
    slot = lax.broadcasted_iota(jnp.int32, (lanes, entries), 0)
    hits = [(slot == rank + k * cap).astype(F32) for k in range(3)]
    place = jnp.concatenate(hits, axis=1).astype(BF16)
    total = None
    for term in split3(rows):
        term = term.astype(F32)
        values = [
            jnp.concatenate([jnp.where(name == d, term, 0.0) for d in range(peers)], axis=0)
            for name in names
        ]
        values = jnp.concatenate(values, axis=1).astype(BF16)
        out = lax.dot_general(values, place, (((1,), (1,)), ((), ())), preferred_element_type=F32)
        total = out if total is None else total + out
    for d in range(peers):
        packed_ref[d] = total[d * 8 : (d + 1) * 8]


def magnetic_step(c, e_ref, h_ref, h1_ref):
    slab = e_ref.shape[1]
    for z in range(slab):
        ex, ey, ez = (c.get(e_ref, k, z) for k in range(3))
        up_x = c.get(e_ref, 0, z + 1) - ex if z + 1 < slab else -ex
        up_y = c.get(e_ref, 1, z + 1) - ey if z + 1 < slab else -ey
        c.put(h1_ref, 0, z, c.get(h_ref, 0, z) - HALF * (ahead_y(ez) - up_y))
        c.put(h1_ref, 1, z, c.get(h_ref, 1, z) - HALF * (up_x - c.ahead_x(e_ref, 2, z)))
        c.put(h1_ref, 2, z, c.get(h_ref, 2, z) - HALF * (c.ahead_x(e_ref, 1, z) - ahead_y(ex)))


def electric_step(c, z, comps, e_ref, h1_ref, ca, cb):
    hx, hy, hz = (c.get(h1_ref, k, z) for k in range(3))
    down_x = hx - c.get(h1_ref, 0, z - 1) if z > 0 else hx
    down_y = hy - c.get(h1_ref, 1, z - 1) if z > 0 else hy
    ex = ca * c.get(e_ref, 0, z) + cb * (behind_y(hz) - down_y)
    ey = ca * c.get(e_ref, 1, z) + cb * (down_x - c.behind_x(h1_ref, 2, z))
    if comps == 2:
        return ex, ey
    ez = ca * c.get(e_ref, 2, z) + cb * (c.behind_x(h1_ref, 1, z) - behind_y(hx))
    return ex, ey, ez


def coefficients(c, eps_ref, sigma_ref, z):
    eps, sigma = c.get(eps_ref, z), c.get(sigma_ref, z)
    cb = 1.0 / (2.0 * eps + sigma)
    return (2.0 * eps - sigma) * cb, cb


def halves_second(
    e_ref,
    h_ref,
    eps_ref,
    sigma_ref,
    packed_hbm,
    chip_hbm,
    far_hbm,
    h1_ref,
    e1_ref,
    low_ref,
    chip_ref,
    far_ref,
    out_sems,
):
    slab, width_x = e_ref.shape[1], e_ref.shape[2]
    top = slab - 1
    odd = odd_device()
    over_rows(width_x, lambda c: magnetic_step(c, e_ref, h_ref, h1_ref))

    def electric(c):
        for z, ref, comps in ((0, low_ref, 2), (top, e1_ref, 3)):
            ca, cb = coefficients(c, eps_ref, sigma_ref, z)
            for k, v in enumerate(electric_step(c, z, comps, e_ref, h1_ref, ca, cb)):
                c.put(ref, k, v)

    over_rows(width_x, electric)

    def boundary(c):
        ex, ey, ez = (c.get(e1_ref, k) for k in range(3))
        hx = c.get(h1_ref, 0, top) - HALF * (ahead_y(ez) + ey)
        hy = c.get(h1_ref, 1, top) + HALF * (ex + c.ahead_x(e1_ref, 2))
        upward = (hx, hy)
        downward = (c.get(low_ref, 0), c.get(low_ref, 1))
        for k in range(2):
            c.put(chip_ref, k, jnp.where(odd, downward[k], upward[k]))
            c.put(far_ref, k, jnp.where(odd, upward[k], downward[k]))

    part = width_x // PARTS
    out = []
    for g in range(PARTS):
        over_rows(width_x, boundary, g * part, (g + 1) * part)
        out = out + send_rows(g, part, chip_ref, far_ref, chip_hbm, far_hbm, out_sems)
    for copy in out:
        copy.wait()


def first_step(
    e_ref,
    h_ref,
    eps_ref,
    sigma_ref,
    after_hbm,
    h1_hbm,
    e1_hbm,
    mat_hbm,
    h1_ref,
    e1_ref,
    mat_ref,
    h1_sem,
    sems,
):
    slab, width_x = e_ref.shape[1], e_ref.shape[2]
    over_rows(width_x, lambda c: magnetic_step(c, e_ref, h_ref, h1_ref))
    out = [pltpu.make_async_copy(h1_ref, h1_hbm, h1_sem)]
    out[0].start()

    def electric(c):
        for z in range(slab):
            ca, cb = coefficients(c, eps_ref, sigma_ref, z)
            c.put(mat_ref, 0, z, ca)
            c.put(mat_ref, 1, z, cb)
            for k, v in enumerate(electric_step(c, z, 3, e_ref, h1_ref, ca, cb)):
                c.put(e1_ref, k, z, v)

    part = width_x // PARTS
    for g in range(PARTS):
        over_rows(width_x, electric, g * part, (g + 1) * part)
        rows = pl.ds(g * part, part)
        pairs = (
            (e1_ref.at[:, :, rows], e1_hbm.at[:, :, rows]),
            (mat_ref.at[:, :, rows], mat_hbm.at[:, :, rows]),
        )
        for i, (a, b) in enumerate(pairs):
            out.append(pltpu.make_async_copy(a, b, sems.at[g, i]))
            out[-1].start()
    for copy in out:
        copy.wait()


def place_entries(cap, got_ref, own_ref, below_ref, above_ref):
    peers, _, lanes = got_ref.shape
    slab, width_x, width_y = own_ref.shape[1:]
    group = LANES // cap
    part = lax.broadcasted_iota(jnp.int32, (8, LANES), 1) // cap

    def row_of(segment):
        blocks = []
        for g in range(0, peers, group):
            block = jnp.zeros((8, LANES), F32)
            for p in range(min(group, peers - g)):
                shift = ((p - segment) * cap) % LANES
                there = got_ref[g + p]
                there = pltpu.roll(there, shift, axis=1) if shift else there
                block = jnp.where(part == p, there, block)
            blocks.append(block)
        return jnp.concatenate(blocks, axis=1)

    def fill(segment, first_line, lines, comps, store):
        row = row_of(segment)
        count = row.shape[1]
        line = row[3:4].astype(jnp.int32) - first_line
        column = row[4:5].astype(jnp.int32)
        where_line = lax.broadcasted_iota(jnp.int32, (lines, count), 0) == line
        left = where_line.astype(F32).astype(BF16)
        where_column = lax.broadcasted_iota(jnp.int32, (width_y, count), 0) == column
        for k in range(comps):
            total = None
            for term in split3(row[k : k + 1]):
                right = jnp.where(where_column, term.astype(F32), 0.0).astype(BF16)
                out = lax.dot_general(
                    left, right, (((1,), (1,)), ((), ())), preferred_element_type=F32
                )
                total = out if total is None else total + out
            store(k, total)

    def store_own(k, total):
        for z in range(slab):
            own_ref[k, z] = total[z * width_x : (z + 1) * width_x]

    def store_below(k, total):
        below_ref[k] = total

    def store_above(k, total):
        above_ref[k] = total

    fill(0, 0, slab * width_x, 3, store_own)
    fill(1, (slab - 1) * width_x, width_x, 3, store_below)
    fill(2, 0, width_x, 2, store_above)


def inside(c, bounds_ref, z, slab, shape):
    deep = lax.axis_index("gz") * slab + z
    in_z = (deep >= bounds_ref[0, 0]) & (deep < bounds_ref[0, 1])
    line = lax.broadcasted_iota(jnp.int32, shape, 0) + c.at
    column = lax.broadcasted_iota(jnp.int32, shape, 1)
    keep = (line >= bounds_ref[1, 0]) & (line < bounds_ref[1, 1])
    keep = keep & (column >= bounds_ref[2, 0]) & (column < bounds_ref[2, 1])
    return jnp.where(keep & in_z, 1.0, 0.0)


def middle(
    cap,
    e_ref,
    forward_hbm,
    got_ref,
    h1_hbm,
    e1_hbm,
    mat_hbm,
    chip_hbm,
    far_hbm,
    timing_ref,
    bounds_ref,
    h2_ref,
    e2_ref,
    grad_ref,
    cb_ref,
    forward_ref,
    h1_ref,
    e1_ref,
    mat_ref,
    chip_ref,
    far_ref,
    own_ref,
    sbelow_ref,
    sabove_ref,
    fs,
    h2a,
    dza,
    sems,
):
    pairs = (
        (far_hbm, far_ref),
        (chip_hbm, chip_ref),
        (e1_hbm, e1_ref),
        (h1_hbm, h1_ref),
        (mat_hbm, mat_ref),
        (forward_hbm, forward_ref),
    )
    copies = [pltpu.make_async_copy(a, b, sems.at[i]) for i, (a, b) in enumerate(pairs)]
    for copy in copies:
        copy.start()
    place_entries(cap, got_ref, own_ref, sbelow_ref, sabove_ref)
    for copy in copies[:-1]:
        copy.wait()
    slab, width_x = e_ref.shape[1], e_ref.shape[2]
    top = slab - 1
    odd = odd_device()
    has_below = jnp.where(lax.axis_index("gz") > 0, 1.0, 0.0).astype(F32)
    wave0, wave1 = timing_ref[0, 0], timing_ref[0, 1]
    weight0, weight1 = timing_ref[1, 0], timing_ref[1, 1]

    def first(c):
        chip = [c.get(chip_ref, k) for k in range(3)]
        far = [c.get(far_ref, k) for k in range(3)]
        low = [jnp.where(odd, a, b) for a, b in zip(chip, far)]
        high = [jnp.where(odd, b, a) for a, b in zip(chip, far)]
        ex, ey = c.get(e_ref, 0, 0), c.get(e_ref, 1, 0)
        hax = has_below * (low[0] + HALF * ey)
        hay = has_below * (low[1] - HALF * ex)
        cb_a, cb_b = low[2], high[2]
        cb = [c.get(mat_ref, 1, z) for z in range(slab)]
        e1 = [
            [c.get(e1_ref, k, z) - wave0 * cb[z] * c.get(own_ref, k, z) for k in range(3)]
            for z in range(slab)
        ]
        e1[0][0] = e1[0][0] + cb[0] * hay
        e1[0][1] = e1[0][1] - cb[0] * hax
        hx = c.get(h1_ref, 0, top) + HALF * high[1]
        hy = c.get(h1_ref, 1, top) - HALF * high[0]
        c.put(h1_ref, 0, top, hx)
        c.put(h1_ref, 1, top, hy)
        bx_far, bx_chip = c.behind_x(far_ref, 0), c.behind_x(chip_ref, 0)
        bx = jnp.where(odd, bx_far, bx_chip)
        e1[top][0] = e1[top][0] + HALF * cb[top] * high[0]
        e1[top][1] = e1[top][1] + HALF * cb[top] * high[1]
        e1[top][2] = e1[top][2] - HALF * cb[top] * (bx + behind_y(high[1]))
        c.put(fs, 0, cb_b * (hy - wave0 * c.get(sabove_ref, 0)))
        c.put(fs, 1, -cb_b * (hx + wave0 * c.get(sabove_ref, 1)))
        for z in range(slab):
            for k in range(3):
                c.put(e1_ref, k, z, e1[z][k])
        dx = cb_a * (HALF * ex - wave0 * c.get(sbelow_ref, 0))
        dy = cb_a * (HALF * ey - wave0 * c.get(sbelow_ref, 1))
        dz = -cb_a * (
            HALF * (c.behind_x(e_ref, 0, 0) + behind_y(ey)) + wave0 * c.get(sbelow_ref, 2)
        )
        c.put(dza, dz)
        c.put(h2a, 0, has_below * HALF * (ey - dy + e1[0][1] - ahead_y(dz)))
        c.put(h2a, 1, has_below * HALF * (dx - ex - e1[0][0]))

    over_rows(width_x, first)

    def second(c):
        c.put(h2a, 1, c.get(h2a, 1) + has_below * HALF * c.ahead_x(dza))
        for z in range(slab):
            ex, ey, ez = (c.get(e1_ref, k, z) for k in range(3))
            if z < top:
                up_x, up_y = c.get(e1_ref, 0, z + 1) - ex, c.get(e1_ref, 1, z + 1) - ey
            else:
                up_x, up_y = c.get(fs, 0) - ex, c.get(fs, 1) - ey
            hx, hy = c.get(h1_ref, 0, z), c.get(h1_ref, 1, z)
            c.put(h2_ref, 0, z, hx - HALF * (ahead_y(ez) - up_y))
            c.put(h2_ref, 1, z, hy - HALF * (up_x - c.ahead_x(e1_ref, 2, z)))
            hz = c.get(h1_ref, 2, z)
            c.put(h2_ref, 2, z, hz - HALF * (c.ahead_x(e1_ref, 1, z) - ahead_y(ex)))

    over_rows(width_x, second)

    def third(c):
        for z in range(slab):
            ca, cb = c.get(mat_ref, 0, z), c.get(mat_ref, 1, z)
            c.put(cb_ref, z, cb)
            hx, hy, hz = (c.get(h2_ref, k, z) for k in range(3))
            if z > 0:
                down_x, down_y = hx - c.get(h2_ref, 0, z - 1), hy - c.get(h2_ref, 1, z - 1)
            else:
                down_x, down_y = hx - c.get(h2a, 0), hy - c.get(h2a, 1)
            curl = (
                behind_y(hz) - down_y,
                down_x - c.behind_x(h2_ref, 2, z),
                c.behind_x(h2_ref, 1, z) - behind_y(hx),
            )
            dot1, dot2 = 0.0, 0.0
            for k in range(3):
                e1 = c.get(e1_ref, k, z)
                e2 = ca * e1 + cb * (curl[k] - wave1 * c.get(own_ref, k, z))
                c.put(e2_ref, k, z, e2)
                fwd = c.get(forward_ref, k, z)
                dot1 = dot1 + e1 * fwd
                dot2 = dot2 + e2 * fwd
            mask = inside(c, bounds_ref, z, slab, ca.shape)
            c.put(grad_ref, z, mask * (weight0 * dot1 + weight1 * dot2))

    copies[-1].wait()
    over_rows(width_x, third)


def last(
    forward_ref,
    h2_ref,
    e2_ref,
    gradp_ref,
    cb_ref,
    chip_hbm,
    far_hbm,
    timing_ref,
    bounds_ref,
    eout_hbm,
    hout_hbm,
    grad_hbm,
    chip_ref,
    far_ref,
    e_ref,
    h_ref,
    grad_ref,
    in_sems,
    sems,
    rest_sems,
):
    slab, width_x = e2_ref.shape[1], e2_ref.shape[2]
    top = slab - 1
    odd = odd_device()
    weight1 = timing_ref[1, 1]
    part = width_x // PARTS
    arriving = []
    for g in range(PARTS):
        rows = pl.ds(g * part, part)
        pairs = ((far_hbm, far_ref), (chip_hbm, chip_ref))
        arriving.append(
            [
                pltpu.make_async_copy(a.at[:, rows], b.at[:, rows], in_sems.at[g, i])
                for i, (a, b) in enumerate(pairs)
            ]
        )
        for copy in arriving[-1]:
            copy.start()
    rest = [
        (h2_ref.at[0:2, 0:top], hout_hbm.at[0:2, 0:top]),
        (h2_ref.at[2], hout_hbm.at[2]),
        (e2_ref.at[2, 0:top], eout_hbm.at[2, 0:top]),
    ]
    rest = [pltpu.make_async_copy(a, b, rest_sems.at[i]) for i, (a, b) in enumerate(rest)]
    for copy in rest:
        copy.start()

    def body(c):
        chip = [c.get(chip_ref, k) for k in range(2)]
        far = [c.get(far_ref, k) for k in range(2)]
        low = [jnp.where(odd, a, b) for a, b in zip(chip, far)]
        high = [jnp.where(odd, b, a) for a, b in zip(chip, far)]
        bx = jnp.where(odd, c.behind_x(far_ref, 0), c.behind_x(chip_ref, 0))
        cb_low, cb_top = c.get(cb_ref, 0), HALF * c.get(cb_ref, top)
        more = [[0.0] * 3 for _ in range(slab)]
        more[0][0] = cb_low * low[1]
        more[0][1] = -cb_low * low[0]
        more[top][0] = more[top][0] + cb_top * high[0]
        more[top][1] = more[top][1] + cb_top * high[1]
        more[top][2] = -cb_top * (bx + behind_y(high[1]))
        for z in range(slab):
            dot = 0.0
            for k in range(3 if z == top else 2):
                delta = more[z][k]
                dot = dot + delta * c.get(forward_ref, k, z)
                c.put(e_ref, k, z, c.get(e2_ref, k, z) + delta)
            mask = inside(c, bounds_ref, z, slab, cb_low.shape)
            c.put(grad_ref, z, c.get(gradp_ref, z) + (weight1 * mask) * dot)
        c.put(h_ref, 0, c.get(h2_ref, 0, top) + HALF * high[1])
        c.put(h_ref, 1, c.get(h2_ref, 1, top) - HALF * high[0])

    copies = []
    for g in range(PARTS):
        for copy in arriving[g]:
            copy.wait()
        over_rows(width_x, body, g * part, (g + 1) * part)
        rows = pl.ds(g * part, part)
        pairs = (
            (e_ref.at[0:2, :, rows], eout_hbm.at[0:2, :, rows]),
            (e_ref.at[2, top, rows], eout_hbm.at[2, top, rows]),
            (h_ref.at[:, rows], hout_hbm.at[0:2, top, rows]),
            (grad_ref.at[:, rows], grad_hbm.at[:, rows]),
        )
        for i, (a, b) in enumerate(pairs):
            copy = pltpu.make_async_copy(a, b, sems.at[g, i])
            copy.start()
            copies.append(copy)
    for copy in rest + copies:
        copy.wait()


def shape(*dims):
    return jax.ShapeDtypeStruct(dims, F32)


def kept(*dims):
    return VMEM(dims, F32)


def sent(*dims):
    return pltpu.HBM(dims, F32)


def call(body, outs, ins, us, limit, scratch=(), in_hbm=(), anywhere=(), out_hbm=False):
    def place(i, x):
        if i in in_hbm:
            return pl.BlockSpec(memory_space=pltpu.HBM)
        if i in anywhere:
            return pl.BlockSpec(memory_space=pl.ANY)
        return pl.BlockSpec(memory_space=SMEM if x.size < 16 else VMEM)

    ins = [
        pltpu.with_memory_space_constraint(x, pltpu.HBM) if i in in_hbm else x
        for i, x in enumerate(ins)
    ]
    return pl.pallas_call(
        body,
        out_shape=outs,
        in_specs=[place(i, x) for i, x in enumerate(ins)],
        out_specs=jax.tree.map(
            lambda _: pl.BlockSpec(memory_space=pltpu.HBM if out_hbm else VMEM), outs
        ),
        scratch_shapes=list(scratch),
        compiler_params=pltpu.CompilerParams(vmem_limit_bytes=limit << 20),
        cost_estimate=pl.CostEstimate(flops=int(us * FLOPS_US), bytes_accessed=0, transcendentals=0),
    )(*ins)


def local(
    e_field,
    h_field,
    forward_field,
    permittivity,
    conductivity,
    owners,
    cells,
    amplitude,
    timing,
    bounds,
):
    slab, wx, wy = permittivity.shape
    peers = lax.axis_size("gz")
    rows = owners.shape[0]
    cap = 2 * rows // peers
    lanes = -(-3 * cap // LANES) * LANES
    cells_all = slab * wx * wy
    chip_pairs = [p for i in range(0, peers - 1, 2) for p in ((i, i + 1), (i + 1, i))]
    far_pairs = [p for i in range(1, peers - 1, 2) for p in ((i, i + 1), (i + 1, i))]

    layer, slabs, fields = (wx, wy), (slab, wx, wy), (3, slab, wx, wy)
    dma = pltpu.SemaphoreType.DMA
    chip1, far1 = call(
        halves_first,
        (sent(3, *layer), sent(3, *layer)),
        (e_field, h_field, permittivity, conductivity),
        3,
        56,
        scratch=(
            VMEM((3, *layer), F32),
            VMEM((2, *layer), F32),
            VMEM((2, *layer), F32),
            VMEM((2, *slabs), F32),
            VMEM((3, *layer), F32),
            VMEM((3, *layer), F32),
            dma((PARTS, 5)),
            dma((PARTS, 2)),
        ),
        in_hbm=(0, 1, 2, 3),
        out_hbm=True,
    )
    begun = far1
    far1 = lax.ppermute(far1, "gz", far_pairs)
    chip1 = lax.ppermute(chip1, "gz", chip_pairs)
    packed = call(
        functools.partial(pack_entries, cap, slab - 1, wx, wy),
        shape(peers, 8, lanes),
        (owners.reshape(1, rows), cells.reshape(1, rows), amplitude, begun),
        1,
        8,
        in_hbm=(3,),
    )
    got = lax.all_to_all(packed, "gz", 0, 0, tiled=True)
    chip2, far2 = call(
        halves_second,
        (sent(2, *layer), sent(2, *layer)),
        (e_field, h_field, permittivity, conductivity, packed),
        3,
        16,
        scratch=(
            VMEM(fields, F32),
            VMEM((3, *layer), F32),
            VMEM((2, *layer), F32),
            VMEM((2, *layer), F32),
            VMEM((2, *layer), F32),
            dma((PARTS, 2)),
        ),
        in_hbm=(4,),
        out_hbm=True,
    )
    h1, e1, mat = call(
        first_step,
        (sent(*fields), sent(*fields), sent(2, *slabs)),
        (e_field, h_field, permittivity, conductivity, far2),
        3,
        16,
        scratch=(
            VMEM(fields, F32),
            VMEM(fields, F32),
            VMEM((2, *slabs), F32),
            dma,
            dma((PARTS, 2)),
        ),
        in_hbm=(4,),
        out_hbm=True,
    )
    far2 = lax.ppermute(far2, "gz", far_pairs)
    chip2 = lax.ppermute(chip2, "gz", chip_pairs)
    h2, e2, grad, cb, forward = call(
        functools.partial(middle, cap),
        (kept(*fields), kept(*fields), kept(*slabs), kept(*slabs), kept(*fields)),
        (e_field, forward_field, got, h1, e1, mat, chip1, far1, timing, bounds),
        6,
        24,
        scratch=(
            VMEM(fields, F32),
            VMEM(fields, F32),
            VMEM((2, *slabs), F32),
            VMEM((3, *layer), F32),
            VMEM((3, *layer), F32),
            VMEM(fields, F32),
            VMEM((3, *layer), F32),
            VMEM((2, *layer), F32),
            VMEM((2, *layer), F32),
            VMEM((2, *layer), F32),
            VMEM(layer, F32),
            dma((6,)),
        ),
        in_hbm=(1, 3, 4, 5),
        anywhere=(6, 7),
    )
    return call(
        last,
        (shape(*fields), shape(*fields), shape(*slabs)),
        (forward, h2, e2, grad, cb, chip2, far2, timing, bounds),
        2.5,
        16,
        scratch=(
            VMEM((2, *layer), F32),
            VMEM((2, *layer), F32),
            VMEM(fields, F32),
            VMEM((2, *layer), F32),
            VMEM(slabs, F32),
            dma((PARTS, 2)),
            dma((PARTS, 4)),
            dma((3,)),
        ),
        anywhere=(5, 6),
        out_hbm=True,
    )


def solution(mesh):
    placed = (
        P(None, "gz", "groups", None),
        P(None, "gz", "groups", None),
        P(None, "gz", "groups", None),
        P("gz", "groups", None),
        P("gz", "groups", None),
        P("gz", "groups"),
        P("gz", "groups"),
        P("groups", "gz"),
        P("groups", None),
        P("groups", None),
    )
    return jax.shard_map(
        local,
        mesh=mesh,
        in_specs=placed,
        out_specs=(
            P(None, "gz", "groups", None),
            P(None, "gz", "groups", None),
            P("gz", "groups", None),
        ),
        check_vma=False,
    )
```

```python
import functools

import jax
import jax.numpy as jnp
from jax import lax
from jax.experimental import pallas as pl
from jax.experimental.pallas import tpu as pltpu
from jax.sharding import PartitionSpec as P

STEPS = 2
ROWS = 24
PARTS = 4
FLOPS_US = 1.15e9
LANES = 128
HALF = 0.5
F32 = jnp.float32
BF16 = jnp.bfloat16
VMEM = pltpu.VMEM
SMEM = pltpu.SMEM


def lanes_of(v):
    return lax.broadcasted_iota(jnp.int32, v.shape, 1)


def ahead_y(v):
    last = v.shape[1] - 1
    return jnp.where(lanes_of(v) < last, pltpu.roll(v, last, axis=1), 0.0) - v


def behind_y(v):
    return v - jnp.where(lanes_of(v) > 0, pltpu.roll(v, 1, axis=1), 0.0)


class Chunk:
    def __init__(self, at, size, width_x):
        self.at, self.size, self.width = at, size, width_x

    def get(self, ref, *index):
        return ref[(*index, pl.ds(self.at, self.size), slice(None))]

    def put(self, ref, *index_and_value):
        *index, value = index_and_value
        ref[(*index, pl.ds(self.at, self.size), slice(None))] = value

    def ahead_x(self, ref, *index):
        here = self.get(ref, *index)
        after = pl.multiple_of(jnp.minimum(self.at + self.size, self.width - 8), 8)
        more = ref[(*index, pl.ds(after, 8), slice(None))]
        more = jnp.where(self.at + self.size < self.width, more, 0.0)
        both = jnp.concatenate([here, more], axis=0)
        return pltpu.roll(both, self.size + 7, axis=0)[: self.size] - here

    def behind_x(self, ref, *index):
        here = self.get(ref, *index)
        before = pl.multiple_of(jnp.maximum(self.at - 8, 0), 8)
        more = ref[(*index, pl.ds(before, 8), slice(None))]
        more = jnp.where(self.at > 0, more, 0.0)
        both = jnp.concatenate([more, here], axis=0)
        return here - pltpu.roll(both, 1, axis=0)[8:]


def over_rows(width_x, body, begin=0, end=None):
    end = width_x if end is None else end
    size = ROWS if (end - begin) % ROWS == 0 else 8

    def step(i, carry):
        body(Chunk(pl.multiple_of(begin + i * size, 8), size, width_x))
        return carry

    lax.fori_loop(0, (end - begin) // size, step, 0)


def odd_device():
    return lax.rem(lax.axis_index("gz"), 2) == 1


def send_rows(g, part, chip_ref, far_ref, chip_hbm, far_hbm, sems):
    rows = pl.ds(g * part, part)
    far = pltpu.make_async_copy(far_ref.at[:, rows], far_hbm.at[:, rows], sems.at[g, 0])
    chip = pltpu.make_async_copy(chip_ref.at[:, rows], chip_hbm.at[:, rows], sems.at[g, 1])
    far.start()
    chip.start()
    return [far, chip]


def halves_first(
    e_hbm,
    h_hbm,
    eps_hbm,
    sigma_hbm,
    chip_hbm,
    far_hbm,
    e_ref,
    h_ref,
    low_ref,
    mat_ref,
    chip_ref,
    far_ref,
    sems,
    out_sems,
):
    slab, width_x = e_hbm.shape[1], e_hbm.shape[2]
    top = slab - 1
    odd = odd_device()
    part = width_x // PARTS
    copies = []
    for g in range(PARTS):
        rows = pl.ds(g * part, part)
        pairs = (
            (e_hbm.at[:, top, rows], e_ref.at[:, rows]),
            (h_hbm.at[0:2, top, rows], h_ref.at[:, rows]),
            (eps_hbm.at[:, rows], mat_ref.at[0, :, rows]),
            (sigma_hbm.at[:, rows], mat_ref.at[1, :, rows]),
            (e_hbm.at[0:2, 0, rows], low_ref.at[:, rows]),
        )
        copies.append(
            [pltpu.make_async_copy(a, b, sems.at[g, i]) for i, (a, b) in enumerate(pairs)]
        )
        for copy in copies[-1]:
            copy.start()

    def body(c):
        ez = c.get(e_ref, 2)
        hx = c.get(h_ref, 0) - HALF * (ahead_y(ez) + c.get(e_ref, 1))
        hy = c.get(h_ref, 1) + HALF * (c.get(e_ref, 0) + c.ahead_x(e_ref, 2))
        cb_top = 1.0 / (2.0 * c.get(mat_ref, 0, top) + c.get(mat_ref, 1, top))
        cb_low = 1.0 / (2.0 * c.get(mat_ref, 0, 0) + c.get(mat_ref, 1, 0))
        upward = (hx, hy, cb_top)
        downward = (c.get(low_ref, 0), c.get(low_ref, 1), cb_low)
        for k in range(3):
            c.put(chip_ref, k, jnp.where(odd, downward[k], upward[k]))
            c.put(far_ref, k, jnp.where(odd, upward[k], downward[k]))

    for copy in copies[0]:
        copy.wait()
    out = []
    for g in range(PARTS):
        if g + 1 < PARTS:
            for copy in copies[g + 1]:
                copy.wait()
        over_rows(width_x, body, g * part, (g + 1) * part)
        out = out + send_rows(g, part, chip_ref, far_ref, chip_hbm, far_hbm, out_sems)
    for copy in out:
        copy.wait()


def split3(v):
    one = v.astype(BF16)
    rest = v - one.astype(F32)
    two = rest.astype(BF16)
    three = (rest - two.astype(F32)).astype(BF16)
    return one, two, three


def pack_entries(cap, top, width_x, width_y, owners_ref, cells_ref, amplitude_ref, after_hbm, packed_ref):
    peers, _, lanes = packed_ref.shape
    owner, cell, amp = owners_ref[...], cells_ref[...], amplitude_ref[...]
    entries = owner.shape[1]
    named = lax.broadcasted_iota(jnp.int32, (peers, entries), 0) == owner
    hot = named.astype(F32).astype(BF16)
    first = lax.broadcasted_iota(jnp.int32, (entries, entries), 0)
    second = lax.broadcasted_iota(jnp.int32, (entries, entries), 1)
    ahead = (first < second).astype(F32).astype(BF16)
    before = jnp.dot(hot, ahead, preferred_element_type=F32)
    rank = jnp.sum(jnp.where(named, before, 0.0), axis=0, keepdims=True).astype(jnp.int32)
    layer = width_x * width_y
    spread = lambda v: jnp.broadcast_to(v, (8, entries))
    names = (
        spread(owner),
        spread(jnp.where(cell >= top * layer, owner + 1, -1)),
        spread(jnp.where(cell < layer, owner - 1, -1)),
    )
    rows = jnp.concatenate([amp, cell.astype(F32), jnp.zeros((4, entries), F32)], axis=0)
    slot = lax.broadcasted_iota(jnp.int32, (lanes, entries), 0)
    hits = [(slot == rank + k * cap).astype(F32) for k in range(3)]
    place = jnp.concatenate(hits, axis=1).astype(BF16)
    total = None
    for term in split3(rows):
        term = term.astype(F32)
        values = [
            jnp.concatenate([jnp.where(name == d, term, 0.0) for d in range(peers)], axis=0)
            for name in names
        ]
        values = jnp.concatenate(values, axis=1).astype(BF16)
        out = lax.dot_general(values, place, (((1,), (1,)), ((), ())), preferred_element_type=F32)
        total = out if total is None else total + out
    for d in range(peers):
        packed_ref[d] = total[d * 8 : d * 8 + 4]


def magnetic_step(c, e_ref, h_ref, h1_ref):
    slab = e_ref.shape[1]
    for z in range(slab):
        ex, ey, ez = (c.get(e_ref, k, z) for k in range(3))
        up_x = c.get(e_ref, 0, z + 1) - ex if z + 1 < slab else -ex
        up_y = c.get(e_ref, 1, z + 1) - ey if z + 1 < slab else -ey
        c.put(h1_ref, 0, z, c.get(h_ref, 0, z) - HALF * (ahead_y(ez) - up_y))
        c.put(h1_ref, 1, z, c.get(h_ref, 1, z) - HALF * (up_x - c.ahead_x(e_ref, 2, z)))
        c.put(h1_ref, 2, z, c.get(h_ref, 2, z) - HALF * (c.ahead_x(e_ref, 1, z) - ahead_y(ex)))


def electric_step(c, z, comps, e_ref, h1_ref, ca, cb):
    hx, hy, hz = (c.get(h1_ref, k, z) for k in range(3))
    down_x = hx - c.get(h1_ref, 0, z - 1) if z > 0 else hx
    down_y = hy - c.get(h1_ref, 1, z - 1) if z > 0 else hy
    ex = ca * c.get(e_ref, 0, z) + cb * (behind_y(hz) - down_y)
    ey = ca * c.get(e_ref, 1, z) + cb * (down_x - c.behind_x(h1_ref, 2, z))
    if comps == 2:
        return ex, ey
    ez = ca * c.get(e_ref, 2, z) + cb * (c.behind_x(h1_ref, 1, z) - behind_y(hx))
    return ex, ey, ez


def halves_second(
    e_ref,
    h_ref,
    eps_hbm,
    sigma_hbm,
    packed_hbm,
    chip_hbm,
    far_hbm,
    h1_hbm,
    e1_hbm,
    mat_hbm,
    h1_ref,
    e1_ref,
    mat_ref,
    chip_ref,
    far_ref,
    in_sems,
    step_sems,
    out_sems,
):
    slab, width_x = e_ref.shape[1], e_ref.shape[2]
    top = slab - 1
    odd = odd_device()
    copies = [
        pltpu.make_async_copy(a, mat_ref.at[i], in_sems.at[i])
        for i, a in enumerate((eps_hbm, sigma_hbm))
    ]
    for copy in copies:
        copy.start()
    over_rows(width_x, lambda c: magnetic_step(c, e_ref, h_ref, h1_ref))
    out = [pltpu.make_async_copy(h1_ref, h1_hbm, step_sems.at[0])]
    out[0].start()
    for copy in copies:
        copy.wait()

    def electric(c):
        for z in range(slab):
            eps, sigma = c.get(mat_ref, 0, z), c.get(mat_ref, 1, z)
            cb = 1.0 / (2.0 * eps + sigma)
            ca = (2.0 * eps - sigma) * cb
            c.put(mat_ref, 0, z, ca)
            c.put(mat_ref, 1, z, cb)
            for k, v in enumerate(electric_step(c, z, 3, e_ref, h1_ref, ca, cb)):
                c.put(e1_ref, k, z, v)

    over_rows(width_x, electric)

    def boundary(c):
        ex, ey, ez = (c.get(e1_ref, k, top) for k in range(3))
        hx = c.get(h1_ref, 0, top) - HALF * (ahead_y(ez) + ey)
        hy = c.get(h1_ref, 1, top) + HALF * (ex + c.ahead_x(e1_ref, 2, top))
        upward = (hx, hy)
        downward = (c.get(e1_ref, 0, 0), c.get(e1_ref, 1, 0))
        for k in range(2):
            c.put(chip_ref, k, jnp.where(odd, downward[k], upward[k]))
            c.put(far_ref, k, jnp.where(odd, upward[k], downward[k]))

    part = width_x // PARTS
    for g in range(PARTS):
        over_rows(width_x, boundary, g * part, (g + 1) * part)
        out = out + send_rows(g, part, chip_ref, far_ref, chip_hbm, far_hbm, out_sems)
        if g == 0:
            for i, (a, b) in enumerate(((e1_ref, e1_hbm), (mat_ref, mat_hbm))):
                out.append(pltpu.make_async_copy(a, b, step_sems.at[1 + i]))
                out[-1].start()
    for copy in out:
        copy.wait()


def place_entries(cap, got_ref, own_ref, below_ref, above_ref):
    peers, _, lanes = got_ref.shape
    slab, width_x, width_y = own_ref.shape[1:]
    group = LANES // cap
    part = lax.broadcasted_iota(jnp.int32, (4, LANES), 1) // cap

    def row_of(segment):
        blocks = []
        for g in range(0, peers, group):
            block = jnp.zeros((4, LANES), F32)
            for p in range(min(group, peers - g)):
                shift = ((p - segment) * cap) % LANES
                there = got_ref[g + p]
                there = pltpu.roll(there, shift, axis=1) if shift else there
                block = jnp.where(part == p, there, block)
            blocks.append(block)
        return jnp.concatenate(blocks, axis=1)

    def fill(segment, first_line, lines, comps, store):
        row = row_of(segment)
        count = row.shape[1]
        cell = row[3:4].astype(jnp.int32)
        line = cell // width_y
        column = cell - line * width_y
        line = line - first_line
        where_line = lax.broadcasted_iota(jnp.int32, (lines, count), 0) == line
        left = where_line.astype(F32).astype(BF16)
        where_column = lax.broadcasted_iota(jnp.int32, (width_y, count), 0) == column
        for k in range(comps):
            total = None
            for term in split3(row[k : k + 1]):
                right = jnp.where(where_column, term.astype(F32), 0.0).astype(BF16)
                out = lax.dot_general(
                    left, right, (((1,), (1,)), ((), ())), preferred_element_type=F32
                )
                total = out if total is None else total + out
            store(k, total)

    def store_own(k, total):
        for z in range(slab):
            own_ref[k, z] = total[z * width_x : (z + 1) * width_x]

    def store_below(k, total):
        below_ref[k] = total

    def store_above(k, total):
        above_ref[k] = total

    fill(0, 0, slab * width_x, 3, store_own)
    fill(1, (slab - 1) * width_x, width_x, 3, store_below)
    fill(2, 0, width_x, 2, store_above)


def inside(c, bounds_ref, z, slab, shape):
    deep = lax.axis_index("gz") * slab + z
    in_z = (deep >= bounds_ref[0, 0]) & (deep < bounds_ref[0, 1])
    line = lax.broadcasted_iota(jnp.int32, shape, 0) + c.at
    column = lax.broadcasted_iota(jnp.int32, shape, 1)
    keep = (line >= bounds_ref[1, 0]) & (line < bounds_ref[1, 1])
    keep = keep & (column >= bounds_ref[2, 0]) & (column < bounds_ref[2, 1])
    return jnp.where(keep & in_z, 1.0, 0.0)


def middle(
    cap,
    e_ref,
    forward_hbm,
    got_ref,
    h1_hbm,
    e1_hbm,
    mat_hbm,
    chip_hbm,
    far_hbm,
    timing_ref,
    bounds_ref,
    h2_ref,
    e2_ref,
    grad_ref,
    cb_ref,
    forward_ref,
    h1_ref,
    e1_ref,
    mat_ref,
    chip_ref,
    far_ref,
    own_ref,
    sbelow_ref,
    sabove_ref,
    fs,
    h2a,
    dza,
    sems,
):
    pairs = (
        (far_hbm, far_ref),
        (chip_hbm, chip_ref),
        (e1_hbm, e1_ref),
        (h1_hbm, h1_ref),
        (mat_hbm, mat_ref),
        (forward_hbm, forward_ref),
    )
    copies = [pltpu.make_async_copy(a, b, sems.at[i]) for i, (a, b) in enumerate(pairs)]
    for copy in copies:
        copy.start()
    place_entries(cap, got_ref, own_ref, sbelow_ref, sabove_ref)
    for copy in copies[:-1]:
        copy.wait()
    slab, width_x = e_ref.shape[1], e_ref.shape[2]
    top = slab - 1
    odd = odd_device()
    has_below = jnp.where(lax.axis_index("gz") > 0, 1.0, 0.0).astype(F32)
    wave0, wave1 = timing_ref[0, 0], timing_ref[0, 1]
    weight0, weight1 = timing_ref[1, 0], timing_ref[1, 1]

    def first(c):
        chip = [c.get(chip_ref, k) for k in range(3)]
        far = [c.get(far_ref, k) for k in range(3)]
        low = [jnp.where(odd, a, b) for a, b in zip(chip, far)]
        high = [jnp.where(odd, b, a) for a, b in zip(chip, far)]
        ex, ey = c.get(e_ref, 0, 0), c.get(e_ref, 1, 0)
        hax = has_below * (low[0] + HALF * ey)
        hay = has_below * (low[1] - HALF * ex)
        cb_a, cb_b = low[2], high[2]
        cb = [c.get(mat_ref, 1, z) for z in range(slab)]
        e1 = [
            [c.get(e1_ref, k, z) - wave0 * cb[z] * c.get(own_ref, k, z) for k in range(3)]
            for z in range(slab)
        ]
        e1[0][0] = e1[0][0] + cb[0] * hay
        e1[0][1] = e1[0][1] - cb[0] * hax
        hx = c.get(h1_ref, 0, top) + HALF * high[1]
        hy = c.get(h1_ref, 1, top) - HALF * high[0]
        c.put(h1_ref, 0, top, hx)
        c.put(h1_ref, 1, top, hy)
        bx_far, bx_chip = c.behind_x(far_ref, 0), c.behind_x(chip_ref, 0)
        bx = jnp.where(odd, bx_far, bx_chip)
        e1[top][0] = e1[top][0] + HALF * cb[top] * high[0]
        e1[top][1] = e1[top][1] + HALF * cb[top] * high[1]
        e1[top][2] = e1[top][2] - HALF * cb[top] * (bx + behind_y(high[1]))
        c.put(fs, 0, cb_b * (hy - wave0 * c.get(sabove_ref, 0)))
        c.put(fs, 1, -cb_b * (hx + wave0 * c.get(sabove_ref, 1)))
        for z in range(slab):
            for k in range(3):
                c.put(e1_ref, k, z, e1[z][k])
        dx = cb_a * (HALF * ex - wave0 * c.get(sbelow_ref, 0))
        dy = cb_a * (HALF * ey - wave0 * c.get(sbelow_ref, 1))
        dz = -cb_a * (
            HALF * (c.behind_x(e_ref, 0, 0) + behind_y(ey)) + wave0 * c.get(sbelow_ref, 2)
        )
        c.put(dza, dz)
        c.put(h2a, 0, has_below * HALF * (ey - dy + e1[0][1] - ahead_y(dz)))
        c.put(h2a, 1, has_below * HALF * (dx - ex - e1[0][0]))

    over_rows(width_x, first)

    def second(c):
        c.put(h2a, 1, c.get(h2a, 1) + has_below * HALF * c.ahead_x(dza))
        for z in range(slab):
            ex, ey, ez = (c.get(e1_ref, k, z) for k in range(3))
            if z < top:
                up_x, up_y = c.get(e1_ref, 0, z + 1) - ex, c.get(e1_ref, 1, z + 1) - ey
            else:
                up_x, up_y = c.get(fs, 0) - ex, c.get(fs, 1) - ey
            hx, hy = c.get(h1_ref, 0, z), c.get(h1_ref, 1, z)
            c.put(h2_ref, 0, z, hx - HALF * (ahead_y(ez) - up_y))
            c.put(h2_ref, 1, z, hy - HALF * (up_x - c.ahead_x(e1_ref, 2, z)))
            hz = c.get(h1_ref, 2, z)
            c.put(h2_ref, 2, z, hz - HALF * (c.ahead_x(e1_ref, 1, z) - ahead_y(ex)))

    over_rows(width_x, second)

    def third(c):
        for z in range(slab):
            ca, cb = c.get(mat_ref, 0, z), c.get(mat_ref, 1, z)
            c.put(cb_ref, z, cb)
            hx, hy, hz = (c.get(h2_ref, k, z) for k in range(3))
            if z > 0:
                down_x, down_y = hx - c.get(h2_ref, 0, z - 1), hy - c.get(h2_ref, 1, z - 1)
            else:
                down_x, down_y = hx - c.get(h2a, 0), hy - c.get(h2a, 1)
            curl = (
                behind_y(hz) - down_y,
                down_x - c.behind_x(h2_ref, 2, z),
                c.behind_x(h2_ref, 1, z) - behind_y(hx),
            )
            dot1, dot2 = 0.0, 0.0
            for k in range(3):
                e1 = c.get(e1_ref, k, z)
                e2 = ca * e1 + cb * (curl[k] - wave1 * c.get(own_ref, k, z))
                c.put(e2_ref, k, z, e2)
                fwd = c.get(forward_ref, k, z)
                dot1 = dot1 + e1 * fwd
                dot2 = dot2 + e2 * fwd
            mask = inside(c, bounds_ref, z, slab, ca.shape)
            c.put(grad_ref, z, mask * (weight0 * dot1 + weight1 * dot2))

    copies[-1].wait()
    over_rows(width_x, third)


def last(
    forward_ref,
    h2_ref,
    e2_ref,
    gradp_ref,
    cb_ref,
    chip_hbm,
    far_hbm,
    timing_ref,
    bounds_ref,
    eout_hbm,
    hout_hbm,
    grad_hbm,
    chip_ref,
    far_ref,
    e_ref,
    h_ref,
    grad_ref,
    in_sems,
    sems,
    rest_sems,
):
    slab, width_x = e2_ref.shape[1], e2_ref.shape[2]
    top = slab - 1
    odd = odd_device()
    weight1 = timing_ref[1, 1]
    part = width_x // PARTS
    arriving = []
    for g in range(PARTS):
        rows = pl.ds(g * part, part)
        pairs = ((far_hbm, far_ref), (chip_hbm, chip_ref))
        arriving.append(
            [
                pltpu.make_async_copy(a.at[:, rows], b.at[:, rows], in_sems.at[g, i])
                for i, (a, b) in enumerate(pairs)
            ]
        )
        for copy in arriving[-1]:
            copy.start()
    rest = [
        (h2_ref.at[0:2, 0:top], hout_hbm.at[0:2, 0:top]),
        (h2_ref.at[2], hout_hbm.at[2]),
        (e2_ref.at[2, 0:top], eout_hbm.at[2, 0:top]),
    ]
    rest = [pltpu.make_async_copy(a, b, rest_sems.at[i]) for i, (a, b) in enumerate(rest)]
    for copy in rest:
        copy.start()

    def body(c):
        chip = [c.get(chip_ref, k) for k in range(2)]
        far = [c.get(far_ref, k) for k in range(2)]
        low = [jnp.where(odd, a, b) for a, b in zip(chip, far)]
        high = [jnp.where(odd, b, a) for a, b in zip(chip, far)]
        bx = jnp.where(odd, c.behind_x(far_ref, 0), c.behind_x(chip_ref, 0))
        cb_low, cb_top = c.get(cb_ref, 0), HALF * c.get(cb_ref, top)
        more = [[0.0] * 3 for _ in range(slab)]
        more[0][0] = cb_low * low[1]
        more[0][1] = -cb_low * low[0]
        more[top][0] = more[top][0] + cb_top * high[0]
        more[top][1] = more[top][1] + cb_top * high[1]
        more[top][2] = -cb_top * (bx + behind_y(high[1]))
        for z in range(slab):
            dot = 0.0
            for k in range(3 if z == top else 2):
                delta = more[z][k]
                dot = dot + delta * c.get(forward_ref, k, z)
                c.put(e_ref, k, z, c.get(e2_ref, k, z) + delta)
            mask = inside(c, bounds_ref, z, slab, cb_low.shape)
            c.put(grad_ref, z, c.get(gradp_ref, z) + (weight1 * mask) * dot)
        c.put(h_ref, 0, c.get(h2_ref, 0, top) + HALF * high[1])
        c.put(h_ref, 1, c.get(h2_ref, 1, top) - HALF * high[0])

    copies = []
    for g in range(PARTS):
        for copy in arriving[g]:
            copy.wait()
        over_rows(width_x, body, g * part, (g + 1) * part)
        rows = pl.ds(g * part, part)
        pairs = (
            (e_ref.at[0:2, :, rows], eout_hbm.at[0:2, :, rows]),
            (e_ref.at[2, top, rows], eout_hbm.at[2, top, rows]),
            (h_ref.at[:, rows], hout_hbm.at[0:2, top, rows]),
            (grad_ref.at[:, rows], grad_hbm.at[:, rows]),
        )
        for i, (a, b) in enumerate(pairs):
            copy = pltpu.make_async_copy(a, b, sems.at[g, i])
            copy.start()
            copies.append(copy)
    for copy in rest + copies:
        copy.wait()


def shape(*dims):
    return jax.ShapeDtypeStruct(dims, F32)


def kept(*dims):
    return VMEM(dims, F32)


def sent(*dims):
    return pltpu.HBM(dims, F32)


def call(body, outs, ins, us, limit, scratch=(), in_hbm=(), anywhere=(), out_hbm=False):
    def place(i, x):
        if i in in_hbm:
            return pl.BlockSpec(memory_space=pltpu.HBM)
        if i in anywhere:
            return pl.BlockSpec(memory_space=pl.ANY)
        return pl.BlockSpec(memory_space=SMEM if x.size < 16 else VMEM)

    ins = [
        pltpu.with_memory_space_constraint(x, pltpu.HBM) if i in in_hbm else x
        for i, x in enumerate(ins)
    ]
    return pl.pallas_call(
        body,
        out_shape=outs,
        in_specs=[place(i, x) for i, x in enumerate(ins)],
        out_specs=jax.tree.map(
            lambda _: pl.BlockSpec(memory_space=pltpu.HBM if out_hbm else VMEM), outs
        ),
        scratch_shapes=list(scratch),
        compiler_params=pltpu.CompilerParams(vmem_limit_bytes=limit << 20),
        cost_estimate=pl.CostEstimate(flops=int(us * FLOPS_US), bytes_accessed=0, transcendentals=0),
    )(*ins)


def local(
    e_field,
    h_field,
    forward_field,
    permittivity,
    conductivity,
    owners,
    cells,
    amplitude,
    timing,
    bounds,
):
    slab, wx, wy = permittivity.shape
    peers = lax.axis_size("gz")
    rows = owners.shape[0]
    cap = 2 * rows // peers
    lanes = -(-3 * cap // LANES) * LANES
    cells_all = slab * wx * wy
    chip_pairs = [p for i in range(0, peers - 1, 2) for p in ((i, i + 1), (i + 1, i))]
    far_pairs = [p for i in range(1, peers - 1, 2) for p in ((i, i + 1), (i + 1, i))]

    layer, slabs, fields = (wx, wy), (slab, wx, wy), (3, slab, wx, wy)
    dma = pltpu.SemaphoreType.DMA
    chip1, far1 = call(
        halves_first,
        (sent(3, *layer), sent(3, *layer)),
        (e_field, h_field, permittivity, conductivity),
        3,
        56,
        scratch=(
            VMEM((3, *layer), F32),
            VMEM((2, *layer), F32),
            VMEM((2, *layer), F32),
            VMEM((2, *slabs), F32),
            VMEM((3, *layer), F32),
            VMEM((3, *layer), F32),
            dma((PARTS, 5)),
            dma((PARTS, 2)),
        ),
        in_hbm=(0, 1, 2, 3),
        out_hbm=True,
    )
    begun = far1
    far1 = lax.ppermute(far1, "gz", far_pairs)
    chip1 = lax.ppermute(chip1, "gz", chip_pairs)
    packed = call(
        functools.partial(pack_entries, cap, slab - 1, wx, wy),
        shape(peers, 4, lanes),
        (owners.reshape(1, rows), cells.reshape(1, rows), amplitude, begun),
        1,
        8,
        in_hbm=(3,),
    )
    got = lax.all_to_all(packed, "gz", 0, 0, tiled=True)
    chip2, far2, h1, e1, mat = call(
        halves_second,
        (sent(2, *layer), sent(2, *layer), sent(*fields), sent(*fields), sent(2, *slabs)),
        (e_field, h_field, permittivity, conductivity, packed),
        3,
        16,
        scratch=(
            VMEM(fields, F32),
            VMEM(fields, F32),
            VMEM((2, *slabs), F32),
            VMEM((2, *layer), F32),
            VMEM((2, *layer), F32),
            dma((2,)),
            dma((3,)),
            dma((PARTS, 2)),
        ),
        in_hbm=(2, 3, 4),
        out_hbm=True,
    )
    far2 = lax.ppermute(far2, "gz", far_pairs)
    chip2 = lax.ppermute(chip2, "gz", chip_pairs)
    h2, e2, grad, cb, forward = call(
        functools.partial(middle, cap),
        (kept(*fields), kept(*fields), kept(*slabs), kept(*slabs), kept(*fields)),
        (e_field, forward_field, got, h1, e1, mat, chip1, far1, timing, bounds),
        6,
        24,
        scratch=(
            VMEM(fields, F32),
            VMEM(fields, F32),
            VMEM((2, *slabs), F32),
            VMEM((3, *layer), F32),
            VMEM((3, *layer), F32),
            VMEM(fields, F32),
            VMEM((3, *layer), F32),
            VMEM((2, *layer), F32),
            VMEM((2, *layer), F32),
            VMEM((2, *layer), F32),
            VMEM(layer, F32),
            dma((6,)),
        ),
        in_hbm=(1, 3, 4, 5),
        anywhere=(6, 7),
    )
    return call(
        last,
        (shape(*fields), shape(*fields), shape(*slabs)),
        (forward, h2, e2, grad, cb, chip2, far2, timing, bounds),
        2.5,
        16,
        scratch=(
            VMEM((2, *layer), F32),
            VMEM((2, *layer), F32),
            VMEM(fields, F32),
            VMEM((2, *layer), F32),
            VMEM(slabs, F32),
            dma((PARTS, 2)),
            dma((PARTS, 4)),
            dma((3,)),
        ),
        anywhere=(5, 6),
        out_hbm=True,
    )


def solution(mesh):
    placed = (
        P(None, "gz", "groups", None),
        P(None, "gz", "groups", None),
        P(None, "gz", "groups", None),
        P("gz", "groups", None),
        P("gz", "groups", None),
        P("gz", "groups"),
        P("gz", "groups"),
        P("groups", "gz"),
        P("groups", None),
        P("groups", None),
    )
    return jax.shard_map(
        local,
        mesh=mesh,
        in_specs=placed,
        out_specs=(
            P(None, "gz", "groups", None),
            P(None, "gz", "groups", None),
            P("gz", "groups", None),
        ),
        check_vma=False,
    )
```

```python
import functools

import jax
import jax.numpy as jnp
from jax import lax
from jax.experimental import pallas as pl
from jax.experimental.pallas import tpu as pltpu
from jax.sharding import PartitionSpec as P

STEPS = 2
ROWS = 64
PARTS = 4
FLOPS_US = 1.15e9
LANES = 128
HALF = 0.5
F32 = jnp.float32
BF16 = jnp.bfloat16
VMEM = pltpu.VMEM
SMEM = pltpu.SMEM


def lanes_of(v):
    return lax.broadcasted_iota(jnp.int32, v.shape, 1)


def ahead_y(v):
    last = v.shape[1] - 1
    return jnp.where(lanes_of(v) < last, pltpu.roll(v, last, axis=1), 0.0) - v


def behind_y(v):
    return v - jnp.where(lanes_of(v) > 0, pltpu.roll(v, 1, axis=1), 0.0)


class Chunk:
    def __init__(self, at, size, width_x):
        self.at, self.size, self.width = at, size, width_x

    def get(self, ref, *index):
        return ref[(*index, pl.ds(self.at, self.size), slice(None))]

    def put(self, ref, *index_and_value):
        *index, value = index_and_value
        ref[(*index, pl.ds(self.at, self.size), slice(None))] = value

    def ahead_x(self, ref, *index):
        here = self.get(ref, *index)
        after = pl.multiple_of(jnp.minimum(self.at + self.size, self.width - 8), 8)
        more = ref[(*index, pl.ds(after, 8), slice(None))]
        more = jnp.where(self.at + self.size < self.width, more, 0.0)
        both = jnp.concatenate([here, more], axis=0)
        return pltpu.roll(both, self.size + 7, axis=0)[: self.size] - here

    def behind_x(self, ref, *index):
        here = self.get(ref, *index)
        before = pl.multiple_of(jnp.maximum(self.at - 8, 0), 8)
        more = ref[(*index, pl.ds(before, 8), slice(None))]
        more = jnp.where(self.at > 0, more, 0.0)
        both = jnp.concatenate([more, here], axis=0)
        return here - pltpu.roll(both, 1, axis=0)[8:]


def over_rows(width_x, body, begin=0, end=None):
    end = width_x if end is None else end
    size = next(k for k in (96, 48, 8) if (end - begin) % k == 0)

    def step(i, carry):
        body(Chunk(pl.multiple_of(begin + i * size, 8), size, width_x))
        return carry

    lax.fori_loop(0, (end - begin) // size, step, 0)


def odd_device():
    return lax.rem(lax.axis_index("gz"), 2) == 1


class Half:
    def __init__(self, up, ins, out_hbm, e_ref, h_ref, mat_ref, out_ref, sems, out_sems):
        e_hbm, h_hbm, eps_hbm, sigma_hbm = ins
        self.up, self.width = up, e_hbm.shape[2]
        self.part = self.width // PARTS
        self.refs = e_ref, h_ref, mat_ref, out_ref
        z = e_hbm.shape[1] - 1 if up else 0
        self.copies, self.out = [], []
        for g in range(PARTS):
            rows = pl.ds(g * self.part, self.part)
            pairs = [
                (eps_hbm.at[z, rows], mat_ref.at[0, rows]),
                (sigma_hbm.at[z, rows], mat_ref.at[1, rows]),
            ]
            if up:
                pairs.append((e_hbm.at[:, z, rows], e_ref.at[:, rows]))
                pairs.append((h_hbm.at[0:2, z, rows], h_ref.at[:, rows]))
            else:
                pairs.append((e_hbm.at[0:2, z, rows], out_ref.at[0:2, rows]))
            self.copies.append(
                [pltpu.make_async_copy(a, b, sems.at[g, i]) for i, (a, b) in enumerate(pairs)]
            )
            self.out.append(
                pltpu.make_async_copy(out_ref.at[:, rows], out_hbm.at[:, rows], out_sems.at[g])
            )

    def start(self):
        for copies in self.copies:
            for copy in copies:
                copy.start()

    def body(self, c):
        e_ref, h_ref, mat_ref, out_ref = self.refs
        c.put(out_ref, 2, 1.0 / (2.0 * c.get(mat_ref, 0) + c.get(mat_ref, 1)))
        if self.up:
            ez = c.get(e_ref, 2)
            c.put(out_ref, 0, c.get(h_ref, 0) - HALF * (ahead_y(ez) + c.get(e_ref, 1)))
            c.put(out_ref, 1, c.get(h_ref, 1) + HALF * (c.get(e_ref, 0) + c.ahead_x(e_ref, 2)))

    def finish(self):
        for copy in self.copies[0]:
            copy.wait()
        for g in range(PARTS):
            if g + 1 < PARTS:
                for copy in self.copies[g + 1]:
                    copy.wait()
            over_rows(self.width, self.body, g * self.part, (g + 1) * self.part)
            self.out[g].start()
        for copy in self.out:
            copy.wait()


def by_parity(when_odd, when_even):
    odd = odd_device()
    pl.when(odd)(when_odd)
    pl.when(jnp.logical_not(odd))(when_even)


def halves_first(e_hbm, h_hbm, eps_hbm, sigma_hbm, far_hbm, *scratch):
    ins = e_hbm, h_hbm, eps_hbm, sigma_hbm

    def run(up):
        half = Half(up, ins, far_hbm, *scratch)
        half.start()
        half.finish()

    by_parity(lambda: run(True), lambda: run(False))


def split3(v):
    one = v.astype(BF16)
    rest = v - one.astype(F32)
    two = rest.astype(BF16)
    three = (rest - two.astype(F32)).astype(BF16)
    return one, two, three


def pack_entries(cap, field, owners_ref, cells_ref, amplitude_ref, packed_ref):
    _, slab, width_x, width_y = field
    top = slab - 1
    peers, _, lanes = packed_ref.shape
    owner, cell, amp = owners_ref[...], cells_ref[...], amplitude_ref[...]
    entries = owner.shape[1]
    named = lax.broadcasted_iota(jnp.int32, (peers, entries), 0) == owner
    hot = named.astype(F32).astype(BF16)
    first = lax.broadcasted_iota(jnp.int32, (entries, entries), 0)
    second = lax.broadcasted_iota(jnp.int32, (entries, entries), 1)
    ahead = (first < second).astype(F32).astype(BF16)
    before = jnp.dot(hot, ahead, preferred_element_type=F32)
    rank = jnp.sum(jnp.where(named, before, 0.0), axis=0, keepdims=True).astype(jnp.int32)
    layer = width_x * width_y
    spread = lambda v: jnp.broadcast_to(v, (8, entries))
    names = (
        spread(owner),
        spread(jnp.where(cell >= top * layer, owner + 1, -1)),
        spread(jnp.where(cell < layer, owner - 1, -1)),
    )
    rows = jnp.concatenate([amp, cell.astype(F32), jnp.zeros((4, entries), F32)], axis=0)
    slot = lax.broadcasted_iota(jnp.int32, (lanes, entries), 0)
    hits = [(slot == rank + k * cap).astype(F32) for k in range(3)]
    place = jnp.concatenate(hits, axis=1).astype(BF16)
    total = None
    for term in split3(rows):
        term = term.astype(F32)
        values = [
            jnp.concatenate([jnp.where(name == d, term, 0.0) for d in range(peers)], axis=0)
            for name in names
        ]
        values = jnp.concatenate(values, axis=1).astype(BF16)
        out = lax.dot_general(values, place, (((1,), (1,)), ((), ())), preferred_element_type=F32)
        total = out if total is None else total + out
    for d in range(peers):
        packed_ref[d] = total[d * 8 : d * 8 + 4]


def magnetic_step(c, e_ref, h_ref, h1_ref):
    slab = e_ref.shape[1]
    for z in range(slab):
        ex, ey, ez = (c.get(e_ref, k, z) for k in range(3))
        up_x = c.get(e_ref, 0, z + 1) - ex if z + 1 < slab else -ex
        up_y = c.get(e_ref, 1, z + 1) - ey if z + 1 < slab else -ey
        c.put(h1_ref, 0, z, c.get(h_ref, 0, z) - HALF * (ahead_y(ez) - up_y))
        c.put(h1_ref, 1, z, c.get(h_ref, 1, z) - HALF * (up_x - c.ahead_x(e_ref, 2, z)))
        c.put(h1_ref, 2, z, c.get(h_ref, 2, z) - HALF * (c.ahead_x(e_ref, 1, z) - ahead_y(ex)))


def electric_step(c, z, comps, e_ref, h1_ref, ca, cb):
    hx, hy, hz = (c.get(h1_ref, k, z) for k in range(3))
    down_x = hx - c.get(h1_ref, 0, z - 1) if z > 0 else hx
    down_y = hy - c.get(h1_ref, 1, z - 1) if z > 0 else hy
    ex = ca * c.get(e_ref, 0, z) + cb * (behind_y(hz) - down_y)
    ey = ca * c.get(e_ref, 1, z) + cb * (down_x - c.behind_x(h1_ref, 2, z))
    if comps == 2:
        return ex, ey
    ez = ca * c.get(e_ref, 2, z) + cb * (c.behind_x(h1_ref, 1, z) - behind_y(hx))
    return ex, ey, ez


def halves_second(
    cap,
    e_ref,
    h_ref,
    eps_hbm,
    sigma_hbm,
    owners_ref,
    cells_ref,
    amplitude_ref,
    after_hbm,
    packed_hbm,
    chip1_hbm,
    chip2_hbm,
    chip3_hbm,
    far_hbm,
    h1_hbm,
    e1_hbm,
    mat_hbm,
    h1_ref,
    e1_ref,
    mat_ref,
    chip_ref,
    far_ref,
    packed_ref,
    in_sems,
    step_sems,
    out_sems,
):
    slab, width_x = e_ref.shape[1], e_ref.shape[2]
    top = slab - 1
    odd = odd_device()
    copies = [
        pltpu.make_async_copy(a, mat_ref.at[i], in_sems.at[i])
        for i, a in enumerate((eps_hbm, sigma_hbm))
    ]
    for copy in copies:
        copy.start()
    pack_entries(cap, e_ref.shape, owners_ref, cells_ref, amplitude_ref, packed_ref)
    out = [pltpu.make_async_copy(packed_ref, packed_hbm, step_sems.at[3])]
    out[0].start()
    over_rows(width_x, lambda c: magnetic_step(c, e_ref, h_ref, h1_ref))
    out.append(pltpu.make_async_copy(h1_ref, h1_hbm, step_sems.at[0]))
    out[1].start()
    for copy in copies:
        copy.wait()

    def electric(c):
        for z in range(slab):
            eps, sigma = c.get(mat_ref, 0, z), c.get(mat_ref, 1, z)
            cb = 1.0 / (2.0 * eps + sigma)
            ca = (2.0 * eps - sigma) * cb
            c.put(mat_ref, 0, z, ca)
            c.put(mat_ref, 1, z, cb)
            for k, v in enumerate(electric_step(c, z, 3, e_ref, h1_ref, ca, cb)):
                c.put(e1_ref, k, z, v)

    over_rows(width_x, electric)

    def boundary(c):
        ex, ey, ez = (c.get(e1_ref, k, top) for k in range(3))
        hx = c.get(h1_ref, 0, top) - HALF * (ahead_y(ez) + ey)
        hy = c.get(h1_ref, 1, top) + HALF * (ex + c.ahead_x(e1_ref, 2, top))
        upward = (
            c.get(h1_ref, 0, top),
            c.get(h1_ref, 1, top),
            c.get(mat_ref, 1, top),
            hx,
            hy,
        )
        downward = (
            c.get(e_ref, 0, 0),
            c.get(e_ref, 1, 0),
            c.get(mat_ref, 1, 0),
            c.get(e1_ref, 0, 0),
            c.get(e1_ref, 1, 0),
        )
        for k in range(5):
            c.put(chip_ref, k, jnp.where(odd, downward[k], upward[k]))
        for k in range(2):
            c.put(far_ref, k, jnp.where(odd, upward[k + 3], downward[k + 3]))

    part = width_x // PARTS
    for g in range(PARTS):
        over_rows(width_x, boundary, g * part, (g + 1) * part)
        rows = pl.ds(g * part, part)
        pairs = (
            (far_ref, far_hbm),
            (chip_ref.at[0:2], chip1_hbm),
            (chip_ref.at[2:3], chip2_hbm),
            (chip_ref.at[3:5], chip3_hbm),
        )
        for i, (a, b) in enumerate(pairs):
            out.append(pltpu.make_async_copy(a.at[:, rows], b.at[:, rows], out_sems.at[g, i]))
            out[-1].start()
        if g == 0:
            for i, (a, b) in enumerate(((e1_ref, e1_hbm), (mat_ref, mat_hbm))):
                out.append(pltpu.make_async_copy(a, b, step_sems.at[1 + i]))
                out[-1].start()
    for copy in out:
        copy.wait()


def place_entries(cap, got_ref, own_ref, below_ref, above_ref):
    peers, _, lanes = got_ref.shape
    slab, width_x, width_y = own_ref.shape[1:]
    group = LANES // cap
    part = lax.broadcasted_iota(jnp.int32, (4, LANES), 1) // cap

    def row_of(segment):
        blocks = []
        for g in range(0, peers, group):
            block = jnp.zeros((4, LANES), F32)
            for p in range(min(group, peers - g)):
                shift = ((p - segment) * cap) % LANES
                there = got_ref[g + p]
                there = pltpu.roll(there, shift, axis=1) if shift else there
                block = jnp.where(part == p, there, block)
            blocks.append(block)
        return jnp.concatenate(blocks, axis=1)

    def fill(segment, first_line, lines, comps, store):
        row = row_of(segment)
        count = row.shape[1]
        cell = row[3:4].astype(jnp.int32)
        line = cell // width_y
        column = cell - line * width_y
        line = line - first_line
        where_line = lax.broadcasted_iota(jnp.int32, (lines, count), 0) == line
        left = where_line.astype(F32).astype(BF16)
        where_column = lax.broadcasted_iota(jnp.int32, (width_y, count), 0) == column
        for k in range(comps):
            total = None
            for term in split3(row[k : k + 1]):
                right = jnp.where(where_column, term.astype(F32), 0.0).astype(BF16)
                out = lax.dot_general(
                    left, right, (((1,), (1,)), ((), ())), preferred_element_type=F32
                )
                total = out if total is None else total + out
            store(k, total)

    def store_own(k, total):
        for z in range(slab):
            own_ref[k, z] = total[z * width_x : (z + 1) * width_x]

    def store_below(k, total):
        below_ref[k] = total

    def store_above(k, total):
        above_ref[k] = total

    fill(0, 0, slab * width_x, 3, store_own)
    fill(1, (slab - 1) * width_x, width_x, 3, store_below)
    fill(2, 0, width_x, 2, store_above)


def inside(c, bounds_ref, z, slab, shape):
    deep = lax.axis_index("gz") * slab + z
    in_z = (deep >= bounds_ref[0, 0]) & (deep < bounds_ref[0, 1])
    line = lax.broadcasted_iota(jnp.int32, shape, 0) + c.at
    column = lax.broadcasted_iota(jnp.int32, shape, 1)
    keep = (line >= bounds_ref[1, 0]) & (line < bounds_ref[1, 1])
    keep = keep & (column >= bounds_ref[2, 0]) & (column < bounds_ref[2, 1])
    return jnp.where(keep & in_z, 1.0, 0.0)


def middle(
    cap,
    e_ref,
    forward_hbm,
    got_ref,
    h1_hbm,
    e1_hbm,
    mat_hbm,
    chip1_hbm,
    chip2_hbm,
    far_hbm,
    timing_ref,
    bounds_ref,
    h2_ref,
    e2_ref,
    grad_ref,
    cb_ref,
    forward_ref,
    eout_hbm,
    hout_hbm,
    h1_ref,
    e1_ref,
    mat_ref,
    chip_ref,
    far_ref,
    own_ref,
    sbelow_ref,
    sabove_ref,
    fs,
    h2a,
    dza,
    sems,
    out_sems,
):
    pairs = (
        (far_hbm, far_ref),
        (chip1_hbm, chip_ref.at[0:2]),
        (chip2_hbm, chip_ref.at[2:3]),
        (e1_hbm, e1_ref),
        (h1_hbm, h1_ref),
        (mat_hbm, mat_ref),
        (forward_hbm, forward_ref),
    )
    copies = [pltpu.make_async_copy(a, b, sems.at[i]) for i, (a, b) in enumerate(pairs)]
    for copy in copies:
        copy.start()
    place_entries(cap, got_ref, own_ref, sbelow_ref, sabove_ref)
    for copy in copies[:-1]:
        copy.wait()
    slab, width_x = e_ref.shape[1], e_ref.shape[2]
    top = slab - 1
    odd = odd_device()
    has_below = jnp.where(lax.axis_index("gz") > 0, 1.0, 0.0).astype(F32)
    wave0, wave1 = timing_ref[0, 0], timing_ref[0, 1]
    weight0, weight1 = timing_ref[1, 0], timing_ref[1, 1]

    def first(c):
        chip = [c.get(chip_ref, k) for k in range(3)]
        far = [c.get(far_ref, k) for k in range(3)]
        low = [jnp.where(odd, a, b) for a, b in zip(chip, far)]
        high = [jnp.where(odd, b, a) for a, b in zip(chip, far)]
        ex, ey = c.get(e_ref, 0, 0), c.get(e_ref, 1, 0)
        hax = has_below * (low[0] + HALF * ey)
        hay = has_below * (low[1] - HALF * ex)
        cb_a, cb_b = low[2], high[2]
        cb = [c.get(mat_ref, 1, z) for z in range(slab)]
        e1 = [
            [c.get(e1_ref, k, z) - wave0 * cb[z] * c.get(own_ref, k, z) for k in range(3)]
            for z in range(slab)
        ]
        e1[0][0] = e1[0][0] + cb[0] * hay
        e1[0][1] = e1[0][1] - cb[0] * hax
        hx = c.get(h1_ref, 0, top) + HALF * high[1]
        hy = c.get(h1_ref, 1, top) - HALF * high[0]
        c.put(h1_ref, 0, top, hx)
        c.put(h1_ref, 1, top, hy)
        bx_far, bx_chip = c.behind_x(far_ref, 0), c.behind_x(chip_ref, 0)
        bx = jnp.where(odd, bx_far, bx_chip)
        e1[top][0] = e1[top][0] + HALF * cb[top] * high[0]
        e1[top][1] = e1[top][1] + HALF * cb[top] * high[1]
        e1[top][2] = e1[top][2] - HALF * cb[top] * (bx + behind_y(high[1]))
        c.put(fs, 0, cb_b * (hy - wave0 * c.get(sabove_ref, 0)))
        c.put(fs, 1, -cb_b * (hx + wave0 * c.get(sabove_ref, 1)))
        for z in range(slab):
            for k in range(3):
                c.put(e1_ref, k, z, e1[z][k])
        dx = cb_a * (HALF * ex - wave0 * c.get(sbelow_ref, 0))
        dy = cb_a * (HALF * ey - wave0 * c.get(sbelow_ref, 1))
        dz = -cb_a * (
            HALF * (c.behind_x(e_ref, 0, 0) + behind_y(ey)) + wave0 * c.get(sbelow_ref, 2)
        )
        c.put(dza, dz)
        c.put(h2a, 0, has_below * HALF * (ey - dy + e1[0][1] - ahead_y(dz)))
        c.put(h2a, 1, has_below * HALF * (dx - ex - e1[0][0]))

    over_rows(width_x, first)

    def second(c):
        c.put(h2a, 1, c.get(h2a, 1) + has_below * HALF * c.ahead_x(dza))
        for z in range(slab):
            ex, ey, ez = (c.get(e1_ref, k, z) for k in range(3))
            if z < top:
                up_x, up_y = c.get(e1_ref, 0, z + 1) - ex, c.get(e1_ref, 1, z + 1) - ey
            else:
                up_x, up_y = c.get(fs, 0) - ex, c.get(fs, 1) - ey
            hx, hy = c.get(h1_ref, 0, z), c.get(h1_ref, 1, z)
            c.put(h2_ref, 0, z, hx - HALF * (ahead_y(ez) - up_y))
            c.put(h2_ref, 1, z, hy - HALF * (up_x - c.ahead_x(e1_ref, 2, z)))
            hz = c.get(h1_ref, 2, z)
            c.put(h2_ref, 2, z, hz - HALF * (c.ahead_x(e1_ref, 1, z) - ahead_y(ex)))

    over_rows(width_x, second)

    def third(c):
        for z in range(slab):
            ca, cb = c.get(mat_ref, 0, z), c.get(mat_ref, 1, z)
            c.put(cb_ref, z, cb)
            hx, hy, hz = (c.get(h2_ref, k, z) for k in range(3))
            if z > 0:
                down_x, down_y = hx - c.get(h2_ref, 0, z - 1), hy - c.get(h2_ref, 1, z - 1)
            else:
                down_x, down_y = hx - c.get(h2a, 0), hy - c.get(h2a, 1)
            curl = (
                behind_y(hz) - down_y,
                down_x - c.behind_x(h2_ref, 2, z),
                c.behind_x(h2_ref, 1, z) - behind_y(hx),
            )
            dot1, dot2 = 0.0, 0.0
            for k in range(3):
                e1 = c.get(e1_ref, k, z)
                e2 = ca * e1 + cb * (curl[k] - wave1 * c.get(own_ref, k, z))
                c.put(e2_ref, k, z, e2)
                fwd = c.get(forward_ref, k, z)
                dot1 = dot1 + e1 * fwd
                dot2 = dot2 + e2 * fwd
            mask = inside(c, bounds_ref, z, slab, ca.shape)
            c.put(grad_ref, z, mask * (weight0 * dot1 + weight1 * dot2))

    copies[-1].wait()
    pairs = (
        (h2_ref.at[0:2, 0:top], hout_hbm.at[0:2, 0:top]),
        (h2_ref.at[2], hout_hbm.at[2]),
        (e2_ref.at[2, 0:top], eout_hbm.at[2, 0:top]),
    )
    done = [pltpu.make_async_copy(a, b, out_sems.at[i]) for i, (a, b) in enumerate(pairs)]
    done[0].start()
    done[1].start()
    over_rows(width_x, third)
    done[2].start()
    for copy in done:
        copy.wait()


def last(
    forward_ref,
    h2_ref,
    e2_ref,
    gradp_ref,
    cb_ref,
    chip_ref,
    far_ref,
    timing_ref,
    bounds_ref,
    ein_hbm,
    hin_hbm,
    eout_hbm,
    hout_hbm,
    grad_hbm,
    e_ref,
    h_ref,
    grad_ref,
    sems,
):
    slab, width_x = e2_ref.shape[1], e2_ref.shape[2]
    top = slab - 1
    odd = odd_device()
    weight1 = timing_ref[1, 1]
    part = width_x // PARTS

    def body(c):
        chip = [c.get(chip_ref, k) for k in range(2)]
        far = [c.get(far_ref, k) for k in range(2)]
        low = [jnp.where(odd, a, b) for a, b in zip(chip, far)]
        high = [jnp.where(odd, b, a) for a, b in zip(chip, far)]
        bx = jnp.where(odd, c.behind_x(far_ref, 0), c.behind_x(chip_ref, 0))
        cb_low, cb_top = c.get(cb_ref, 0), HALF * c.get(cb_ref, top)
        more = [[0.0] * 3 for _ in range(slab)]
        more[0][0] = cb_low * low[1]
        more[0][1] = -cb_low * low[0]
        more[top][0] = more[top][0] + cb_top * high[0]
        more[top][1] = more[top][1] + cb_top * high[1]
        more[top][2] = -cb_top * (bx + behind_y(high[1]))
        for z in range(slab):
            dot = 0.0
            for k in range(3 if z == top else 2):
                delta = more[z][k]
                dot = dot + delta * c.get(forward_ref, k, z)
                c.put(e_ref, k, z, c.get(e2_ref, k, z) + delta)
            mask = inside(c, bounds_ref, z, slab, cb_low.shape)
            c.put(grad_ref, z, c.get(gradp_ref, z) + (weight1 * mask) * dot)
        c.put(h_ref, 0, c.get(h2_ref, 0, top) + HALF * high[1])
        c.put(h_ref, 1, c.get(h2_ref, 1, top) - HALF * high[0])

    copies = []
    for g in range(PARTS):
        over_rows(width_x, body, g * part, (g + 1) * part)
        rows = pl.ds(g * part, part)
        pairs = (
            (e_ref.at[0:2, :, rows], eout_hbm.at[0:2, :, rows]),
            (e_ref.at[2, top, rows], eout_hbm.at[2, top, rows]),
            (h_ref.at[:, rows], hout_hbm.at[0:2, top, rows]),
            (grad_ref.at[:, rows], grad_hbm.at[:, rows]),
        )
        for i, (a, b) in enumerate(pairs):
            copy = pltpu.make_async_copy(a, b, sems.at[g, i])
            copy.start()
            copies.append(copy)
    for copy in copies:
        copy.wait()


def shape(*dims):
    return jax.ShapeDtypeStruct(dims, F32)


def kept(*dims):
    return VMEM(dims, F32)


def sent(*dims):
    return pltpu.HBM(dims, F32)


def call(body, outs, ins, us, limit, scratch=(), in_hbm=(), anywhere=(), aliases=None):
    def place(i, x):
        if i in in_hbm:
            return pl.BlockSpec(memory_space=pltpu.HBM)
        if i in anywhere:
            return pl.BlockSpec(memory_space=pl.ANY)
        return pl.BlockSpec(memory_space=SMEM if x.size < 16 else VMEM)

    ins = [
        pltpu.with_memory_space_constraint(x, pltpu.HBM) if i in in_hbm else x
        for i, x in enumerate(ins)
    ]
    return pl.pallas_call(
        body,
        out_shape=outs,
        in_specs=[place(i, x) for i, x in enumerate(ins)],
        out_specs=jax.tree.map(
            lambda x: pl.BlockSpec(memory_space=getattr(x, "memory_space", VMEM)), outs
        ),
        input_output_aliases=aliases or {},
        scratch_shapes=list(scratch),
        compiler_params=pltpu.CompilerParams(vmem_limit_bytes=limit << 20),
        cost_estimate=pl.CostEstimate(flops=int(us * FLOPS_US), bytes_accessed=0, transcendentals=0),
    )(*ins)


def local(
    e_field,
    h_field,
    forward_field,
    permittivity,
    conductivity,
    owners,
    cells,
    amplitude,
    timing,
    bounds,
):
    slab, wx, wy = permittivity.shape
    peers = lax.axis_size("gz")
    rows = owners.shape[0]
    cap = 2 * rows // peers
    lanes = -(-3 * cap // LANES) * LANES
    cells_all = slab * wx * wy
    chip_pairs = [p for i in range(0, peers - 1, 2) for p in ((i, i + 1), (i + 1, i))]
    far_pairs = [p for i in range(1, peers - 1, 2) for p in ((i, i + 1), (i + 1, i))]

    layer, slabs, fields = (wx, wy), (slab, wx, wy), (3, slab, wx, wy)
    dma = pltpu.SemaphoreType.DMA
    begun = call(
        halves_first,
        sent(3, *layer),
        (e_field, h_field, permittivity, conductivity),
        2,
        56,
        scratch=(
            VMEM((3, *layer), F32),
            VMEM((2, *layer), F32),
            VMEM((2, *layer), F32),
            VMEM((3, *layer), F32),
            dma((PARTS, 4)),
            dma((PARTS,)),
        ),
        in_hbm=(0, 1, 2, 3),
    )
    far1 = lax.ppermute(begun, "gz", far_pairs)
    packed, chip1, chip2, chip3, far2, h1, e1, mat = call(
        functools.partial(halves_second, cap),
        (
            sent(peers, 4, lanes),
            sent(2, *layer),
            sent(1, *layer),
            sent(2, *layer),
            sent(2, *layer),
            sent(*fields),
            sent(*fields),
            sent(2, *slabs),
        ),
        (
            e_field,
            h_field,
            permittivity,
            conductivity,
            owners.reshape(1, rows),
            cells.reshape(1, rows),
            amplitude,
            begun,
        ),
        3,
        16,
        scratch=(
            VMEM(fields, F32),
            VMEM(fields, F32),
            VMEM((2, *slabs), F32),
            VMEM((5, *layer), F32),
            VMEM((2, *layer), F32),
            VMEM((peers, 4, lanes), F32),
            dma((2,)),
            dma((4,)),
            dma((PARTS, 4)),
        ),
        in_hbm=(2, 3, 7),
    )
    got = lax.all_to_all(packed, "gz", 0, 0, tiled=True)
    far2 = lax.ppermute(far2, "gz", far_pairs)
    chip1, chip2, chip3 = (lax.ppermute(x, "gz", chip_pairs) for x in (chip1, chip2, chip3))
    h2, e2, grad, cb, forward, e_part, h_part = call(
        functools.partial(middle, cap),
        (
            kept(*fields),
            kept(*fields),
            kept(*slabs),
            kept(*slabs),
            kept(*fields),
            sent(*fields),
            sent(*fields),
        ),
        (e_field, forward_field, got, h1, e1, mat, chip1, chip2, far1, timing, bounds),
        6,
        24,
        scratch=(
            VMEM(fields, F32),
            VMEM(fields, F32),
            VMEM((2, *slabs), F32),
            VMEM((3, *layer), F32),
            VMEM((3, *layer), F32),
            VMEM(fields, F32),
            VMEM((3, *layer), F32),
            VMEM((2, *layer), F32),
            VMEM((2, *layer), F32),
            VMEM((2, *layer), F32),
            VMEM(layer, F32),
            dma((7,)),
            dma((3,)),
        ),
        in_hbm=(1, 3, 4, 5),
        anywhere=(6, 7, 8),
    )
    return call(
        last,
        (sent(*fields), sent(*fields), sent(*slabs)),
        (forward, h2, e2, grad, cb, chip3, far2, timing, bounds, e_part, h_part),
        2.5,
        16,
        scratch=(
            VMEM(fields, F32),
            VMEM((2, *layer), F32),
            VMEM(slabs, F32),
            dma((PARTS, 4)),
        ),
        in_hbm=(9, 10),
        aliases={9: 0, 10: 1},
    )


def solution(mesh):
    placed = (
        P(None, "gz", "groups", None),
        P(None, "gz", "groups", None),
        P(None, "gz", "groups", None),
        P("gz", "groups", None),
        P("gz", "groups", None),
        P("gz", "groups"),
        P("gz", "groups"),
        P("groups", "gz"),
        P("groups", None),
        P("groups", None),
    )
    return jax.shard_map(
        local,
        mesh=mesh,
        in_specs=placed,
        out_specs=(
            P(None, "gz", "groups", None),
            P(None, "gz", "groups", None),
            P("gz", "groups", None),
        ),
        check_vma=False,
    )
```

```python
import functools

import jax
import jax.numpy as jnp
from jax import lax
from jax.experimental import pallas as pl
from jax.experimental.pallas import tpu as pltpu
from jax.sharding import PartitionSpec as P

STEPS = 2
ROWS = 64
PARTS = 4
FLOPS_US = 1.15e9
LANES = 128
HALF = 0.5
F32 = jnp.float32
BF16 = jnp.bfloat16
VMEM = pltpu.VMEM
SMEM = pltpu.SMEM


def lanes_of(v):
    return lax.broadcasted_iota(jnp.int32, v.shape, 1)


def ahead_y(v):
    last = v.shape[1] - 1
    return jnp.where(lanes_of(v) < last, pltpu.roll(v, last, axis=1), 0.0) - v


def behind_y(v):
    return v - jnp.where(lanes_of(v) > 0, pltpu.roll(v, 1, axis=1), 0.0)


class Chunk:
    def __init__(self, at, size, width_x):
        self.at, self.size, self.width = at, size, width_x

    def get(self, ref, *index):
        return ref[(*index, pl.ds(self.at, self.size), slice(None))]

    def put(self, ref, *index_and_value):
        *index, value = index_and_value
        ref[(*index, pl.ds(self.at, self.size), slice(None))] = value

    def ahead_x(self, ref, *index):
        here = self.get(ref, *index)
        after = pl.multiple_of(jnp.minimum(self.at + self.size, self.width - 8), 8)
        more = ref[(*index, pl.ds(after, 8), slice(None))]
        more = jnp.where(self.at + self.size < self.width, more, 0.0)
        both = jnp.concatenate([here, more], axis=0)
        return pltpu.roll(both, self.size + 7, axis=0)[: self.size] - here

    def behind_x(self, ref, *index):
        here = self.get(ref, *index)
        before = pl.multiple_of(jnp.maximum(self.at - 8, 0), 8)
        more = ref[(*index, pl.ds(before, 8), slice(None))]
        more = jnp.where(self.at > 0, more, 0.0)
        both = jnp.concatenate([more, here], axis=0)
        return here - pltpu.roll(both, 1, axis=0)[8:]


def over_rows(width_x, body, begin=0, end=None):
    end = width_x if end is None else end
    size = next(k for k in (96, 48, 8) if (end - begin) % k == 0)

    def step(i, carry):
        body(Chunk(pl.multiple_of(begin + i * size, 8), size, width_x))
        return carry

    lax.fori_loop(0, (end - begin) // size, step, 0)


def odd_device():
    return lax.rem(lax.axis_index("gz"), 2) == 1


class Half:
    def __init__(self, up, ins, out_hbm, e_ref, h_ref, mat_ref, out_ref, sems, out_sems):
        e_hbm, h_hbm, eps_hbm, sigma_hbm = ins
        self.up, self.width = up, e_hbm.shape[2]
        self.part = self.width // PARTS
        self.refs = e_ref, h_ref, mat_ref, out_ref
        z = e_hbm.shape[1] - 1 if up else 0
        self.copies, self.out = [], []
        for g in range(PARTS):
            rows = pl.ds(g * self.part, self.part)
            pairs = [
                (eps_hbm.at[z, rows], mat_ref.at[0, rows]),
                (sigma_hbm.at[z, rows], mat_ref.at[1, rows]),
            ]
            if up:
                pairs.append((e_hbm.at[:, z, rows], e_ref.at[:, rows]))
                pairs.append((h_hbm.at[0:2, z, rows], h_ref.at[:, rows]))
            else:
                pairs.append((e_hbm.at[0:2, z, rows], out_ref.at[0:2, rows]))
            self.copies.append(
                [pltpu.make_async_copy(a, b, sems.at[g, i]) for i, (a, b) in enumerate(pairs)]
            )
            self.out.append(
                pltpu.make_async_copy(out_ref.at[:, rows], out_hbm.at[:, rows], out_sems.at[g])
            )

    def start(self):
        for copies in self.copies:
            for copy in copies:
                copy.start()

    def body(self, c):
        e_ref, h_ref, mat_ref, out_ref = self.refs
        c.put(out_ref, 2, 1.0 / (2.0 * c.get(mat_ref, 0) + c.get(mat_ref, 1)))
        if self.up:
            ez = c.get(e_ref, 2)
            c.put(out_ref, 0, c.get(h_ref, 0) - HALF * (ahead_y(ez) + c.get(e_ref, 1)))
            c.put(out_ref, 1, c.get(h_ref, 1) + HALF * (c.get(e_ref, 0) + c.ahead_x(e_ref, 2)))

    def finish(self):
        for copy in self.copies[0]:
            copy.wait()
        for g in range(PARTS):
            if g + 1 < PARTS:
                for copy in self.copies[g + 1]:
                    copy.wait()
            over_rows(self.width, self.body, g * self.part, (g + 1) * self.part)
            self.out[g].start()
        for copy in self.out:
            copy.wait()


def by_parity(when_odd, when_even):
    odd = odd_device()
    pl.when(odd)(when_odd)
    pl.when(jnp.logical_not(odd))(when_even)


def halves_first(e_hbm, h_hbm, eps_hbm, sigma_hbm, far_hbm, *scratch):
    ins = e_hbm, h_hbm, eps_hbm, sigma_hbm

    def run(up):
        half = Half(up, ins, far_hbm, *scratch)
        half.start()
        half.finish()

    by_parity(lambda: run(True), lambda: run(False))


def split3(v):
    one = v.astype(BF16)
    rest = v - one.astype(F32)
    two = rest.astype(BF16)
    three = (rest - two.astype(F32)).astype(BF16)
    return one, two, three


def pack_entries(cap, field, owners_ref, cells_ref, amplitude_ref, packed_ref):
    _, slab, width_x, width_y = field
    top = slab - 1
    peers, _, lanes = packed_ref.shape
    owner, cell, amp = owners_ref[...], cells_ref[...], amplitude_ref[...]
    entries = owner.shape[1]
    named = lax.broadcasted_iota(jnp.int32, (peers, entries), 0) == owner
    hot = named.astype(F32).astype(BF16)
    first = lax.broadcasted_iota(jnp.int32, (entries, entries), 0)
    second = lax.broadcasted_iota(jnp.int32, (entries, entries), 1)
    ahead = (first < second).astype(F32).astype(BF16)
    before = jnp.dot(hot, ahead, preferred_element_type=F32)
    rank = jnp.sum(jnp.where(named, before, 0.0), axis=0, keepdims=True).astype(jnp.int32)
    layer = width_x * width_y
    spread = lambda v: jnp.broadcast_to(v, (8, entries))
    names = (
        spread(owner),
        spread(jnp.where(cell >= top * layer, owner + 1, -1)),
        spread(jnp.where(cell < layer, owner - 1, -1)),
    )
    rows = jnp.concatenate([amp, cell.astype(F32), jnp.zeros((4, entries), F32)], axis=0)
    slot = lax.broadcasted_iota(jnp.int32, (lanes, entries), 0)
    hits = [(slot == rank + k * cap).astype(F32) for k in range(3)]
    place = jnp.concatenate(hits, axis=1).astype(BF16)
    total = None
    for term in split3(rows):
        term = term.astype(F32)
        values = [
            jnp.concatenate([jnp.where(name == d, term, 0.0) for d in range(peers)], axis=0)
            for name in names
        ]
        values = jnp.concatenate(values, axis=1).astype(BF16)
        out = lax.dot_general(values, place, (((1,), (1,)), ((), ())), preferred_element_type=F32)
        total = out if total is None else total + out
    for d in range(peers):
        packed_ref[d] = total[d * 8 : d * 8 + 4]


def magnetic_step(c, e_ref, h_ref, h1_ref):
    slab = e_ref.shape[1]
    for z in range(slab):
        ex, ey, ez = (c.get(e_ref, k, z) for k in range(3))
        up_x = c.get(e_ref, 0, z + 1) - ex if z + 1 < slab else -ex
        up_y = c.get(e_ref, 1, z + 1) - ey if z + 1 < slab else -ey
        c.put(h1_ref, 0, z, c.get(h_ref, 0, z) - HALF * (ahead_y(ez) - up_y))
        c.put(h1_ref, 1, z, c.get(h_ref, 1, z) - HALF * (up_x - c.ahead_x(e_ref, 2, z)))
        c.put(h1_ref, 2, z, c.get(h_ref, 2, z) - HALF * (c.ahead_x(e_ref, 1, z) - ahead_y(ex)))


def electric_step(c, z, comps, e_ref, h1_ref, ca, cb):
    hx, hy, hz = (c.get(h1_ref, k, z) for k in range(3))
    down_x = hx - c.get(h1_ref, 0, z - 1) if z > 0 else hx
    down_y = hy - c.get(h1_ref, 1, z - 1) if z > 0 else hy
    ex = ca * c.get(e_ref, 0, z) + cb * (behind_y(hz) - down_y)
    ey = ca * c.get(e_ref, 1, z) + cb * (down_x - c.behind_x(h1_ref, 2, z))
    if comps == 2:
        return ex, ey
    ez = ca * c.get(e_ref, 2, z) + cb * (c.behind_x(h1_ref, 1, z) - behind_y(hx))
    return ex, ey, ez


def electric_all(c, e_ref, h1_ref, e1_ref, mat_ref):
    for z in range(e_ref.shape[1]):
        eps, sigma = c.get(mat_ref, 0, z), c.get(mat_ref, 1, z)
        cb = 1.0 / (2.0 * eps + sigma)
        ca = (2.0 * eps - sigma) * cb
        c.put(mat_ref, 0, z, ca)
        c.put(mat_ref, 1, z, cb)
        for k, v in enumerate(electric_step(c, z, 3, e_ref, h1_ref, ca, cb)):
            c.put(e1_ref, k, z, v)


def halves_second(
    cap,
    e_ref,
    h_ref,
    eps_hbm,
    sigma_hbm,
    owners_ref,
    cells_ref,
    amplitude_ref,
    after_hbm,
    packed_hbm,
    chip0_hbm,
    chip1_hbm,
    chip2_hbm,
    chip3_hbm,
    far_hbm,
    h1_ref,
    e1_ref,
    mat_ref,
    chip_ref,
    far_ref,
    packed_ref,
    in_sems,
    step_sems,
    out_sems,
):
    slab, width_x = e_ref.shape[1], e_ref.shape[2]
    top = slab - 1
    odd = odd_device()
    copies = [
        pltpu.make_async_copy(a, mat_ref.at[i], in_sems.at[i])
        for i, a in enumerate((eps_hbm, sigma_hbm))
    ]
    for copy in copies:
        copy.start()
    pack_entries(cap, e_ref.shape, owners_ref, cells_ref, amplitude_ref, packed_ref)
    out = [pltpu.make_async_copy(packed_ref, packed_hbm, step_sems.at[0])]
    out[0].start()
    over_rows(width_x, lambda c: magnetic_step(c, e_ref, h_ref, h1_ref))
    for copy in copies:
        copy.wait()

    over_rows(width_x, lambda c: electric_all(c, e_ref, h1_ref, e1_ref, mat_ref))

    def boundary(c):
        ex, ey, ez = (c.get(e1_ref, k, top) for k in range(3))
        hx = c.get(h1_ref, 0, top) - HALF * (ahead_y(ez) + ey)
        hy = c.get(h1_ref, 1, top) + HALF * (ex + c.ahead_x(e1_ref, 2, top))
        upward = (
            c.get(h1_ref, 0, top),
            c.get(h1_ref, 1, top),
            c.get(mat_ref, 1, top),
            hx,
            hy,
        )
        downward = (
            c.get(e_ref, 0, 0),
            c.get(e_ref, 1, 0),
            c.get(mat_ref, 1, 0),
            c.get(e1_ref, 0, 0),
            c.get(e1_ref, 1, 0),
        )
        for k in range(5):
            c.put(chip_ref, k, jnp.where(odd, downward[k], upward[k]))
        for k in range(2):
            c.put(far_ref, k, jnp.where(odd, upward[k + 3], downward[k + 3]))

    part = width_x // PARTS
    for g in range(PARTS):
        over_rows(width_x, boundary, g * part, (g + 1) * part)
        rows = pl.ds(g * part, part)
        pairs = (
            (far_ref, far_hbm),
            (chip_ref.at[0:1], chip0_hbm),
            (chip_ref.at[1:2], chip1_hbm),
            (chip_ref.at[2:3], chip2_hbm),
            (chip_ref.at[3:5], chip3_hbm),
        )
        for i, (a, b) in enumerate(pairs):
            out.append(pltpu.make_async_copy(a.at[:, rows], b.at[:, rows], out_sems.at[g, i]))
            out[-1].start()
    for copy in out:
        copy.wait()


def place_entries(cap, got_ref, own_ref, below_ref, above_ref):
    peers, _, lanes = got_ref.shape
    slab, width_x, width_y = own_ref.shape[1:]
    group = LANES // cap
    part = lax.broadcasted_iota(jnp.int32, (4, LANES), 1) // cap

    def row_of(segment):
        blocks = []
        for g in range(0, peers, group):
            block = jnp.zeros((4, LANES), F32)
            for p in range(min(group, peers - g)):
                shift = ((p - segment) * cap) % LANES
                there = got_ref[g + p]
                there = pltpu.roll(there, shift, axis=1) if shift else there
                block = jnp.where(part == p, there, block)
            blocks.append(block)
        return jnp.concatenate(blocks, axis=1)

    def fill(segment, first_line, lines, comps, store):
        row = row_of(segment)
        count = row.shape[1]
        cell = row[3:4].astype(jnp.int32)
        line = cell // width_y
        column = cell - line * width_y
        line = line - first_line
        where_line = lax.broadcasted_iota(jnp.int32, (lines, count), 0) == line
        left = where_line.astype(F32).astype(BF16)
        where_column = lax.broadcasted_iota(jnp.int32, (width_y, count), 0) == column
        for k in range(comps):
            total = None
            for term in split3(row[k : k + 1]):
                right = jnp.where(where_column, term.astype(F32), 0.0).astype(BF16)
                out = lax.dot_general(
                    left, right, (((1,), (1,)), ((), ())), preferred_element_type=F32
                )
                total = out if total is None else total + out
            store(k, total)

    def store_own(k, total):
        for z in range(slab):
            own_ref[k, z] = total[z * width_x : (z + 1) * width_x]

    def store_below(k, total):
        below_ref[k] = total

    def store_above(k, total):
        above_ref[k] = total

    fill(0, 0, slab * width_x, 3, store_own)
    fill(1, (slab - 1) * width_x, width_x, 3, store_below)
    fill(2, 0, width_x, 2, store_above)


def inside(c, bounds_ref, z, slab, shape):
    deep = lax.axis_index("gz") * slab + z
    in_z = (deep >= bounds_ref[0, 0]) & (deep < bounds_ref[0, 1])
    line = lax.broadcasted_iota(jnp.int32, shape, 0) + c.at
    column = lax.broadcasted_iota(jnp.int32, shape, 1)
    keep = (line >= bounds_ref[1, 0]) & (line < bounds_ref[1, 1])
    keep = keep & (column >= bounds_ref[2, 0]) & (column < bounds_ref[2, 1])
    return jnp.where(keep & in_z, 1.0, 0.0)


def middle(
    cap,
    e_hbm,
    forward_hbm,
    got_ref,
    h_hbm,
    eps_hbm,
    sigma_hbm,
    chip0_hbm,
    chip1_hbm,
    chip2_hbm,
    far_hbm,
    timing_ref,
    bounds_ref,
    h2_ref,
    e2_ref,
    grad_ref,
    cb_ref,
    forward_ref,
    hout_hbm,
    e_ref,
    h_ref,
    h1_ref,
    e1_ref,
    mat_ref,
    chip_ref,
    far_ref,
    own_ref,
    sbelow_ref,
    sabove_ref,
    fs,
    h2a,
    dza,
    sems,
    out_sems,
):
    pairs = (
        (e_hbm, e_ref),
        (h_hbm, h_ref),
        (far_hbm, far_ref),
        (chip0_hbm, chip_ref.at[0:1]),
        (chip1_hbm, chip_ref.at[1:2]),
        (chip2_hbm, chip_ref.at[2:3]),
        (eps_hbm, mat_ref.at[0]),
        (sigma_hbm, mat_ref.at[1]),
        (forward_hbm, forward_ref),
    )
    copies = [pltpu.make_async_copy(a, b, sems.at[i]) for i, (a, b) in enumerate(pairs)]
    for copy in copies:
        copy.start()
    place_entries(cap, got_ref, own_ref, sbelow_ref, sabove_ref)
    for copy in copies[:2]:
        copy.wait()
    over_rows(e_ref.shape[2], lambda c: magnetic_step(c, e_ref, h_ref, h1_ref))
    for copy in copies[2:-1]:
        copy.wait()
    over_rows(e_ref.shape[2], lambda c: electric_all(c, e_ref, h1_ref, e1_ref, mat_ref))
    slab, width_x = e_ref.shape[1], e_ref.shape[2]
    top = slab - 1
    odd = odd_device()
    has_below = jnp.where(lax.axis_index("gz") > 0, 1.0, 0.0).astype(F32)
    wave0, wave1 = timing_ref[0, 0], timing_ref[0, 1]
    weight0, weight1 = timing_ref[1, 0], timing_ref[1, 1]

    def first(c):
        chip = [c.get(chip_ref, k) for k in range(3)]
        far = [c.get(far_ref, k) for k in range(3)]
        low = [jnp.where(odd, a, b) for a, b in zip(chip, far)]
        high = [jnp.where(odd, b, a) for a, b in zip(chip, far)]
        ex, ey = c.get(e_ref, 0, 0), c.get(e_ref, 1, 0)
        hax = has_below * (low[0] + HALF * ey)
        hay = has_below * (low[1] - HALF * ex)
        cb_a, cb_b = low[2], high[2]
        cb = [c.get(mat_ref, 1, z) for z in range(slab)]
        e1 = [
            [c.get(e1_ref, k, z) - wave0 * cb[z] * c.get(own_ref, k, z) for k in range(3)]
            for z in range(slab)
        ]
        e1[0][0] = e1[0][0] + cb[0] * hay
        e1[0][1] = e1[0][1] - cb[0] * hax
        hx = c.get(h1_ref, 0, top) + HALF * high[1]
        hy = c.get(h1_ref, 1, top) - HALF * high[0]
        c.put(h1_ref, 0, top, hx)
        c.put(h1_ref, 1, top, hy)
        bx_far, bx_chip = c.behind_x(far_ref, 0), c.behind_x(chip_ref, 0)
        bx = jnp.where(odd, bx_far, bx_chip)
        e1[top][0] = e1[top][0] + HALF * cb[top] * high[0]
        e1[top][1] = e1[top][1] + HALF * cb[top] * high[1]
        e1[top][2] = e1[top][2] - HALF * cb[top] * (bx + behind_y(high[1]))
        c.put(fs, 0, cb_b * (hy - wave0 * c.get(sabove_ref, 0)))
        c.put(fs, 1, -cb_b * (hx + wave0 * c.get(sabove_ref, 1)))
        for z in range(slab):
            for k in range(3):
                c.put(e1_ref, k, z, e1[z][k])
        dx = cb_a * (HALF * ex - wave0 * c.get(sbelow_ref, 0))
        dy = cb_a * (HALF * ey - wave0 * c.get(sbelow_ref, 1))
        dz = -cb_a * (
            HALF * (c.behind_x(e_ref, 0, 0) + behind_y(ey)) + wave0 * c.get(sbelow_ref, 2)
        )
        c.put(dza, dz)
        c.put(h2a, 0, has_below * HALF * (ey - dy + e1[0][1] - ahead_y(dz)))
        c.put(h2a, 1, has_below * HALF * (dx - ex - e1[0][0]))

    over_rows(width_x, first)

    def second(c):
        c.put(h2a, 1, c.get(h2a, 1) + has_below * HALF * c.ahead_x(dza))
        for z in range(slab):
            ex, ey, ez = (c.get(e1_ref, k, z) for k in range(3))
            if z < top:
                up_x, up_y = c.get(e1_ref, 0, z + 1) - ex, c.get(e1_ref, 1, z + 1) - ey
            else:
                up_x, up_y = c.get(fs, 0) - ex, c.get(fs, 1) - ey
            hx, hy = c.get(h1_ref, 0, z), c.get(h1_ref, 1, z)
            c.put(h2_ref, 0, z, hx - HALF * (ahead_y(ez) - up_y))
            c.put(h2_ref, 1, z, hy - HALF * (up_x - c.ahead_x(e1_ref, 2, z)))
            hz = c.get(h1_ref, 2, z)
            c.put(h2_ref, 2, z, hz - HALF * (c.ahead_x(e1_ref, 1, z) - ahead_y(ex)))

    over_rows(width_x, second)

    def third(c):
        for z in range(slab):
            ca, cb = c.get(mat_ref, 0, z), c.get(mat_ref, 1, z)
            c.put(cb_ref, z, cb)
            hx, hy, hz = (c.get(h2_ref, k, z) for k in range(3))
            if z > 0:
                down_x, down_y = hx - c.get(h2_ref, 0, z - 1), hy - c.get(h2_ref, 1, z - 1)
            else:
                down_x, down_y = hx - c.get(h2a, 0), hy - c.get(h2a, 1)
            curl = (
                behind_y(hz) - down_y,
                down_x - c.behind_x(h2_ref, 2, z),
                c.behind_x(h2_ref, 1, z) - behind_y(hx),
            )
            dot1, dot2 = 0.0, 0.0
            for k in range(3):
                e1 = c.get(e1_ref, k, z)
                e2 = ca * e1 + cb * (curl[k] - wave1 * c.get(own_ref, k, z))
                c.put(e2_ref, k, z, e2)
                fwd = c.get(forward_ref, k, z)
                dot1 = dot1 + e1 * fwd
                dot2 = dot2 + e2 * fwd
            mask = inside(c, bounds_ref, z, slab, ca.shape)
            c.put(grad_ref, z, mask * (weight0 * dot1 + weight1 * dot2))

    copies[-1].wait()
    pairs = (
        (h2_ref.at[0:2, 0:top], hout_hbm.at[0:2, 0:top]),
        (h2_ref.at[2], hout_hbm.at[2]),
    )
    done = [pltpu.make_async_copy(a, b, out_sems.at[i]) for i, (a, b) in enumerate(pairs)]
    for copy in done:
        copy.start()
    over_rows(width_x, third)
    for copy in done:
        copy.wait()


def last(
    forward_ref,
    h2_ref,
    e2_ref,
    gradp_ref,
    cb_ref,
    chip_ref,
    far_ref,
    timing_ref,
    bounds_ref,
    hin_hbm,
    eout_hbm,
    hout_hbm,
    grad_hbm,
    e_ref,
    h_ref,
    grad_ref,
    sems,
):
    slab, width_x = e2_ref.shape[1], e2_ref.shape[2]
    top = slab - 1
    odd = odd_device()
    weight1 = timing_ref[1, 1]
    part = width_x // PARTS

    def body(c):
        chip = [c.get(chip_ref, k) for k in range(2)]
        far = [c.get(far_ref, k) for k in range(2)]
        low = [jnp.where(odd, a, b) for a, b in zip(chip, far)]
        high = [jnp.where(odd, b, a) for a, b in zip(chip, far)]
        bx = jnp.where(odd, c.behind_x(far_ref, 0), c.behind_x(chip_ref, 0))
        cb_low, cb_top = c.get(cb_ref, 0), HALF * c.get(cb_ref, top)
        more = [[0.0] * 3 for _ in range(slab)]
        more[0][0] = cb_low * low[1]
        more[0][1] = -cb_low * low[0]
        more[top][0] = more[top][0] + cb_top * high[0]
        more[top][1] = more[top][1] + cb_top * high[1]
        more[top][2] = -cb_top * (bx + behind_y(high[1]))
        for z in range(slab):
            dot = 0.0
            for k in range(3):
                e2 = c.get(e2_ref, k, z)
                if k < 2 or z == top:
                    e2 = e2 + more[z][k]
                    dot = dot + more[z][k] * c.get(forward_ref, k, z)
                c.put(e_ref, k, z, e2)
            mask = inside(c, bounds_ref, z, slab, cb_low.shape)
            c.put(grad_ref, z, c.get(gradp_ref, z) + (weight1 * mask) * dot)
        c.put(h_ref, 0, c.get(h2_ref, 0, top) + HALF * high[1])
        c.put(h_ref, 1, c.get(h2_ref, 1, top) - HALF * high[0])

    copies = []
    for g in range(PARTS):
        over_rows(width_x, body, g * part, (g + 1) * part)
        rows = pl.ds(g * part, part)
        pairs = (
            (e_ref.at[:, :, rows], eout_hbm.at[:, :, rows]),
            (h_ref.at[:, rows], hout_hbm.at[0:2, top, rows]),
            (grad_ref.at[:, rows], grad_hbm.at[:, rows]),
        )
        for i, (a, b) in enumerate(pairs):
            copy = pltpu.make_async_copy(a, b, sems.at[g, i])
            copy.start()
            copies.append(copy)
    for copy in copies:
        copy.wait()


def shape(*dims):
    return jax.ShapeDtypeStruct(dims, F32)


def kept(*dims):
    return VMEM(dims, F32)


def sent(*dims):
    return pltpu.HBM(dims, F32)


def call(body, outs, ins, us, limit, scratch=(), in_hbm=(), anywhere=(), aliases=None):
    def place(i, x):
        if i in in_hbm:
            return pl.BlockSpec(memory_space=pltpu.HBM)
        if i in anywhere:
            return pl.BlockSpec(memory_space=pl.ANY)
        return pl.BlockSpec(memory_space=SMEM if x.size < 16 else VMEM)

    ins = [
        pltpu.with_memory_space_constraint(x, pltpu.HBM) if i in in_hbm else x
        for i, x in enumerate(ins)
    ]
    return pl.pallas_call(
        body,
        out_shape=outs,
        in_specs=[place(i, x) for i, x in enumerate(ins)],
        out_specs=jax.tree.map(
            lambda x: pl.BlockSpec(memory_space=getattr(x, "memory_space", VMEM)), outs
        ),
        input_output_aliases=aliases or {},
        scratch_shapes=list(scratch),
        compiler_params=pltpu.CompilerParams(vmem_limit_bytes=limit << 20),
        cost_estimate=pl.CostEstimate(flops=int(us * FLOPS_US), bytes_accessed=0, transcendentals=0),
    )(*ins)


def local(
    e_field,
    h_field,
    forward_field,
    permittivity,
    conductivity,
    owners,
    cells,
    amplitude,
    timing,
    bounds,
):
    slab, wx, wy = permittivity.shape
    peers = lax.axis_size("gz")
    rows = owners.shape[0]
    cap = 2 * rows // peers
    lanes = -(-3 * cap // LANES) * LANES
    cells_all = slab * wx * wy
    chip_pairs = [p for i in range(0, peers - 1, 2) for p in ((i, i + 1), (i + 1, i))]
    far_pairs = [p for i in range(1, peers - 1, 2) for p in ((i, i + 1), (i + 1, i))]

    layer, slabs, fields = (wx, wy), (slab, wx, wy), (3, slab, wx, wy)
    dma = pltpu.SemaphoreType.DMA
    begun = call(
        halves_first,
        sent(3, *layer),
        (e_field, h_field, permittivity, conductivity),
        2,
        56,
        scratch=(
            VMEM((3, *layer), F32),
            VMEM((2, *layer), F32),
            VMEM((2, *layer), F32),
            VMEM((3, *layer), F32),
            dma((PARTS, 4)),
            dma((PARTS,)),
        ),
        in_hbm=(0, 1, 2, 3),
    )
    far1 = lax.ppermute(begun, "gz", far_pairs)
    packed, chip0, chip1, chip2, chip3, far2 = call(
        functools.partial(halves_second, cap),
        (
            sent(peers, 4, lanes),
            sent(1, *layer),
            sent(1, *layer),
            sent(1, *layer),
            sent(2, *layer),
            sent(2, *layer),
        ),
        (
            e_field,
            h_field,
            permittivity,
            conductivity,
            owners.reshape(1, rows),
            cells.reshape(1, rows),
            amplitude,
            begun,
        ),
        3,
        16,
        scratch=(
            VMEM(fields, F32),
            VMEM(fields, F32),
            VMEM((2, *slabs), F32),
            VMEM((5, *layer), F32),
            VMEM((2, *layer), F32),
            VMEM((peers, 4, lanes), F32),
            dma((2,)),
            dma((1,)),
            dma((PARTS, 5)),
        ),
        in_hbm=(2, 3, 7),
    )
    got = lax.all_to_all(packed, "gz", 0, 0, tiled=True)
    far2 = lax.ppermute(far2, "gz", far_pairs)
    chip0, chip1, chip2, chip3 = (
        lax.ppermute(x, "gz", chip_pairs) for x in (chip0, chip1, chip2, chip3)
    )
    h2, e2, grad, cb, forward, h_part = call(
        functools.partial(middle, cap),
        (
            kept(*fields),
            kept(*fields),
            kept(*slabs),
            kept(*slabs),
            kept(*fields),
            sent(*fields),
        ),
        (e_field, forward_field, got, h_field, permittivity, conductivity, chip0, chip1, chip2, far1, timing, bounds),
        6,
        24,
        scratch=(
            VMEM(fields, F32),
            VMEM(fields, F32),
            VMEM(fields, F32),
            VMEM(fields, F32),
            VMEM((2, *slabs), F32),
            VMEM((3, *layer), F32),
            VMEM((3, *layer), F32),
            VMEM(fields, F32),
            VMEM((3, *layer), F32),
            VMEM((2, *layer), F32),
            VMEM((2, *layer), F32),
            VMEM((2, *layer), F32),
            VMEM(layer, F32),
            dma((9,)),
            dma((2,)),
        ),
        in_hbm=(0, 1, 3, 4, 5),
        anywhere=(6, 7, 8, 9),
    )
    return call(
        last,
        (sent(*fields), sent(*fields), sent(*slabs)),
        (forward, h2, e2, grad, cb, chip3, far2, timing, bounds, h_part),
        2.5,
        16,
        scratch=(
            VMEM(fields, F32),
            VMEM((2, *layer), F32),
            VMEM(slabs, F32),
            dma((PARTS, 3)),
        ),
        in_hbm=(9,),
        aliases={9: 1},
    )


def solution(mesh):
    placed = (
        P(None, "gz", "groups", None),
        P(None, "gz", "groups", None),
        P(None, "gz", "groups", None),
        P("gz", "groups", None),
        P("gz", "groups", None),
        P("gz", "groups"),
        P("gz", "groups"),
        P("groups", "gz"),
        P("groups", None),
        P("groups", None),
    )
    return jax.shard_map(
        local,
        mesh=mesh,
        in_specs=placed,
        out_specs=(
            P(None, "gz", "groups", None),
            P(None, "gz", "groups", None),
            P("gz", "groups", None),
        ),
        check_vma=False,
    )
```

```python
import functools

import jax
import jax.numpy as jnp
from jax import lax
from jax.experimental import pallas as pl
from jax.experimental.pallas import tpu as pltpu
from jax.sharding import PartitionSpec as P

STEPS = 2
ROWS = 64
PARTS = 4
FLOPS_US = 1.15e9
LANES = 128
HALF = 0.5
F32 = jnp.float32
BF16 = jnp.bfloat16
VMEM = pltpu.VMEM
SMEM = pltpu.SMEM


def lanes_of(v):
    return lax.broadcasted_iota(jnp.int32, v.shape, 1)


def ahead_y(v):
    last = v.shape[1] - 1
    return jnp.where(lanes_of(v) < last, pltpu.roll(v, last, axis=1), 0.0) - v


def behind_y(v):
    return v - jnp.where(lanes_of(v) > 0, pltpu.roll(v, 1, axis=1), 0.0)


class Chunk:
    def __init__(self, at, size, width_x):
        self.at, self.size, self.width = at, size, width_x

    def get(self, ref, *index):
        return ref[(*index, pl.ds(self.at, self.size), slice(None))]

    def put(self, ref, *index_and_value):
        *index, value = index_and_value
        ref[(*index, pl.ds(self.at, self.size), slice(None))] = value

    def ahead_x(self, ref, *index):
        here = self.get(ref, *index)
        after = pl.multiple_of(jnp.minimum(self.at + self.size, self.width - 8), 8)
        more = ref[(*index, pl.ds(after, 8), slice(None))]
        more = jnp.where(self.at + self.size < self.width, more, 0.0)
        both = jnp.concatenate([here, more], axis=0)
        return pltpu.roll(both, self.size + 7, axis=0)[: self.size] - here

    def behind_x(self, ref, *index):
        here = self.get(ref, *index)
        before = pl.multiple_of(jnp.maximum(self.at - 8, 0), 8)
        more = ref[(*index, pl.ds(before, 8), slice(None))]
        more = jnp.where(self.at > 0, more, 0.0)
        both = jnp.concatenate([more, here], axis=0)
        return here - pltpu.roll(both, 1, axis=0)[8:]


def over_rows(width_x, body, begin=0, end=None):
    end = width_x if end is None else end
    size = next(k for k in (96, 48, 8) if (end - begin) % k == 0)

    def step(i, carry):
        body(Chunk(pl.multiple_of(begin + i * size, 8), size, width_x))
        return carry

    lax.fori_loop(0, (end - begin) // size, step, 0)


def odd_device():
    return lax.rem(lax.axis_index("gz"), 2) == 1


class Half:
    def __init__(self, up, ins, out_hbm, e_ref, h_ref, mat_ref, out_ref, sems, out_sems):
        e_hbm, h_hbm, eps_hbm, sigma_hbm = ins
        self.up, self.width = up, e_hbm.shape[2]
        self.part = self.width // PARTS
        self.refs = e_ref, h_ref, mat_ref, out_ref
        z = e_hbm.shape[1] - 1 if up else 0
        self.copies, self.out = [], []
        for g in range(PARTS):
            rows = pl.ds(g * self.part, self.part)
            pairs = [
                (eps_hbm.at[z, rows], mat_ref.at[0, rows]),
                (sigma_hbm.at[z, rows], mat_ref.at[1, rows]),
            ]
            if up:
                pairs.append((e_hbm.at[:, z, rows], e_ref.at[:, rows]))
                pairs.append((h_hbm.at[0:2, z, rows], h_ref.at[:, rows]))
            else:
                pairs.append((e_hbm.at[0:2, z, rows], out_ref.at[0:2, rows]))
            self.copies.append(
                [pltpu.make_async_copy(a, b, sems.at[g, i]) for i, (a, b) in enumerate(pairs)]
            )
            self.out.append(
                pltpu.make_async_copy(out_ref.at[:, rows], out_hbm.at[:, rows], out_sems.at[g])
            )

    def start(self):
        for copies in self.copies:
            for copy in copies:
                copy.start()

    def body(self, c):
        e_ref, h_ref, mat_ref, out_ref = self.refs
        c.put(out_ref, 2, 1.0 / (2.0 * c.get(mat_ref, 0) + c.get(mat_ref, 1)))
        if self.up:
            ez = c.get(e_ref, 2)
            c.put(out_ref, 0, c.get(h_ref, 0) - HALF * (ahead_y(ez) + c.get(e_ref, 1)))
            c.put(out_ref, 1, c.get(h_ref, 1) + HALF * (c.get(e_ref, 0) + c.ahead_x(e_ref, 2)))

    def finish(self):
        for copy in self.copies[0]:
            copy.wait()
        for g in range(PARTS):
            if g + 1 < PARTS:
                for copy in self.copies[g + 1]:
                    copy.wait()
            over_rows(self.width, self.body, g * self.part, (g + 1) * self.part)
            self.out[g].start()
        for copy in self.out:
            copy.wait()


def start_all(copies):
    for copy in copies:
        copy.start()


def wait_all(copies):
    for copy in copies:
        copy.wait()


def by_parity(when_odd, when_even):
    odd = odd_device()
    pl.when(odd)(when_odd)
    pl.when(jnp.logical_not(odd))(when_even)


def halves_first(e_hbm, h_hbm, eps_hbm, sigma_hbm, far_hbm, *scratch):
    ins = e_hbm, h_hbm, eps_hbm, sigma_hbm

    def run(up):
        half = Half(up, ins, far_hbm, *scratch)
        half.start()
        half.finish()

    by_parity(lambda: run(True), lambda: run(False))


def split3(v):
    one = v.astype(BF16)
    rest = v - one.astype(F32)
    two = rest.astype(BF16)
    three = (rest - two.astype(F32)).astype(BF16)
    return one, two, three


def pack_entries(cap, field, owners_ref, cells_ref, amplitude_ref, packed_ref):
    _, slab, width_x, width_y = field
    top = slab - 1
    peers, _, lanes = packed_ref.shape
    owner, cell, amp = owners_ref[...], cells_ref[...], amplitude_ref[...]
    entries = owner.shape[1]
    named = lax.broadcasted_iota(jnp.int32, (peers, entries), 0) == owner
    hot = named.astype(F32).astype(BF16)
    first = lax.broadcasted_iota(jnp.int32, (entries, entries), 0)
    second = lax.broadcasted_iota(jnp.int32, (entries, entries), 1)
    ahead = (first < second).astype(F32).astype(BF16)
    before = jnp.dot(hot, ahead, preferred_element_type=F32)
    rank = jnp.sum(jnp.where(named, before, 0.0), axis=0, keepdims=True).astype(jnp.int32)
    layer = width_x * width_y
    spread = lambda v: jnp.broadcast_to(v, (8, entries))
    names = (
        spread(owner),
        spread(jnp.where(cell >= top * layer, owner + 1, -1)),
        spread(jnp.where(cell < layer, owner - 1, -1)),
    )
    rows = jnp.concatenate([amp, cell.astype(F32), jnp.zeros((4, entries), F32)], axis=0)
    slot = lax.broadcasted_iota(jnp.int32, (lanes, entries), 0)
    hits = [(slot == rank + k * cap).astype(F32) for k in range(3)]
    place = jnp.concatenate(hits, axis=1).astype(BF16)
    total = None
    for term in split3(rows):
        term = term.astype(F32)
        values = [
            jnp.concatenate([jnp.where(name == d, term, 0.0) for d in range(peers)], axis=0)
            for name in names
        ]
        values = jnp.concatenate(values, axis=1).astype(BF16)
        out = lax.dot_general(values, place, (((1,), (1,)), ((), ())), preferred_element_type=F32)
        total = out if total is None else total + out
    for d in range(peers):
        packed_ref[d] = total[d * 8 : d * 8 + 4]


def magnetic_step(c, e_ref, h_ref, h1_ref):
    slab = e_ref.shape[1]
    for z in range(slab):
        ex, ey, ez = (c.get(e_ref, k, z) for k in range(3))
        up_x = c.get(e_ref, 0, z + 1) - ex if z + 1 < slab else -ex
        up_y = c.get(e_ref, 1, z + 1) - ey if z + 1 < slab else -ey
        c.put(h1_ref, 0, z, c.get(h_ref, 0, z) - HALF * (ahead_y(ez) - up_y))
        c.put(h1_ref, 1, z, c.get(h_ref, 1, z) - HALF * (up_x - c.ahead_x(e_ref, 2, z)))
        c.put(h1_ref, 2, z, c.get(h_ref, 2, z) - HALF * (c.ahead_x(e_ref, 1, z) - ahead_y(ex)))


def electric_step(c, z, comps, e_ref, h1_ref, ca, cb):
    hx, hy, hz = (c.get(h1_ref, k, z) for k in range(3))
    down_x = hx - c.get(h1_ref, 0, z - 1) if z > 0 else hx
    down_y = hy - c.get(h1_ref, 1, z - 1) if z > 0 else hy
    ex = ca * c.get(e_ref, 0, z) + cb * (behind_y(hz) - down_y)
    ey = ca * c.get(e_ref, 1, z) + cb * (down_x - c.behind_x(h1_ref, 2, z))
    if comps == 2:
        return ex, ey
    ez = ca * c.get(e_ref, 2, z) + cb * (c.behind_x(h1_ref, 1, z) - behind_y(hx))
    return ex, ey, ez


def electric_all(c, e_ref, h1_ref, e1_ref, mat_ref):
    for z in range(e_ref.shape[1]):
        eps, sigma = c.get(mat_ref, 0, z), c.get(mat_ref, 1, z)
        cb = 1.0 / (2.0 * eps + sigma)
        ca = (2.0 * eps - sigma) * cb
        c.put(mat_ref, 0, z, ca)
        c.put(mat_ref, 1, z, cb)
        for k, v in enumerate(electric_step(c, z, 3, e_ref, h1_ref, ca, cb)):
            c.put(e1_ref, k, z, v)


def halves_second(
    cap,
    e_ref,
    h_ref,
    eps_hbm,
    sigma_hbm,
    owners_ref,
    cells_ref,
    amplitude_ref,
    after_hbm,
    packed_hbm,
    chip0_hbm,
    chip1_hbm,
    far_hbm,
    h1_ref,
    e1_ref,
    mat_ref,
    chip_ref,
    far_ref,
    packed_ref,
    in_sems,
    step_sems,
    out_sems,
):
    slab, width_x = e_ref.shape[1], e_ref.shape[2]
    top = slab - 1
    odd = odd_device()
    copies = [
        pltpu.make_async_copy(a, mat_ref.at[i], in_sems.at[i])
        for i, a in enumerate((eps_hbm, sigma_hbm))
    ]
    for copy in copies:
        copy.start()
    pack_entries(cap, e_ref.shape, owners_ref, cells_ref, amplitude_ref, packed_ref)
    out = [pltpu.make_async_copy(packed_ref, packed_hbm, step_sems.at[0])]
    out[0].start()
    over_rows(width_x, lambda c: magnetic_step(c, e_ref, h_ref, h1_ref))
    for copy in copies:
        copy.wait()

    over_rows(width_x, lambda c: electric_all(c, e_ref, h1_ref, e1_ref, mat_ref))

    def boundary(c):
        ex, ey, ez = (c.get(e1_ref, k, top) for k in range(3))
        hx = c.get(h1_ref, 0, top) - HALF * (ahead_y(ez) + ey)
        hy = c.get(h1_ref, 1, top) + HALF * (ex + c.ahead_x(e1_ref, 2, top))
        upward = (
            c.get(h1_ref, 0, top),
            c.get(h1_ref, 1, top),
            c.get(mat_ref, 1, top),
            hx,
            hy,
        )
        downward = (
            c.get(e_ref, 0, 0),
            c.get(e_ref, 1, 0),
            c.get(mat_ref, 1, 0),
            c.get(e1_ref, 0, 0),
            c.get(e1_ref, 1, 0),
        )
        for k in range(5):
            c.put(chip_ref, k, jnp.where(odd, downward[k], upward[k]))
        for k in range(2):
            c.put(far_ref, k, jnp.where(odd, upward[k + 3], downward[k + 3]))

    part = width_x // PARTS
    for g in range(PARTS):
        over_rows(width_x, boundary, g * part, (g + 1) * part)
        rows = pl.ds(g * part, part)
        pairs = (
            (far_ref, far_hbm),
            (chip_ref.at[0:3], chip0_hbm),
            (chip_ref.at[3:5], chip1_hbm),
        )
        for i, (a, b) in enumerate(pairs):
            out.append(pltpu.make_async_copy(a.at[:, rows], b.at[:, rows], out_sems.at[g, i]))
            out[-1].start()
    for copy in out:
        copy.wait()


def place_entries(cap, got_ref, own_ref, below_ref, above_ref):
    peers, _, lanes = got_ref.shape
    slab, width_x, width_y = own_ref.shape[1:]
    group = LANES // cap
    part = lax.broadcasted_iota(jnp.int32, (4, LANES), 1) // cap

    def row_of(segment):
        blocks = []
        for g in range(0, peers, group):
            block = jnp.zeros((4, LANES), F32)
            for p in range(min(group, peers - g)):
                shift = ((p - segment) * cap) % LANES
                there = got_ref[g + p]
                there = pltpu.roll(there, shift, axis=1) if shift else there
                block = jnp.where(part == p, there, block)
            blocks.append(block)
        return jnp.concatenate(blocks, axis=1)

    def fill(segment, first_line, lines, comps, store):
        row = row_of(segment)
        count = row.shape[1]
        cell = row[3:4].astype(jnp.int32)
        line = cell // width_y
        column = cell - line * width_y
        line = line - first_line
        where_line = lax.broadcasted_iota(jnp.int32, (lines, count), 0) == line
        left = where_line.astype(F32).astype(BF16)
        where_column = lax.broadcasted_iota(jnp.int32, (width_y, count), 0) == column
        for k in range(comps):
            total = None
            for term in split3(row[k : k + 1]):
                right = jnp.where(where_column, term.astype(F32), 0.0).astype(BF16)
                out = lax.dot_general(
                    left, right, (((1,), (1,)), ((), ())), preferred_element_type=F32
                )
                total = out if total is None else total + out
            store(k, total)

    def store_own(k, total):
        for z in range(slab):
            own_ref[k, z] = total[z * width_x : (z + 1) * width_x]

    def store_below(k, total):
        below_ref[k] = total

    def store_above(k, total):
        above_ref[k] = total

    fill(0, 0, slab * width_x, 3, store_own)
    fill(1, (slab - 1) * width_x, width_x, 3, store_below)
    fill(2, 0, width_x, 2, store_above)


def inside(c, bounds_ref, z, slab, shape):
    deep = lax.axis_index("gz") * slab + z
    in_z = (deep >= bounds_ref[0, 0]) & (deep < bounds_ref[0, 1])
    line = lax.broadcasted_iota(jnp.int32, shape, 0) + c.at
    column = lax.broadcasted_iota(jnp.int32, shape, 1)
    keep = (line >= bounds_ref[1, 0]) & (line < bounds_ref[1, 1])
    keep = keep & (column >= bounds_ref[2, 0]) & (column < bounds_ref[2, 1])
    return jnp.where(keep & in_z, 1.0, 0.0)


def middle(
    cap,
    e_ref,
    forward_hbm,
    got_ref,
    h_ref,
    eps_hbm,
    sigma_hbm,
    chip0_hbm,
    chip1_hbm,
    far_hbm,
    timing_ref,
    bounds_ref,
    h2_ref,
    e2_ref,
    grad_ref,
    cb_ref,
    forward_ref,
    eout_hbm,
    hout_hbm,
    gout_hbm,
    h1_ref,
    e1_ref,
    mat_ref,
    chip_ref,
    far_ref,
    own_ref,
    sbelow_ref,
    sabove_ref,
    fs,
    h2a,
    dza,
    sems,
    out_sems,
    odd_sems,
    even_sems,
):
    pairs = (
        (far_hbm, far_ref),
        (chip0_hbm, chip_ref.at[0:3]),
        (chip1_hbm, chip_ref.at[3:5]),
        (eps_hbm, mat_ref.at[0]),
        (sigma_hbm, mat_ref.at[1]),
        (forward_hbm, forward_ref),
    )
    copies = [pltpu.make_async_copy(a, b, sems.at[i]) for i, (a, b) in enumerate(pairs)]
    for copy in copies:
        copy.start()
    place_entries(cap, got_ref, own_ref, sbelow_ref, sabove_ref)
    over_rows(e_ref.shape[2], lambda c: magnetic_step(c, e_ref, h_ref, h1_ref))
    for copy in copies[:-1]:
        copy.wait()
    over_rows(e_ref.shape[2], lambda c: electric_all(c, e_ref, h1_ref, e1_ref, mat_ref))
    slab, width_x = e_ref.shape[1], e_ref.shape[2]
    top = slab - 1
    odd = odd_device()
    has_below = jnp.where(lax.axis_index("gz") > 0, 1.0, 0.0).astype(F32)
    wave0, wave1 = timing_ref[0, 0], timing_ref[0, 1]
    weight0, weight1 = timing_ref[1, 0], timing_ref[1, 1]

    def first(c):
        chip = [c.get(chip_ref, k) for k in range(3)]
        far = [c.get(far_ref, k) for k in range(3)]
        low = [jnp.where(odd, a, b) for a, b in zip(chip, far)]
        high = [jnp.where(odd, b, a) for a, b in zip(chip, far)]
        ex, ey = c.get(e_ref, 0, 0), c.get(e_ref, 1, 0)
        hax = has_below * (low[0] + HALF * ey)
        hay = has_below * (low[1] - HALF * ex)
        cb_a, cb_b = low[2], high[2]
        cb = [c.get(mat_ref, 1, z) for z in range(slab)]
        e1 = [
            [c.get(e1_ref, k, z) - wave0 * cb[z] * c.get(own_ref, k, z) for k in range(3)]
            for z in range(slab)
        ]
        e1[0][0] = e1[0][0] + cb[0] * hay
        e1[0][1] = e1[0][1] - cb[0] * hax
        hx = c.get(h1_ref, 0, top) + HALF * high[1]
        hy = c.get(h1_ref, 1, top) - HALF * high[0]
        c.put(h1_ref, 0, top, hx)
        c.put(h1_ref, 1, top, hy)
        bx_far, bx_chip = c.behind_x(far_ref, 0), c.behind_x(chip_ref, 0)
        bx = jnp.where(odd, bx_far, bx_chip)
        e1[top][0] = e1[top][0] + HALF * cb[top] * high[0]
        e1[top][1] = e1[top][1] + HALF * cb[top] * high[1]
        e1[top][2] = e1[top][2] - HALF * cb[top] * (bx + behind_y(high[1]))
        from_chip = [c.get(chip_ref, k) for k in (3, 4)]
        beside = [jnp.where(odd, 0.0, v) for v in from_chip]
        c.put(fs, 0, beside[0] + cb_b * (hy - wave0 * c.get(sabove_ref, 0)))
        c.put(fs, 1, beside[1] - cb_b * (hx + wave0 * c.get(sabove_ref, 1)))
        for z in range(slab):
            for k in range(3):
                c.put(e1_ref, k, z, e1[z][k])
        dx = cb_a * (HALF * ex - wave0 * c.get(sbelow_ref, 0))
        dy = cb_a * (HALF * ey - wave0 * c.get(sbelow_ref, 1))
        dz = -cb_a * (
            HALF * (c.behind_x(e_ref, 0, 0) + behind_y(ey)) + wave0 * c.get(sbelow_ref, 2)
        )
        c.put(dza, dz)
        beside = [jnp.where(odd, v, 0.0) for v in from_chip]
        c.put(h2a, 0, beside[0] + has_below * HALF * (ey - dy + e1[0][1] - ahead_y(dz)))
        c.put(h2a, 1, beside[1] + has_below * HALF * (dx - ex - e1[0][0]))

    over_rows(width_x, first)

    def second(c):
        c.put(h2a, 1, c.get(h2a, 1) + has_below * HALF * c.ahead_x(dza))
        for z in range(slab):
            ex, ey, ez = (c.get(e1_ref, k, z) for k in range(3))
            if z < top:
                up_x, up_y = c.get(e1_ref, 0, z + 1) - ex, c.get(e1_ref, 1, z + 1) - ey
            else:
                up_x, up_y = c.get(fs, 0) - ex, c.get(fs, 1) - ey
            hx, hy = c.get(h1_ref, 0, z), c.get(h1_ref, 1, z)
            c.put(h2_ref, 0, z, hx - HALF * (ahead_y(ez) - up_y))
            c.put(h2_ref, 1, z, hy - HALF * (up_x - c.ahead_x(e1_ref, 2, z)))
            hz = c.get(h1_ref, 2, z)
            c.put(h2_ref, 2, z, hz - HALF * (c.ahead_x(e1_ref, 1, z) - ahead_y(ex)))

    over_rows(width_x, second)

    def third(c):
        for z in range(slab):
            ca, cb = c.get(mat_ref, 0, z), c.get(mat_ref, 1, z)
            c.put(cb_ref, z, cb)
            hx, hy, hz = (c.get(h2_ref, k, z) for k in range(3))
            if z > 0:
                down_x, down_y = hx - c.get(h2_ref, 0, z - 1), hy - c.get(h2_ref, 1, z - 1)
            else:
                down_x, down_y = hx - c.get(h2a, 0), hy - c.get(h2a, 1)
            curl = (
                behind_y(hz) - down_y,
                down_x - c.behind_x(h2_ref, 2, z),
                c.behind_x(h2_ref, 1, z) - behind_y(hx),
            )
            dot1, dot2 = 0.0, 0.0
            for k in range(3):
                e1 = c.get(e1_ref, k, z)
                e2 = ca * e1 + cb * (curl[k] - wave1 * c.get(own_ref, k, z))
                c.put(e2_ref, k, z, e2)
                fwd = c.get(forward_ref, k, z)
                dot1 = dot1 + e1 * fwd
                dot2 = dot2 + e2 * fwd
            mask = inside(c, bounds_ref, z, slab, ca.shape)
            c.put(grad_ref, z, mask * (weight0 * dot1 + weight1 * dot2))

    copies[-1].wait()

    def copies_of(pairs, sems):
        return [pltpu.make_async_copy(a, b, sems.at[i]) for i, (a, b) in enumerate(pairs)]

    done = copies_of(
        (
            (h2_ref.at[0:2, 0:top], hout_hbm.at[0:2, 0:top]),
            (h2_ref.at[2], hout_hbm.at[2]),
        ),
        out_sems,
    )
    for copy in done:
        copy.start()
    part = width_x // 2
    odd_copies, even_copies = [], []
    for g in range(2):
        over_rows(width_x, third, g * part, (g + 1) * part)
        rows = pl.ds(g * part, part)
        for_odd = copies_of(
            (
                (e2_ref.at[:, 0:top, rows], eout_hbm.at[:, 0:top, rows]),
                (grad_ref.at[0:top, rows], gout_hbm.at[0:top, rows]),
            ),
            odd_sems.at[g],
        )
        for_even = copies_of(
            (
                (e2_ref.at[:, 1:slab, rows], eout_hbm.at[:, 1:slab, rows]),
                (grad_ref.at[1:slab, rows], gout_hbm.at[1:slab, rows]),
                (h2_ref.at[0:2, top, rows], hout_hbm.at[0:2, top, rows]),
                (e2_ref.at[2, 0, rows], eout_hbm.at[2, 0, rows]),
            ),
            even_sems.at[g],
        )
        by_parity(lambda: start_all(for_odd), lambda: start_all(for_even))
        odd_copies, even_copies = odd_copies + for_odd, even_copies + for_even
    by_parity(lambda: wait_all(odd_copies), lambda: wait_all(even_copies))
    wait_all(done)


def last(
    forward_ref,
    h2_ref,
    e2_ref,
    gradp_ref,
    cb_ref,
    far_ref,
    timing_ref,
    bounds_ref,
    ein_hbm,
    hin_hbm,
    gin_hbm,
    eout_hbm,
    hout_hbm,
    grad_hbm,
    e_ref,
    h_ref,
    grad_ref,
    sems,
):
    slab, width_x = e2_ref.shape[1], e2_ref.shape[2]
    top = slab - 1
    weight1 = timing_ref[1, 1]
    part = width_x // PARTS

    def finish(c, z, deltas):
        dot = 0.0
        for k, delta in enumerate(deltas):
            dot = dot + delta * c.get(forward_ref, k, z)
            c.put(e_ref, k, c.get(e2_ref, k, z) + delta)
        mask = inside(c, bounds_ref, z, slab, dot.shape)
        c.put(grad_ref, c.get(gradp_ref, z) + (weight1 * mask) * dot)

    def above(c):
        fx, fy = c.get(far_ref, 0), c.get(far_ref, 1)
        cb = HALF * c.get(cb_ref, top)
        finish(c, top, (cb * fx, cb * fy, -cb * (c.behind_x(far_ref, 0) + behind_y(fy))))
        c.put(h_ref, 0, c.get(h2_ref, 0, top) + HALF * fy)
        c.put(h_ref, 1, c.get(h2_ref, 1, top) - HALF * fx)

    def below(c):
        cb = c.get(cb_ref, 0)
        finish(c, 0, (cb * c.get(far_ref, 1), -cb * c.get(far_ref, 0)))

    def run(z, body, comps, with_h):
        copies = []
        for g in range(PARTS):
            over_rows(width_x, body, g * part, (g + 1) * part)
            rows = pl.ds(g * part, part)
            pairs = [
                (e_ref.at[0:comps, rows], eout_hbm.at[0:comps, z, rows]),
                (grad_ref.at[rows], grad_hbm.at[z, rows]),
            ]
            if with_h:
                pairs.append((h_ref.at[:, rows], hout_hbm.at[0:2, z, rows]))
            for i, (a, b) in enumerate(pairs):
                copies.append(pltpu.make_async_copy(a, b, sems.at[g, i]))
                copies[-1].start()
        for copy in copies:
            copy.wait()

    by_parity(lambda: run(top, above, 3, True), lambda: run(0, below, 2, False))


def settle(near_hbm, far_hbm, out_hbm, near_ref, sem):
    copy = pltpu.make_async_copy(near_hbm.at[0, 0:8], near_ref, sem)
    copy.start()
    copy.wait()


def shape(*dims):
    return jax.ShapeDtypeStruct(dims, F32)


def kept(*dims):
    return VMEM(dims, F32)


def sent(*dims):
    return pltpu.HBM(dims, F32)


def call(body, outs, ins, us, limit, scratch=(), in_hbm=(), anywhere=(), aliases=None):
    def place(i, x):
        if i in in_hbm:
            return pl.BlockSpec(memory_space=pltpu.HBM)
        if i in anywhere:
            return pl.BlockSpec(memory_space=pl.ANY)
        return pl.BlockSpec(memory_space=SMEM if x.size < 16 else VMEM)

    ins = [
        pltpu.with_memory_space_constraint(x, pltpu.HBM) if i in in_hbm else x
        for i, x in enumerate(ins)
    ]
    return pl.pallas_call(
        body,
        out_shape=outs,
        in_specs=[place(i, x) for i, x in enumerate(ins)],
        out_specs=jax.tree.map(
            lambda x: pl.BlockSpec(memory_space=getattr(x, "memory_space", VMEM)), outs
        ),
        input_output_aliases=aliases or {},
        scratch_shapes=list(scratch),
        compiler_params=pltpu.CompilerParams(vmem_limit_bytes=limit << 20),
        cost_estimate=pl.CostEstimate(flops=int(us * FLOPS_US), bytes_accessed=0, transcendentals=0),
    )(*ins)


def local(
    e_field,
    h_field,
    forward_field,
    permittivity,
    conductivity,
    owners,
    cells,
    amplitude,
    timing,
    bounds,
):
    slab, wx, wy = permittivity.shape
    peers = lax.axis_size("gz")
    rows = owners.shape[0]
    cap = 2 * rows // peers
    lanes = -(-3 * cap // LANES) * LANES
    cells_all = slab * wx * wy
    chip_pairs = [p for i in range(0, peers - 1, 2) for p in ((i, i + 1), (i + 1, i))]
    far_pairs = [p for i in range(1, peers - 1, 2) for p in ((i, i + 1), (i + 1, i))]

    layer, slabs, fields = (wx, wy), (slab, wx, wy), (3, slab, wx, wy)
    dma = pltpu.SemaphoreType.DMA
    begun = call(
        halves_first,
        sent(3, *layer),
        (e_field, h_field, permittivity, conductivity),
        2,
        56,
        scratch=(
            VMEM((3, *layer), F32),
            VMEM((2, *layer), F32),
            VMEM((2, *layer), F32),
            VMEM((3, *layer), F32),
            dma((PARTS, 4)),
            dma((PARTS,)),
        ),
        in_hbm=(0, 1, 2, 3),
    )
    far1 = lax.ppermute(begun, "gz", far_pairs)
    packed, chip0, chip1, far2 = call(
        functools.partial(halves_second, cap),
        (
            sent(peers, 4, lanes),
            sent(3, *layer),
            sent(2, *layer),
            sent(2, *layer),
        ),
        (
            e_field,
            h_field,
            permittivity,
            conductivity,
            owners.reshape(1, rows),
            cells.reshape(1, rows),
            amplitude,
            begun,
        ),
        3,
        16,
        scratch=(
            VMEM(fields, F32),
            VMEM(fields, F32),
            VMEM((2, *slabs), F32),
            VMEM((5, *layer), F32),
            VMEM((2, *layer), F32),
            VMEM((peers, 4, lanes), F32),
            dma((2,)),
            dma((1,)),
            dma((PARTS, 3)),
        ),
        in_hbm=(2, 3, 7),
    )
    got = lax.all_to_all(packed, "gz", 0, 0, tiled=True)
    far2 = call(
        settle,
        sent(2, *layer),
        (chip1, far2),
        3,
        8,
        scratch=(VMEM((8, wy), F32), dma),
        in_hbm=(0, 1),
        aliases={1: 0},
    )
    far2 = lax.ppermute(far2, "gz", far_pairs)
    chip0, chip1 = (
        lax.ppermute(x, "gz", chip_pairs) for x in (chip0, chip1)
    )
    h2, e2, grad, cb, forward, e_part, h_part, grad_part = call(
        functools.partial(middle, cap),
        (
            kept(*fields),
            kept(*fields),
            kept(*slabs),
            kept(*slabs),
            kept(*fields),
            sent(*fields),
            sent(*fields),
            sent(*slabs),
        ),
        (
            e_field,
            forward_field,
            got,
            h_field,
            permittivity,
            conductivity,
            chip0,
            chip1,
            far1,
            timing,
            bounds,
        ),
        6,
        24,
        scratch=(
            VMEM(fields, F32),
            VMEM(fields, F32),
            VMEM((2, *slabs), F32),
            VMEM((5, *layer), F32),
            VMEM((3, *layer), F32),
            VMEM(fields, F32),
            VMEM((3, *layer), F32),
            VMEM((2, *layer), F32),
            VMEM((2, *layer), F32),
            VMEM((2, *layer), F32),
            VMEM(layer, F32),
            dma((6,)),
            dma((2,)),
            dma((2, 2)),
            dma((2, 4)),
        ),
        in_hbm=(1, 4, 5, 6, 7),
        anywhere=(8,),
    )
    return call(
        last,
        (sent(*fields), sent(*fields), sent(*slabs)),
        (forward, h2, e2, grad, cb, far2, timing, bounds, e_part, h_part, grad_part),
        2.5,
        16,
        scratch=(
            VMEM((3, *layer), F32),
            VMEM((2, *layer), F32),
            VMEM(layer, F32),
            dma((PARTS, 3)),
        ),
        in_hbm=(8, 9, 10),
        aliases={8: 0, 9: 1, 10: 2},
    )


def solution(mesh):
    placed = (
        P(None, "gz", "groups", None),
        P(None, "gz", "groups", None),
        P(None, "gz", "groups", None),
        P("gz", "groups", None),
        P("gz", "groups", None),
        P("gz", "groups"),
        P("gz", "groups"),
        P("groups", "gz"),
        P("groups", None),
        P("groups", None),
    )
    return jax.shard_map(
        local,
        mesh=mesh,
        in_specs=placed,
        out_specs=(
            P(None, "gz", "groups", None),
            P(None, "gz", "groups", None),
            P("gz", "groups", None),
        ),
        check_vma=False,
    )
```

```python
import functools

import jax
import jax.numpy as jnp
from jax import lax
from jax.experimental import pallas as pl
from jax.experimental.pallas import tpu as pltpu
from jax.sharding import PartitionSpec as P

STEPS = 2
ROWS = 64
PARTS = 4
FLOPS_US = 1.15e9
LANES = 128
HALF = 0.5
F32 = jnp.float32
BF16 = jnp.bfloat16
VMEM = pltpu.VMEM
SMEM = pltpu.SMEM


def lanes_of(v):
    return lax.broadcasted_iota(jnp.int32, v.shape, 1)


def ahead_y(v):
    last = v.shape[1] - 1
    return jnp.where(lanes_of(v) < last, pltpu.roll(v, last, axis=1), 0.0) - v


def behind_y(v):
    return v - jnp.where(lanes_of(v) > 0, pltpu.roll(v, 1, axis=1), 0.0)


class Chunk:
    def __init__(self, at, size, width_x):
        self.at, self.size, self.width = at, size, width_x

    def get(self, ref, *index):
        return ref[(*index, pl.ds(self.at, self.size), slice(None))]

    def put(self, ref, *index_and_value):
        *index, value = index_and_value
        ref[(*index, pl.ds(self.at, self.size), slice(None))] = value

    def ahead_x(self, ref, *index):
        here = self.get(ref, *index)
        after = pl.multiple_of(jnp.minimum(self.at + self.size, self.width - 8), 8)
        more = ref[(*index, pl.ds(after, 8), slice(None))]
        more = jnp.where(self.at + self.size < self.width, more, 0.0)
        both = jnp.concatenate([here, more], axis=0)
        return pltpu.roll(both, self.size + 7, axis=0)[: self.size] - here

    def behind_x(self, ref, *index):
        here = self.get(ref, *index)
        before = pl.multiple_of(jnp.maximum(self.at - 8, 0), 8)
        more = ref[(*index, pl.ds(before, 8), slice(None))]
        more = jnp.where(self.at > 0, more, 0.0)
        both = jnp.concatenate([more, here], axis=0)
        return here - pltpu.roll(both, 1, axis=0)[8:]


def over_rows(width_x, body, begin=0, end=None):
    end = width_x if end is None else end
    size = next(k for k in (96, 48, 8) if (end - begin) % k == 0)

    def step(i, carry):
        body(Chunk(pl.multiple_of(begin + i * size, 8), size, width_x))
        return carry

    lax.fori_loop(0, (end - begin) // size, step, 0)


def odd_device():
    return lax.rem(lax.axis_index("gz"), 2) == 1


class Half:
    def __init__(self, up, ins, out_hbm, e_ref, h_ref, mat_ref, out_ref, sems, out_sems):
        e_hbm, h_hbm, eps_hbm, sigma_hbm = ins
        self.up, self.width = up, e_hbm.shape[2]
        self.part = self.width // PARTS
        self.refs = e_ref, h_ref, mat_ref, out_ref
        z = e_hbm.shape[1] - 1 if up else 0
        self.copies, self.out = [], []
        for g in range(PARTS):
            rows = pl.ds(g * self.part, self.part)
            pairs = [
                (eps_hbm.at[z, rows], mat_ref.at[0, rows]),
                (sigma_hbm.at[z, rows], mat_ref.at[1, rows]),
            ]
            if up:
                pairs.append((e_hbm.at[:, z, rows], e_ref.at[:, rows]))
                pairs.append((h_hbm.at[0:2, z, rows], h_ref.at[:, rows]))
            else:
                pairs.append((e_hbm.at[0:2, z, rows], out_ref.at[0:2, rows]))
            self.copies.append(
                [pltpu.make_async_copy(a, b, sems.at[g, i]) for i, (a, b) in enumerate(pairs)]
            )
            self.out.append(
                pltpu.make_async_copy(out_ref.at[:, rows], out_hbm.at[:, rows], out_sems.at[g])
            )

    def start(self):
        for copies in self.copies:
            for copy in copies:
                copy.start()

    def body(self, c):
        e_ref, h_ref, mat_ref, out_ref = self.refs
        c.put(out_ref, 2, 1.0 / (2.0 * c.get(mat_ref, 0) + c.get(mat_ref, 1)))
        if self.up:
            ez = c.get(e_ref, 2)
            c.put(out_ref, 0, c.get(h_ref, 0) - HALF * (ahead_y(ez) + c.get(e_ref, 1)))
            c.put(out_ref, 1, c.get(h_ref, 1) + HALF * (c.get(e_ref, 0) + c.ahead_x(e_ref, 2)))

    def finish(self):
        for copy in self.copies[0]:
            copy.wait()
        for g in range(PARTS):
            if g + 1 < PARTS:
                for copy in self.copies[g + 1]:
                    copy.wait()
            over_rows(self.width, self.body, g * self.part, (g + 1) * self.part)
            self.out[g].start()
        for copy in self.out:
            copy.wait()


def start_all(copies):
    for copy in copies:
        copy.start()


def wait_all(copies):
    for copy in copies:
        copy.wait()


def by_parity(when_odd, when_even):
    odd = odd_device()
    pl.when(odd)(when_odd)
    pl.when(jnp.logical_not(odd))(when_even)


def halves_first(e_hbm, h_hbm, eps_hbm, sigma_hbm, far_hbm, *scratch):
    ins = e_hbm, h_hbm, eps_hbm, sigma_hbm

    def run(up):
        half = Half(up, ins, far_hbm, *scratch)
        half.start()
        half.finish()

    by_parity(lambda: run(True), lambda: run(False))


def split3(v):
    one = v.astype(BF16)
    rest = v - one.astype(F32)
    two = rest.astype(BF16)
    three = (rest - two.astype(F32)).astype(BF16)
    return one, two, three


def pack_entries(cap, field, owners_ref, cells_ref, amplitude_ref, packed_ref):
    _, slab, width_x, width_y = field
    top = slab - 1
    peers, _, lanes = packed_ref.shape
    owner, cell, amp = owners_ref[...], cells_ref[...], amplitude_ref[...]
    entries = owner.shape[1]
    named = lax.broadcasted_iota(jnp.int32, (peers, entries), 0) == owner
    hot = named.astype(F32).astype(BF16)
    first = lax.broadcasted_iota(jnp.int32, (entries, entries), 0)
    second = lax.broadcasted_iota(jnp.int32, (entries, entries), 1)
    ahead = (first < second).astype(F32).astype(BF16)
    before = jnp.dot(hot, ahead, preferred_element_type=F32)
    rank = jnp.sum(jnp.where(named, before, 0.0), axis=0, keepdims=True).astype(jnp.int32)
    layer = width_x * width_y
    spread = lambda v: jnp.broadcast_to(v, (8, entries))
    names = (
        spread(owner),
        spread(jnp.where(cell >= top * layer, owner + 1, -1)),
        spread(jnp.where(cell < layer, owner - 1, -1)),
    )
    rows = jnp.concatenate([amp, cell.astype(F32), jnp.zeros((4, entries), F32)], axis=0)
    slot = lax.broadcasted_iota(jnp.int32, (lanes, entries), 0)
    hits = [(slot == rank + k * cap).astype(F32) for k in range(3)]
    place = jnp.concatenate(hits, axis=1).astype(BF16)
    total = None
    for term in split3(rows):
        term = term.astype(F32)
        values = [
            jnp.concatenate([jnp.where(name == d, term, 0.0) for d in range(peers)], axis=0)
            for name in names
        ]
        values = jnp.concatenate(values, axis=1).astype(BF16)
        out = lax.dot_general(values, place, (((1,), (1,)), ((), ())), preferred_element_type=F32)
        total = out if total is None else total + out
    for d in range(peers):
        packed_ref[d] = total[d * 8 : d * 8 + 4]


def magnetic_step(c, e_ref, h_ref, h1_ref):
    slab = e_ref.shape[1]
    for z in range(slab):
        ex, ey, ez = (c.get(e_ref, k, z) for k in range(3))
        up_x = c.get(e_ref, 0, z + 1) - ex if z + 1 < slab else -ex
        up_y = c.get(e_ref, 1, z + 1) - ey if z + 1 < slab else -ey
        c.put(h1_ref, 0, z, c.get(h_ref, 0, z) - HALF * (ahead_y(ez) - up_y))
        c.put(h1_ref, 1, z, c.get(h_ref, 1, z) - HALF * (up_x - c.ahead_x(e_ref, 2, z)))
        c.put(h1_ref, 2, z, c.get(h_ref, 2, z) - HALF * (c.ahead_x(e_ref, 1, z) - ahead_y(ex)))


def electric_step(c, z, comps, e_ref, h1_ref, ca, cb):
    hx, hy, hz = (c.get(h1_ref, k, z) for k in range(3))
    down_x = hx - c.get(h1_ref, 0, z - 1) if z > 0 else hx
    down_y = hy - c.get(h1_ref, 1, z - 1) if z > 0 else hy
    ex = ca * c.get(e_ref, 0, z) + cb * (behind_y(hz) - down_y)
    ey = ca * c.get(e_ref, 1, z) + cb * (down_x - c.behind_x(h1_ref, 2, z))
    if comps == 2:
        return ex, ey
    ez = ca * c.get(e_ref, 2, z) + cb * (c.behind_x(h1_ref, 1, z) - behind_y(hx))
    return ex, ey, ez


def electric_all(c, e_ref, h1_ref, e1_ref, mat_ref):
    for z in range(e_ref.shape[1]):
        eps, sigma = c.get(mat_ref, 0, z), c.get(mat_ref, 1, z)
        cb = 1.0 / (2.0 * eps + sigma)
        ca = (2.0 * eps - sigma) * cb
        c.put(mat_ref, 0, z, ca)
        c.put(mat_ref, 1, z, cb)
        for k, v in enumerate(electric_step(c, z, 3, e_ref, h1_ref, ca, cb)):
            c.put(e1_ref, k, z, v)


def halves_second(
    cap,
    e_ref,
    h_ref,
    eps_hbm,
    sigma_hbm,
    owners_ref,
    cells_ref,
    amplitude_ref,
    after_hbm,
    packed_hbm,
    chip0_hbm,
    chip1_hbm,
    far_hbm,
    h1_ref,
    e1_ref,
    mat_ref,
    chip_ref,
    far_ref,
    packed_ref,
    in_sems,
    step_sems,
    out_sems,
):
    slab, width_x = e_ref.shape[1], e_ref.shape[2]
    top = slab - 1
    odd = odd_device()
    copies = [
        pltpu.make_async_copy(a, mat_ref.at[i], in_sems.at[i])
        for i, a in enumerate((eps_hbm, sigma_hbm))
    ]
    for copy in copies:
        copy.start()
    pack_entries(cap, e_ref.shape, owners_ref, cells_ref, amplitude_ref, packed_ref)
    out = [pltpu.make_async_copy(packed_ref, packed_hbm, step_sems.at[0])]
    out[0].start()
    over_rows(width_x, lambda c: magnetic_step(c, e_ref, h_ref, h1_ref))
    for copy in copies:
        copy.wait()

    over_rows(width_x, lambda c: electric_all(c, e_ref, h1_ref, e1_ref, mat_ref))

    def boundary(c):
        ex, ey, ez = (c.get(e1_ref, k, top) for k in range(3))
        hx = c.get(h1_ref, 0, top) - HALF * (ahead_y(ez) + ey)
        hy = c.get(h1_ref, 1, top) + HALF * (ex + c.ahead_x(e1_ref, 2, top))
        upward = (
            c.get(h1_ref, 0, top),
            c.get(h1_ref, 1, top),
            c.get(mat_ref, 1, top),
            hx,
            hy,
        )
        downward = (
            c.get(e_ref, 0, 0),
            c.get(e_ref, 1, 0),
            c.get(mat_ref, 1, 0),
            c.get(e1_ref, 0, 0),
            c.get(e1_ref, 1, 0),
        )
        for k in range(5):
            c.put(chip_ref, k, jnp.where(odd, downward[k], upward[k]))
        for k in range(2):
            c.put(far_ref, k, jnp.where(odd, upward[k + 3], downward[k + 3]))

    part = width_x // PARTS
    for g in range(PARTS):
        over_rows(width_x, boundary, g * part, (g + 1) * part)
        rows = pl.ds(g * part, part)
        pairs = (
            (far_ref, far_hbm),
            (chip_ref.at[0:3], chip0_hbm),
            (chip_ref.at[3:5], chip1_hbm),
        )
        for i, (a, b) in enumerate(pairs):
            out.append(pltpu.make_async_copy(a.at[:, rows], b.at[:, rows], out_sems.at[g, i]))
            out[-1].start()
    for copy in out:
        copy.wait()


def place_entries(cap, got_ref, own_ref, below_ref, above_ref):
    peers, _, lanes = got_ref.shape
    slab, width_x, width_y = own_ref.shape[1:]
    group = LANES // cap
    part = lax.broadcasted_iota(jnp.int32, (4, LANES), 1) // cap

    def row_of(segment):
        blocks = []
        for g in range(0, peers, group):
            block = jnp.zeros((4, LANES), F32)
            for p in range(min(group, peers - g)):
                shift = ((p - segment) * cap) % LANES
                there = got_ref[g + p]
                there = pltpu.roll(there, shift, axis=1) if shift else there
                block = jnp.where(part == p, there, block)
            blocks.append(block)
        return jnp.concatenate(blocks, axis=1)

    def fill(segment, first_line, lines, comps, store):
        row = row_of(segment)
        count = row.shape[1]
        cell = row[3:4].astype(jnp.int32)
        line = cell // width_y
        column = cell - line * width_y
        line = line - first_line
        where_line = lax.broadcasted_iota(jnp.int32, (lines, count), 0) == line
        left = where_line.astype(F32).astype(BF16)
        where_column = lax.broadcasted_iota(jnp.int32, (width_y, count), 0) == column
        for k in range(comps):
            total = None
            for term in split3(row[k : k + 1]):
                right = jnp.where(where_column, term.astype(F32), 0.0).astype(BF16)
                out = lax.dot_general(
                    left, right, (((1,), (1,)), ((), ())), preferred_element_type=F32
                )
                total = out if total is None else total + out
            store(k, total)

    def store_own(k, total):
        for z in range(slab):
            own_ref[k, z] = total[z * width_x : (z + 1) * width_x]

    def store_below(k, total):
        below_ref[k] = total

    def store_above(k, total):
        above_ref[k] = total

    fill(0, 0, slab * width_x, 3, store_own)
    fill(1, (slab - 1) * width_x, width_x, 3, store_below)
    fill(2, 0, width_x, 2, store_above)


def inside(c, bounds_ref, z, slab, shape):
    deep = lax.axis_index("gz") * slab + z
    in_z = (deep >= bounds_ref[0, 0]) & (deep < bounds_ref[0, 1])
    line = lax.broadcasted_iota(jnp.int32, shape, 0) + c.at
    column = lax.broadcasted_iota(jnp.int32, shape, 1)
    keep = (line >= bounds_ref[1, 0]) & (line < bounds_ref[1, 1])
    keep = keep & (column >= bounds_ref[2, 0]) & (column < bounds_ref[2, 1])
    return jnp.where(keep & in_z, 1.0, 0.0)


def middle(
    cap,
    e_ref,
    forward_hbm,
    got_ref,
    h_ref,
    eps_hbm,
    sigma_hbm,
    chip0_hbm,
    chip1_hbm,
    far_hbm,
    timing_ref,
    bounds_ref,
    h2_ref,
    e2_ref,
    grad_ref,
    cb_ref,
    share_ref,
    forward_ref,
    eout_hbm,
    hout_hbm,
    gout_hbm,
    h1_ref,
    e1_ref,
    mat_ref,
    chip_ref,
    far_ref,
    own_ref,
    sbelow_ref,
    sabove_ref,
    fs,
    h2a,
    dza,
    sems,
    out_sems,
    odd_sems,
    even_sems,
):
    pairs = (
        (far_hbm, far_ref),
        (chip0_hbm, chip_ref.at[0:3]),
        (chip1_hbm, chip_ref.at[3:5]),
        (eps_hbm, mat_ref.at[0]),
        (sigma_hbm, mat_ref.at[1]),
        (forward_hbm, forward_ref),
    )
    copies = [pltpu.make_async_copy(a, b, sems.at[i]) for i, (a, b) in enumerate(pairs)]
    for copy in copies:
        copy.start()
    place_entries(cap, got_ref, own_ref, sbelow_ref, sabove_ref)
    over_rows(e_ref.shape[2], lambda c: magnetic_step(c, e_ref, h_ref, h1_ref))
    for copy in copies[:-1]:
        copy.wait()
    over_rows(e_ref.shape[2], lambda c: electric_all(c, e_ref, h1_ref, e1_ref, mat_ref))
    slab, width_x = e_ref.shape[1], e_ref.shape[2]
    top = slab - 1
    odd = odd_device()
    has_below = jnp.where(lax.axis_index("gz") > 0, 1.0, 0.0).astype(F32)
    wave0, wave1 = timing_ref[0, 0], timing_ref[0, 1]
    weight0, weight1 = timing_ref[1, 0], timing_ref[1, 1]

    def first(c):
        chip = [c.get(chip_ref, k) for k in range(3)]
        far = [c.get(far_ref, k) for k in range(3)]
        low = [jnp.where(odd, a, b) for a, b in zip(chip, far)]
        high = [jnp.where(odd, b, a) for a, b in zip(chip, far)]
        ex, ey = c.get(e_ref, 0, 0), c.get(e_ref, 1, 0)
        hax = has_below * (low[0] + HALF * ey)
        hay = has_below * (low[1] - HALF * ex)
        cb_a, cb_b = low[2], high[2]
        cb = [c.get(mat_ref, 1, z) for z in range(slab)]
        e1 = [
            [c.get(e1_ref, k, z) - wave0 * cb[z] * c.get(own_ref, k, z) for k in range(3)]
            for z in range(slab)
        ]
        e1[0][0] = e1[0][0] + cb[0] * hay
        e1[0][1] = e1[0][1] - cb[0] * hax
        hx = c.get(h1_ref, 0, top) + HALF * high[1]
        hy = c.get(h1_ref, 1, top) - HALF * high[0]
        c.put(h1_ref, 0, top, hx)
        c.put(h1_ref, 1, top, hy)
        bx_far, bx_chip = c.behind_x(far_ref, 0), c.behind_x(chip_ref, 0)
        bx = jnp.where(odd, bx_far, bx_chip)
        e1[top][0] = e1[top][0] + HALF * cb[top] * high[0]
        e1[top][1] = e1[top][1] + HALF * cb[top] * high[1]
        e1[top][2] = e1[top][2] - HALF * cb[top] * (bx + behind_y(high[1]))
        from_chip = [c.get(chip_ref, k) for k in (3, 4)]
        beside = [jnp.where(odd, 0.0, v) for v in from_chip]
        c.put(fs, 0, beside[0] + cb_b * (hy - wave0 * c.get(sabove_ref, 0)))
        c.put(fs, 1, beside[1] - cb_b * (hx + wave0 * c.get(sabove_ref, 1)))
        for z in range(slab):
            for k in range(3):
                c.put(e1_ref, k, z, e1[z][k])
        dx = cb_a * (HALF * ex - wave0 * c.get(sbelow_ref, 0))
        dy = cb_a * (HALF * ey - wave0 * c.get(sbelow_ref, 1))
        dz = -cb_a * (
            HALF * (c.behind_x(e_ref, 0, 0) + behind_y(ey)) + wave0 * c.get(sbelow_ref, 2)
        )
        c.put(dza, dz)
        beside = [jnp.where(odd, v, 0.0) for v in from_chip]
        c.put(h2a, 0, beside[0] + has_below * HALF * (ey - dy + e1[0][1] - ahead_y(dz)))
        c.put(h2a, 1, beside[1] + has_below * HALF * (dx - ex - e1[0][0]))

    over_rows(width_x, first)

    def second(c):
        c.put(h2a, 1, c.get(h2a, 1) + has_below * HALF * c.ahead_x(dza))
        for z in range(slab):
            ex, ey, ez = (c.get(e1_ref, k, z) for k in range(3))
            if z < top:
                up_x, up_y = c.get(e1_ref, 0, z + 1) - ex, c.get(e1_ref, 1, z + 1) - ey
            else:
                up_x, up_y = c.get(fs, 0) - ex, c.get(fs, 1) - ey
            hx, hy = c.get(h1_ref, 0, z), c.get(h1_ref, 1, z)
            c.put(h2_ref, 0, z, hx - HALF * (ahead_y(ez) - up_y))
            c.put(h2_ref, 1, z, hy - HALF * (up_x - c.ahead_x(e1_ref, 2, z)))
            hz = c.get(h1_ref, 2, z)
            c.put(h2_ref, 2, z, hz - HALF * (c.ahead_x(e1_ref, 1, z) - ahead_y(ex)))

    over_rows(width_x, second)

    def third(c):
        for z in range(slab):
            ca, cb = c.get(mat_ref, 0, z), c.get(mat_ref, 1, z)
            c.put(cb_ref, z, cb)
            hx, hy, hz = (c.get(h2_ref, k, z) for k in range(3))
            if z > 0:
                down_x, down_y = hx - c.get(h2_ref, 0, z - 1), hy - c.get(h2_ref, 1, z - 1)
            else:
                down_x, down_y = hx - c.get(h2a, 0), hy - c.get(h2a, 1)
            curl = (
                behind_y(hz) - down_y,
                down_x - c.behind_x(h2_ref, 2, z),
                c.behind_x(h2_ref, 1, z) - behind_y(hx),
            )
            dot1, dot2 = 0.0, 0.0
            for k in range(3):
                e1 = c.get(e1_ref, k, z)
                e2 = ca * e1 + cb * (curl[k] - wave1 * c.get(own_ref, k, z))
                c.put(e2_ref, k, z, e2)
                fwd = c.get(forward_ref, k, z)
                dot1 = dot1 + e1 * fwd
                dot2 = dot2 + e2 * fwd
            mask = inside(c, bounds_ref, z, slab, ca.shape)
            c.put(share_ref, z, weight1 * mask)
            c.put(grad_ref, z, mask * (weight0 * dot1 + weight1 * dot2))

    copies[-1].wait()

    def copies_of(pairs, sems):
        return [pltpu.make_async_copy(a, b, sems.at[i]) for i, (a, b) in enumerate(pairs)]

    done = copies_of(
        (
            (h2_ref.at[0:2, 0:top], hout_hbm.at[0:2, 0:top]),
            (h2_ref.at[2], hout_hbm.at[2]),
        ),
        out_sems,
    )
    for copy in done:
        copy.start()
    part = width_x // 2
    odd_copies, even_copies = [], []
    for g in range(2):
        over_rows(width_x, third, g * part, (g + 1) * part)
        rows = pl.ds(g * part, part)
        for_odd = copies_of(
            (
                (e2_ref.at[:, 0:top, rows], eout_hbm.at[:, 0:top, rows]),
                (grad_ref.at[0:top, rows], gout_hbm.at[0:top, rows]),
            ),
            odd_sems.at[g],
        )
        for_even = copies_of(
            (
                (e2_ref.at[:, 1:slab, rows], eout_hbm.at[:, 1:slab, rows]),
                (grad_ref.at[1:slab, rows], gout_hbm.at[1:slab, rows]),
                (h2_ref.at[0:2, top, rows], hout_hbm.at[0:2, top, rows]),
                (e2_ref.at[2, 0, rows], eout_hbm.at[2, 0, rows]),
            ),
            even_sems.at[g],
        )
        by_parity(lambda: start_all(for_odd), lambda: start_all(for_even))
        odd_copies, even_copies = odd_copies + for_odd, even_copies + for_even
    by_parity(lambda: wait_all(odd_copies), lambda: wait_all(even_copies))
    wait_all(done)


def last(
    forward_ref,
    h2_ref,
    e2_ref,
    gradp_ref,
    cb_ref,
    share_ref,
    far_ref,
    ein_hbm,
    hin_hbm,
    gin_hbm,
    eout_hbm,
    hout_hbm,
    grad_hbm,
    e_ref,
    h_ref,
    grad_ref,
    sems,
):
    slab, width_x = e2_ref.shape[1], e2_ref.shape[2]
    top = slab - 1
    part = width_x // PARTS

    def finish(c, z, deltas):
        dot = 0.0
        for k, delta in enumerate(deltas):
            dot = dot + delta * c.get(forward_ref, k, z)
            c.put(e_ref, k, c.get(e2_ref, k, z) + delta)
        c.put(grad_ref, c.get(gradp_ref, z) + c.get(share_ref, z) * dot)

    def above(c):
        fx, fy = c.get(far_ref, 0), c.get(far_ref, 1)
        cb = HALF * c.get(cb_ref, top)
        finish(c, top, (cb * fx, cb * fy, -cb * (c.behind_x(far_ref, 0) + behind_y(fy))))
        c.put(h_ref, 0, c.get(h2_ref, 0, top) + HALF * fy)
        c.put(h_ref, 1, c.get(h2_ref, 1, top) - HALF * fx)

    def below(c):
        cb = c.get(cb_ref, 0)
        finish(c, 0, (cb * c.get(far_ref, 1), -cb * c.get(far_ref, 0)))

    def run(z, body, comps, with_h):
        copies = []
        for g in range(PARTS):
            over_rows(width_x, body, g * part, (g + 1) * part)
            rows = pl.ds(g * part, part)
            pairs = [
                (e_ref.at[0:comps, rows], eout_hbm.at[0:comps, z, rows]),
                (grad_ref.at[rows], grad_hbm.at[z, rows]),
            ]
            if with_h:
                pairs.append((h_ref.at[:, rows], hout_hbm.at[0:2, z, rows]))
            for i, (a, b) in enumerate(pairs):
                copies.append(pltpu.make_async_copy(a, b, sems.at[g, i]))
                copies[-1].start()
        for copy in copies:
            copy.wait()

    by_parity(lambda: run(top, above, 3, True), lambda: run(0, below, 2, False))


def settle(near_hbm, far_hbm, out_hbm, near_ref, sem):
    copy = pltpu.make_async_copy(near_hbm.at[0, 0:8], near_ref, sem)
    copy.start()
    copy.wait()


def shape(*dims):
    return jax.ShapeDtypeStruct(dims, F32)


def kept(*dims):
    return VMEM(dims, F32)


def sent(*dims):
    return pltpu.HBM(dims, F32)


def call(body, outs, ins, us, limit, scratch=(), in_hbm=(), anywhere=(), aliases=None):
    def place(i, x):
        if i in in_hbm:
            return pl.BlockSpec(memory_space=pltpu.HBM)
        if i in anywhere:
            return pl.BlockSpec(memory_space=pl.ANY)
        return pl.BlockSpec(memory_space=SMEM if x.size < 16 else VMEM)

    ins = [
        pltpu.with_memory_space_constraint(x, pltpu.HBM) if i in in_hbm else x
        for i, x in enumerate(ins)
    ]
    return pl.pallas_call(
        body,
        out_shape=outs,
        in_specs=[place(i, x) for i, x in enumerate(ins)],
        out_specs=jax.tree.map(
            lambda x: pl.BlockSpec(memory_space=getattr(x, "memory_space", VMEM)), outs
        ),
        input_output_aliases=aliases or {},
        scratch_shapes=list(scratch),
        compiler_params=pltpu.CompilerParams(vmem_limit_bytes=limit << 20),
        cost_estimate=pl.CostEstimate(flops=int(us * FLOPS_US), bytes_accessed=0, transcendentals=0),
    )(*ins)


def local(
    e_field,
    h_field,
    forward_field,
    permittivity,
    conductivity,
    owners,
    cells,
    amplitude,
    timing,
    bounds,
):
    slab, wx, wy = permittivity.shape
    peers = lax.axis_size("gz")
    rows = owners.shape[0]
    cap = 2 * rows // peers
    lanes = -(-3 * cap // LANES) * LANES
    cells_all = slab * wx * wy
    chip_pairs = [p for i in range(0, peers - 1, 2) for p in ((i, i + 1), (i + 1, i))]
    far_pairs = [p for i in range(1, peers - 1, 2) for p in ((i, i + 1), (i + 1, i))]

    layer, slabs, fields = (wx, wy), (slab, wx, wy), (3, slab, wx, wy)
    dma = pltpu.SemaphoreType.DMA
    begun = call(
        halves_first,
        sent(3, *layer),
        (e_field, h_field, permittivity, conductivity),
        2,
        56,
        scratch=(
            VMEM((3, *layer), F32),
            VMEM((2, *layer), F32),
            VMEM((2, *layer), F32),
            VMEM((3, *layer), F32),
            dma((PARTS, 4)),
            dma((PARTS,)),
        ),
        in_hbm=(0, 1, 2, 3),
    )
    far1 = lax.ppermute(begun, "gz", far_pairs)
    packed, chip0, chip1, far2 = call(
        functools.partial(halves_second, cap),
        (
            sent(peers, 4, lanes),
            sent(3, *layer),
            sent(2, *layer),
            sent(2, *layer),
        ),
        (
            e_field,
            h_field,
            permittivity,
            conductivity,
            owners.reshape(1, rows),
            cells.reshape(1, rows),
            amplitude,
            begun,
        ),
        3,
        16,
        scratch=(
            VMEM(fields, F32),
            VMEM(fields, F32),
            VMEM((2, *slabs), F32),
            VMEM((5, *layer), F32),
            VMEM((2, *layer), F32),
            VMEM((peers, 4, lanes), F32),
            dma((2,)),
            dma((1,)),
            dma((PARTS, 3)),
        ),
        in_hbm=(2, 3, 7),
    )
    got = lax.all_to_all(packed, "gz", 0, 0, tiled=True)
    far2 = call(
        settle,
        sent(2, *layer),
        (chip1, far2),
        3,
        8,
        scratch=(VMEM((8, wy), F32), dma),
        in_hbm=(0, 1),
        aliases={1: 0},
    )
    far2 = lax.ppermute(far2, "gz", far_pairs)
    chip0, chip1 = (
        lax.ppermute(x, "gz", chip_pairs) for x in (chip0, chip1)
    )
    h2, e2, grad, cb, share, forward, e_part, h_part, grad_part = call(
        functools.partial(middle, cap),
        (
            kept(*fields),
            kept(*fields),
            kept(*slabs),
            kept(*slabs),
            kept(*slabs),
            kept(*fields),
            sent(*fields),
            sent(*fields),
            sent(*slabs),
        ),
        (
            e_field,
            forward_field,
            got,
            h_field,
            permittivity,
            conductivity,
            chip0,
            chip1,
            far1,
            timing,
            bounds,
        ),
        6,
        24,
        scratch=(
            VMEM(fields, F32),
            VMEM(fields, F32),
            VMEM((2, *slabs), F32),
            VMEM((5, *layer), F32),
            VMEM((3, *layer), F32),
            VMEM(fields, F32),
            VMEM((3, *layer), F32),
            VMEM((2, *layer), F32),
            VMEM((2, *layer), F32),
            VMEM((2, *layer), F32),
            VMEM(layer, F32),
            dma((6,)),
            dma((2,)),
            dma((2, 2)),
            dma((2, 4)),
        ),
        in_hbm=(1, 4, 5, 6, 7),
        anywhere=(8,),
    )
    return call(
        last,
        (sent(*fields), sent(*fields), sent(*slabs)),
        (forward, h2, e2, grad, cb, share, far2, e_part, h_part, grad_part),
        2.5,
        16,
        scratch=(
            VMEM((3, *layer), F32),
            VMEM((2, *layer), F32),
            VMEM(layer, F32),
            dma((PARTS, 3)),
        ),
        in_hbm=(7, 8, 9),
        aliases={7: 0, 8: 1, 9: 2},
    )


def solution(mesh):
    placed = (
        P(None, "gz", "groups", None),
        P(None, "gz", "groups", None),
        P(None, "gz", "groups", None),
        P("gz", "groups", None),
        P("gz", "groups", None),
        P("gz", "groups"),
        P("gz", "groups"),
        P("groups", "gz"),
        P("groups", None),
        P("groups", None),
    )
    return jax.shard_map(
        local,
        mesh=mesh,
        in_specs=placed,
        out_specs=(
            P(None, "gz", "groups", None),
            P(None, "gz", "groups", None),
            P("gz", "groups", None),
        ),
        check_vma=False,
    )
```

```python
import functools

import jax
import jax.numpy as jnp
from jax import lax
from jax.experimental import pallas as pl
from jax.experimental.pallas import tpu as pltpu
from jax.sharding import PartitionSpec as P

STEPS = 2
ROWS = 64
PARTS = 4
FLOPS_US = 1.15e9
LANES = 128
HALF = 0.5
F32 = jnp.float32
BF16 = jnp.bfloat16
VMEM = pltpu.VMEM
SMEM = pltpu.SMEM


def lanes_of(v):
    return lax.broadcasted_iota(jnp.int32, v.shape, 1)


def ahead_y(v):
    last = v.shape[1] - 1
    return jnp.where(lanes_of(v) < last, pltpu.roll(v, last, axis=1), 0.0) - v


def behind_y(v):
    return v - jnp.where(lanes_of(v) > 0, pltpu.roll(v, 1, axis=1), 0.0)


class Chunk:
    def __init__(self, at, size, width_x):
        self.at, self.size, self.width = at, size, width_x

    def get(self, ref, *index):
        return ref[(*index, pl.ds(self.at, self.size), slice(None))]

    def put(self, ref, *index_and_value):
        *index, value = index_and_value
        ref[(*index, pl.ds(self.at, self.size), slice(None))] = value

    def ahead_x(self, ref, *index):
        here = self.get(ref, *index)
        after = pl.multiple_of(jnp.minimum(self.at + self.size, self.width - 8), 8)
        more = ref[(*index, pl.ds(after, 8), slice(None))]
        more = jnp.where(self.at + self.size < self.width, more, 0.0)
        both = jnp.concatenate([here, more], axis=0)
        return pltpu.roll(both, self.size + 7, axis=0)[: self.size] - here

    def behind_x(self, ref, *index):
        here = self.get(ref, *index)
        before = pl.multiple_of(jnp.maximum(self.at - 8, 0), 8)
        more = ref[(*index, pl.ds(before, 8), slice(None))]
        more = jnp.where(self.at > 0, more, 0.0)
        both = jnp.concatenate([more, here], axis=0)
        return here - pltpu.roll(both, 1, axis=0)[8:]


def over_rows(width_x, body, begin=0, end=None):
    end = width_x if end is None else end
    size = next(k for k in (96, 48, 8) if (end - begin) % k == 0)

    def step(i, carry):
        body(Chunk(pl.multiple_of(begin + i * size, 8), size, width_x))
        return carry

    lax.fori_loop(0, (end - begin) // size, step, 0)


def odd_device():
    return lax.rem(lax.axis_index("gz"), 2) == 1


class Half:
    def __init__(self, up, ins, out_hbm, e_ref, h_ref, mat_ref, out_ref, sems, out_sems):
        e_hbm, h_hbm, eps_hbm, sigma_hbm = ins
        self.up, self.width = up, e_hbm.shape[2]
        self.part = self.width // PARTS
        self.refs = e_ref, h_ref, mat_ref, out_ref
        z = e_hbm.shape[1] - 1 if up else 0
        self.copies, self.out = [], []
        for g in range(PARTS):
            rows = pl.ds(g * self.part, self.part)
            pairs = [
                (eps_hbm.at[z, rows], mat_ref.at[0, rows]),
                (sigma_hbm.at[z, rows], mat_ref.at[1, rows]),
            ]
            if up:
                pairs.append((e_hbm.at[:, z, rows], e_ref.at[:, rows]))
                pairs.append((h_hbm.at[0:2, z, rows], h_ref.at[:, rows]))
            else:
                pairs.append((e_hbm.at[0:2, z, rows], out_ref.at[0:2, rows]))
            self.copies.append(
                [pltpu.make_async_copy(a, b, sems.at[g, i]) for i, (a, b) in enumerate(pairs)]
            )
            self.out.append(
                pltpu.make_async_copy(out_ref.at[:, rows], out_hbm.at[:, rows], out_sems.at[g])
            )

    def start(self):
        for copies in self.copies:
            for copy in copies:
                copy.start()

    def body(self, c):
        e_ref, h_ref, mat_ref, out_ref = self.refs
        c.put(out_ref, 2, 1.0 / (2.0 * c.get(mat_ref, 0) + c.get(mat_ref, 1)))
        if self.up:
            ez = c.get(e_ref, 2)
            c.put(out_ref, 0, c.get(h_ref, 0) - HALF * (ahead_y(ez) + c.get(e_ref, 1)))
            c.put(out_ref, 1, c.get(h_ref, 1) + HALF * (c.get(e_ref, 0) + c.ahead_x(e_ref, 2)))

    def finish(self):
        for copy in self.copies[0]:
            copy.wait()
        for g in range(PARTS):
            if g + 1 < PARTS:
                for copy in self.copies[g + 1]:
                    copy.wait()
            over_rows(self.width, self.body, g * self.part, (g + 1) * self.part)
            self.out[g].start()
        for copy in self.out:
            copy.wait()


def start_all(copies):
    for copy in copies:
        copy.start()


def wait_all(copies):
    for copy in copies:
        copy.wait()


def by_parity(when_odd, when_even):
    odd = odd_device()
    pl.when(odd)(when_odd)
    pl.when(jnp.logical_not(odd))(when_even)


def halves_first(e_hbm, h_hbm, eps_hbm, sigma_hbm, far_hbm, *scratch):
    ins = e_hbm, h_hbm, eps_hbm, sigma_hbm

    def run(up):
        half = Half(up, ins, far_hbm, *scratch)
        half.start()
        half.finish()

    by_parity(lambda: run(True), lambda: run(False))


def split3(v):
    one = v.astype(BF16)
    rest = v - one.astype(F32)
    two = rest.astype(BF16)
    three = (rest - two.astype(F32)).astype(BF16)
    return one, two, three


def pack_entries(cap, field, owners_ref, cells_ref, amplitude_ref, packed_ref):
    _, slab, width_x, width_y = field
    top = slab - 1
    peers, _, lanes = packed_ref.shape
    owner, cell, amp = owners_ref[...], cells_ref[...], amplitude_ref[...]
    entries = owner.shape[1]
    named = lax.broadcasted_iota(jnp.int32, (peers, entries), 0) == owner
    hot = named.astype(F32).astype(BF16)
    first = lax.broadcasted_iota(jnp.int32, (entries, entries), 0)
    second = lax.broadcasted_iota(jnp.int32, (entries, entries), 1)
    ahead = (first < second).astype(F32).astype(BF16)
    before = jnp.dot(hot, ahead, preferred_element_type=F32)
    rank = jnp.sum(jnp.where(named, before, 0.0), axis=0, keepdims=True).astype(jnp.int32)
    layer = width_x * width_y
    spread = lambda v: jnp.broadcast_to(v, (8, entries))
    names = (
        spread(owner),
        spread(jnp.where(cell >= top * layer, owner + 1, -1)),
        spread(jnp.where(cell < layer, owner - 1, -1)),
    )
    rows = jnp.concatenate([amp, cell.astype(F32), jnp.zeros((4, entries), F32)], axis=0)
    slot = lax.broadcasted_iota(jnp.int32, (lanes, entries), 0)
    hits = [(slot == rank + k * cap).astype(F32) for k in range(3)]
    place = jnp.concatenate(hits, axis=1).astype(BF16)
    total = None
    for term in split3(rows):
        term = term.astype(F32)
        values = [
            jnp.concatenate([jnp.where(name == d, term, 0.0) for d in range(peers)], axis=0)
            for name in names
        ]
        values = jnp.concatenate(values, axis=1).astype(BF16)
        out = lax.dot_general(values, place, (((1,), (1,)), ((), ())), preferred_element_type=F32)
        total = out if total is None else total + out
    for d in range(peers):
        packed_ref[d] = total[d * 8 : d * 8 + 4]


def magnetic_step(c, e_ref, h_ref, h1_ref):
    slab = e_ref.shape[1]
    for z in range(slab):
        ex, ey, ez = (c.get(e_ref, k, z) for k in range(3))
        up_x = c.get(e_ref, 0, z + 1) - ex if z + 1 < slab else -ex
        up_y = c.get(e_ref, 1, z + 1) - ey if z + 1 < slab else -ey
        c.put(h1_ref, 0, z, c.get(h_ref, 0, z) - HALF * (ahead_y(ez) - up_y))
        c.put(h1_ref, 1, z, c.get(h_ref, 1, z) - HALF * (up_x - c.ahead_x(e_ref, 2, z)))
        c.put(h1_ref, 2, z, c.get(h_ref, 2, z) - HALF * (c.ahead_x(e_ref, 1, z) - ahead_y(ex)))


def electric_step(c, z, comps, e_ref, h1_ref, ca, cb):
    hx, hy, hz = (c.get(h1_ref, k, z) for k in range(3))
    down_x = hx - c.get(h1_ref, 0, z - 1) if z > 0 else hx
    down_y = hy - c.get(h1_ref, 1, z - 1) if z > 0 else hy
    ex = ca * c.get(e_ref, 0, z) + cb * (behind_y(hz) - down_y)
    ey = ca * c.get(e_ref, 1, z) + cb * (down_x - c.behind_x(h1_ref, 2, z))
    if comps == 2:
        return ex, ey
    ez = ca * c.get(e_ref, 2, z) + cb * (c.behind_x(h1_ref, 1, z) - behind_y(hx))
    return ex, ey, ez


def electric_all(c, e_ref, h1_ref, e1_ref, mat_ref):
    for z in range(e_ref.shape[1]):
        eps, sigma = c.get(mat_ref, 0, z), c.get(mat_ref, 1, z)
        cb = 1.0 / (2.0 * eps + sigma)
        ca = (2.0 * eps - sigma) * cb
        c.put(mat_ref, 0, z, ca)
        c.put(mat_ref, 1, z, cb)
        for k, v in enumerate(electric_step(c, z, 3, e_ref, h1_ref, ca, cb)):
            c.put(e1_ref, k, z, v)


def halves_second(
    cap,
    e_ref,
    h_ref,
    eps_hbm,
    sigma_hbm,
    owners_ref,
    cells_ref,
    amplitude_ref,
    after_hbm,
    packed_hbm,
    chip0_hbm,
    chip1_hbm,
    far_hbm,
    h1_ref,
    e1_ref,
    mat_ref,
    chip_ref,
    far_ref,
    packed_ref,
    in_sems,
    step_sems,
    out_sems,
):
    slab, width_x = e_ref.shape[1], e_ref.shape[2]
    top = slab - 1
    odd = odd_device()
    copies = [
        pltpu.make_async_copy(a, mat_ref.at[i], in_sems.at[i])
        for i, a in enumerate((eps_hbm, sigma_hbm))
    ]
    for copy in copies:
        copy.start()
    pack_entries(cap, e_ref.shape, owners_ref, cells_ref, amplitude_ref, packed_ref)
    out = [pltpu.make_async_copy(packed_ref, packed_hbm, step_sems.at[0])]
    out[0].start()
    over_rows(width_x, lambda c: magnetic_step(c, e_ref, h_ref, h1_ref))
    for copy in copies:
        copy.wait()

    over_rows(width_x, lambda c: electric_all(c, e_ref, h1_ref, e1_ref, mat_ref))

    def boundary(c):
        ex, ey, ez = (c.get(e1_ref, k, top) for k in range(3))
        hx = c.get(h1_ref, 0, top) - HALF * (ahead_y(ez) + ey)
        hy = c.get(h1_ref, 1, top) + HALF * (ex + c.ahead_x(e1_ref, 2, top))
        upward = (
            c.get(h1_ref, 0, top),
            c.get(h1_ref, 1, top),
            c.get(mat_ref, 1, top),
            hx,
            hy,
        )
        downward = (
            c.get(e_ref, 0, 0),
            c.get(e_ref, 1, 0),
            c.get(mat_ref, 1, 0),
            c.get(e1_ref, 0, 0),
            c.get(e1_ref, 1, 0),
        )
        for k in range(5):
            c.put(chip_ref, k, jnp.where(odd, downward[k], upward[k]))
        for k in range(2):
            c.put(far_ref, k, jnp.where(odd, upward[k + 3], downward[k + 3]))

    part = width_x // PARTS
    for g in range(PARTS):
        over_rows(width_x, boundary, g * part, (g + 1) * part)
        rows = pl.ds(g * part, part)
        pairs = (
            (far_ref, far_hbm),
            (chip_ref.at[0:3], chip0_hbm),
            (chip_ref.at[3:5], chip1_hbm),
        )
        for i, (a, b) in enumerate(pairs):
            out.append(pltpu.make_async_copy(a.at[:, rows], b.at[:, rows], out_sems.at[g, i]))
            out[-1].start()
    for copy in out:
        copy.wait()


def place_entries(cap, got_ref, own_ref, below_ref, above_ref):
    peers, _, lanes = got_ref.shape
    slab, width_x, width_y = own_ref.shape[1:]
    group = LANES // cap
    part = lax.broadcasted_iota(jnp.int32, (4, LANES), 1) // cap

    def row_of(segment):
        blocks = []
        for g in range(0, peers, group):
            block = jnp.zeros((4, LANES), F32)
            for p in range(min(group, peers - g)):
                shift = ((p - segment) * cap) % LANES
                there = got_ref[g + p]
                there = pltpu.roll(there, shift, axis=1) if shift else there
                block = jnp.where(part == p, there, block)
            blocks.append(block)
        return jnp.concatenate(blocks, axis=1)

    def fill(segment, first_line, lines, comps, store):
        row = row_of(segment)
        count = row.shape[1]
        cell = row[3:4].astype(jnp.int32)
        line = cell // width_y
        column = cell - line * width_y
        line = line - first_line
        where_line = lax.broadcasted_iota(jnp.int32, (lines, count), 0) == line
        left = where_line.astype(F32).astype(BF16)
        where_column = lax.broadcasted_iota(jnp.int32, (width_y, count), 0) == column
        for k in range(comps):
            total = None
            for term in split3(row[k : k + 1]):
                right = jnp.where(where_column, term.astype(F32), 0.0).astype(BF16)
                out = lax.dot_general(
                    left, right, (((1,), (1,)), ((), ())), preferred_element_type=F32
                )
                total = out if total is None else total + out
            store(k, total)

    def store_own(k, total):
        for z in range(slab):
            own_ref[k, z] = total[z * width_x : (z + 1) * width_x]

    def store_below(k, total):
        below_ref[k] = total

    def store_above(k, total):
        above_ref[k] = total

    fill(0, 0, slab * width_x, 3, store_own)
    fill(1, (slab - 1) * width_x, width_x, 3, store_below)
    fill(2, 0, width_x, 2, store_above)


def inside(c, bounds_ref, z, slab, shape):
    def between(k, at):
        return jnp.where((at >= bounds_ref[k : k + 1, 0:1]) & (at < bounds_ref[k : k + 1, 1:2]), 1.0, 0.0)

    deep = jnp.full((1, shape[1]), lax.axis_index("gz") * slab + z, jnp.int32)
    line = lax.broadcasted_iota(jnp.int32, (shape[0], 1), 0) + c.at
    column = lax.broadcasted_iota(jnp.int32, (1, shape[1]), 1)
    return between(1, line) * (between(0, deep) * between(2, column))


def middle(
    cap,
    e_ref,
    forward_hbm,
    got_ref,
    h_ref,
    eps_hbm,
    sigma_hbm,
    chip0_hbm,
    chip1_hbm,
    far_hbm,
    timing_ref,
    bounds_ref,
    h2_ref,
    e2_ref,
    grad_ref,
    cb_ref,
    share_ref,
    forward_ref,
    eout_hbm,
    hout_hbm,
    gout_hbm,
    h1_ref,
    e1_ref,
    mat_ref,
    chip_ref,
    far_ref,
    own_ref,
    sbelow_ref,
    sabove_ref,
    fs,
    h2a,
    dza,
    sems,
    out_sems,
    odd_sems,
    even_sems,
):
    pairs = (
        (far_hbm, far_ref),
        (chip0_hbm, chip_ref.at[0:3]),
        (chip1_hbm, chip_ref.at[3:5]),
        (eps_hbm, mat_ref.at[0]),
        (sigma_hbm, mat_ref.at[1]),
        (forward_hbm, forward_ref),
    )
    copies = [pltpu.make_async_copy(a, b, sems.at[i]) for i, (a, b) in enumerate(pairs)]
    for copy in copies:
        copy.start()
    place_entries(cap, got_ref, own_ref, sbelow_ref, sabove_ref)
    over_rows(e_ref.shape[2], lambda c: magnetic_step(c, e_ref, h_ref, h1_ref))
    for copy in copies[:-1]:
        copy.wait()
    over_rows(e_ref.shape[2], lambda c: electric_all(c, e_ref, h1_ref, e1_ref, mat_ref))
    slab, width_x = e_ref.shape[1], e_ref.shape[2]
    top = slab - 1
    odd = odd_device()
    has_below = jnp.where(lax.axis_index("gz") > 0, 1.0, 0.0).astype(F32)
    wave0, wave1 = timing_ref[0:1, 0:1], timing_ref[0:1, 1:2]
    weight0, weight1 = timing_ref[1:2, 0:1], timing_ref[1:2, 1:2]

    def first(c):
        chip = [c.get(chip_ref, k) for k in range(3)]
        far = [c.get(far_ref, k) for k in range(3)]
        low = [jnp.where(odd, a, b) for a, b in zip(chip, far)]
        high = [jnp.where(odd, b, a) for a, b in zip(chip, far)]
        ex, ey = c.get(e_ref, 0, 0), c.get(e_ref, 1, 0)
        hax = has_below * (low[0] + HALF * ey)
        hay = has_below * (low[1] - HALF * ex)
        cb_a, cb_b = low[2], high[2]
        cb = [c.get(mat_ref, 1, z) for z in range(slab)]
        e1 = [
            [c.get(e1_ref, k, z) - wave0 * cb[z] * c.get(own_ref, k, z) for k in range(3)]
            for z in range(slab)
        ]
        e1[0][0] = e1[0][0] + cb[0] * hay
        e1[0][1] = e1[0][1] - cb[0] * hax
        hx = c.get(h1_ref, 0, top) + HALF * high[1]
        hy = c.get(h1_ref, 1, top) - HALF * high[0]
        c.put(h1_ref, 0, top, hx)
        c.put(h1_ref, 1, top, hy)
        bx_far, bx_chip = c.behind_x(far_ref, 0), c.behind_x(chip_ref, 0)
        bx = jnp.where(odd, bx_far, bx_chip)
        e1[top][0] = e1[top][0] + HALF * cb[top] * high[0]
        e1[top][1] = e1[top][1] + HALF * cb[top] * high[1]
        e1[top][2] = e1[top][2] - HALF * cb[top] * (bx + behind_y(high[1]))
        from_chip = [c.get(chip_ref, k) for k in (3, 4)]
        beside = [jnp.where(odd, 0.0, v) for v in from_chip]
        c.put(fs, 0, beside[0] + cb_b * (hy - wave0 * c.get(sabove_ref, 0)))
        c.put(fs, 1, beside[1] - cb_b * (hx + wave0 * c.get(sabove_ref, 1)))
        for z in range(slab):
            for k in range(3):
                c.put(e1_ref, k, z, e1[z][k])
        dx = cb_a * (HALF * ex - wave0 * c.get(sbelow_ref, 0))
        dy = cb_a * (HALF * ey - wave0 * c.get(sbelow_ref, 1))
        dz = -cb_a * (
            HALF * (c.behind_x(e_ref, 0, 0) + behind_y(ey)) + wave0 * c.get(sbelow_ref, 2)
        )
        c.put(dza, dz)
        beside = [jnp.where(odd, v, 0.0) for v in from_chip]
        c.put(h2a, 0, beside[0] + has_below * HALF * (ey - dy + e1[0][1] - ahead_y(dz)))
        c.put(h2a, 1, beside[1] + has_below * HALF * (dx - ex - e1[0][0]))

    over_rows(width_x, first)

    def second(c):
        c.put(h2a, 1, c.get(h2a, 1) + has_below * HALF * c.ahead_x(dza))
        for z in range(slab):
            ex, ey, ez = (c.get(e1_ref, k, z) for k in range(3))
            if z < top:
                up_x, up_y = c.get(e1_ref, 0, z + 1) - ex, c.get(e1_ref, 1, z + 1) - ey
            else:
                up_x, up_y = c.get(fs, 0) - ex, c.get(fs, 1) - ey
            hx, hy = c.get(h1_ref, 0, z), c.get(h1_ref, 1, z)
            c.put(h2_ref, 0, z, hx - HALF * (ahead_y(ez) - up_y))
            c.put(h2_ref, 1, z, hy - HALF * (up_x - c.ahead_x(e1_ref, 2, z)))
            hz = c.get(h1_ref, 2, z)
            c.put(h2_ref, 2, z, hz - HALF * (c.ahead_x(e1_ref, 1, z) - ahead_y(ex)))

    over_rows(width_x, second)

    def third(c):
        for z in range(slab):
            ca, cb = c.get(mat_ref, 0, z), c.get(mat_ref, 1, z)
            c.put(cb_ref, z, cb)
            hx, hy, hz = (c.get(h2_ref, k, z) for k in range(3))
            if z > 0:
                down_x, down_y = hx - c.get(h2_ref, 0, z - 1), hy - c.get(h2_ref, 1, z - 1)
            else:
                down_x, down_y = hx - c.get(h2a, 0), hy - c.get(h2a, 1)
            curl = (
                behind_y(hz) - down_y,
                down_x - c.behind_x(h2_ref, 2, z),
                c.behind_x(h2_ref, 1, z) - behind_y(hx),
            )
            dot1, dot2 = 0.0, 0.0
            for k in range(3):
                e1 = c.get(e1_ref, k, z)
                e2 = ca * e1 + cb * (curl[k] - wave1 * c.get(own_ref, k, z))
                c.put(e2_ref, k, z, e2)
                fwd = c.get(forward_ref, k, z)
                dot1 = dot1 + e1 * fwd
                dot2 = dot2 + e2 * fwd
            mask = inside(c, bounds_ref, z, slab, ca.shape)
            c.put(share_ref, z, weight1 * mask)
            c.put(grad_ref, z, mask * (weight0 * dot1 + weight1 * dot2))

    copies[-1].wait()

    def copies_of(pairs, sems):
        return [pltpu.make_async_copy(a, b, sems.at[i]) for i, (a, b) in enumerate(pairs)]

    done = copies_of(
        (
            (h2_ref.at[0:2, 0:top], hout_hbm.at[0:2, 0:top]),
            (h2_ref.at[2], hout_hbm.at[2]),
        ),
        out_sems,
    )
    for copy in done:
        copy.start()
    part = width_x // 2
    odd_copies, even_copies = [], []
    for g in range(2):
        over_rows(width_x, third, g * part, (g + 1) * part)
        rows = pl.ds(g * part, part)
        for_odd = copies_of(
            (
                (e2_ref.at[:, 0:top, rows], eout_hbm.at[:, 0:top, rows]),
                (grad_ref.at[0:top, rows], gout_hbm.at[0:top, rows]),
            ),
            odd_sems.at[g],
        )
        for_even = copies_of(
            (
                (e2_ref.at[:, 1:slab, rows], eout_hbm.at[:, 1:slab, rows]),
                (grad_ref.at[1:slab, rows], gout_hbm.at[1:slab, rows]),
                (h2_ref.at[0:2, top, rows], hout_hbm.at[0:2, top, rows]),
                (e2_ref.at[2, 0, rows], eout_hbm.at[2, 0, rows]),
            ),
            even_sems.at[g],
        )
        by_parity(lambda: start_all(for_odd), lambda: start_all(for_even))
        odd_copies, even_copies = odd_copies + for_odd, even_copies + for_even
    by_parity(lambda: wait_all(odd_copies), lambda: wait_all(even_copies))
    wait_all(done)


def last(
    forward_ref,
    h2_ref,
    e2_ref,
    gradp_ref,
    cb_ref,
    share_ref,
    far_ref,
    ein_hbm,
    hin_hbm,
    gin_hbm,
    eout_hbm,
    hout_hbm,
    grad_hbm,
    e_ref,
    h_ref,
    grad_ref,
    sems,
):
    slab, width_x = e2_ref.shape[1], e2_ref.shape[2]
    top = slab - 1
    part = width_x // PARTS

    def finish(c, z, deltas):
        dot = 0.0
        for k, delta in enumerate(deltas):
            dot = dot + delta * c.get(forward_ref, k, z)
            c.put(e_ref, k, c.get(e2_ref, k, z) + delta)
        c.put(grad_ref, c.get(gradp_ref, z) + c.get(share_ref, z) * dot)

    def above(c):
        fx, fy = c.get(far_ref, 0), c.get(far_ref, 1)
        cb = HALF * c.get(cb_ref, top)
        finish(c, top, (cb * fx, cb * fy, -cb * (c.behind_x(far_ref, 0) + behind_y(fy))))
        c.put(h_ref, 0, c.get(h2_ref, 0, top) + HALF * fy)
        c.put(h_ref, 1, c.get(h2_ref, 1, top) - HALF * fx)

    def below(c):
        cb = c.get(cb_ref, 0)
        finish(c, 0, (cb * c.get(far_ref, 1), -cb * c.get(far_ref, 0)))

    def run(z, body, comps, with_h):
        copies = []
        for g in range(PARTS):
            over_rows(width_x, body, g * part, (g + 1) * part)
            rows = pl.ds(g * part, part)
            pairs = [
                (e_ref.at[0:comps, rows], eout_hbm.at[0:comps, z, rows]),
                (grad_ref.at[rows], grad_hbm.at[z, rows]),
            ]
            if with_h:
                pairs.append((h_ref.at[:, rows], hout_hbm.at[0:2, z, rows]))
            for i, (a, b) in enumerate(pairs):
                copies.append(pltpu.make_async_copy(a, b, sems.at[g, i]))
                copies[-1].start()
        for copy in copies:
            copy.wait()

    by_parity(lambda: run(top, above, 3, True), lambda: run(0, below, 2, False))


def settle(near_hbm, far_hbm, out_hbm, near_ref, sem):
    copy = pltpu.make_async_copy(near_hbm.at[0, 0:8], near_ref, sem)
    copy.start()
    copy.wait()


def shape(*dims):
    return jax.ShapeDtypeStruct(dims, F32)


def kept(*dims):
    return VMEM(dims, F32)


def sent(*dims):
    return pltpu.HBM(dims, F32)


def call(body, outs, ins, us, limit, scratch=(), in_hbm=(), anywhere=(), aliases=None):
    def place(i, x):
        if i in in_hbm:
            return pl.BlockSpec(memory_space=pltpu.HBM)
        if i in anywhere:
            return pl.BlockSpec(memory_space=pl.ANY)
        return pl.BlockSpec(memory_space=VMEM)

    ins = [
        pltpu.with_memory_space_constraint(x, pltpu.HBM) if i in in_hbm else x
        for i, x in enumerate(ins)
    ]
    return pl.pallas_call(
        body,
        out_shape=outs,
        in_specs=[place(i, x) for i, x in enumerate(ins)],
        out_specs=jax.tree.map(
            lambda x: pl.BlockSpec(memory_space=getattr(x, "memory_space", VMEM)), outs
        ),
        input_output_aliases=aliases or {},
        scratch_shapes=list(scratch),
        compiler_params=pltpu.CompilerParams(vmem_limit_bytes=limit << 20),
        cost_estimate=pl.CostEstimate(flops=int(us * FLOPS_US), bytes_accessed=0, transcendentals=0),
    )(*ins)


def local(
    e_field,
    h_field,
    forward_field,
    permittivity,
    conductivity,
    owners,
    cells,
    amplitude,
    timing,
    bounds,
):
    slab, wx, wy = permittivity.shape
    peers = lax.axis_size("gz")
    rows = owners.shape[0]
    cap = 2 * rows // peers
    lanes = -(-3 * cap // LANES) * LANES
    cells_all = slab * wx * wy
    chip_pairs = [p for i in range(0, peers - 1, 2) for p in ((i, i + 1), (i + 1, i))]
    far_pairs = [p for i in range(1, peers - 1, 2) for p in ((i, i + 1), (i + 1, i))]

    layer, slabs, fields = (wx, wy), (slab, wx, wy), (3, slab, wx, wy)
    dma = pltpu.SemaphoreType.DMA
    begun = call(
        halves_first,
        sent(3, *layer),
        (e_field, h_field, permittivity, conductivity),
        2,
        56,
        scratch=(
            VMEM((3, *layer), F32),
            VMEM((2, *layer), F32),
            VMEM((2, *layer), F32),
            VMEM((3, *layer), F32),
            dma((PARTS, 4)),
            dma((PARTS,)),
        ),
        in_hbm=(0, 1, 2, 3),
    )
    far1 = lax.ppermute(begun, "gz", far_pairs)
    packed, chip0, chip1, far2 = call(
        functools.partial(halves_second, cap),
        (
            sent(peers, 4, lanes),
            sent(3, *layer),
            sent(2, *layer),
            sent(2, *layer),
        ),
        (
            e_field,
            h_field,
            permittivity,
            conductivity,
            owners.reshape(1, rows),
            cells.reshape(1, rows),
            amplitude,
            begun,
        ),
        3,
        16,
        scratch=(
            VMEM(fields, F32),
            VMEM(fields, F32),
            VMEM((2, *slabs), F32),
            VMEM((5, *layer), F32),
            VMEM((2, *layer), F32),
            VMEM((peers, 4, lanes), F32),
            dma((2,)),
            dma((1,)),
            dma((PARTS, 3)),
        ),
        in_hbm=(2, 3, 7),
    )
    got = lax.all_to_all(packed, "gz", 0, 0, tiled=True)
    far2 = call(
        settle,
        sent(2, *layer),
        (chip1, far2),
        3,
        8,
        scratch=(VMEM((8, wy), F32), dma),
        in_hbm=(0, 1),
        aliases={1: 0},
    )
    far2 = lax.ppermute(far2, "gz", far_pairs)
    chip0, chip1 = (
        lax.ppermute(x, "gz", chip_pairs) for x in (chip0, chip1)
    )
    h2, e2, grad, cb, share, forward, e_part, h_part, grad_part = call(
        functools.partial(middle, cap),
        (
            kept(*fields),
            kept(*fields),
            kept(*slabs),
            kept(*slabs),
            kept(*slabs),
            kept(*fields),
            sent(*fields),
            sent(*fields),
            sent(*slabs),
        ),
        (
            e_field,
            forward_field,
            got,
            h_field,
            permittivity,
            conductivity,
            chip0,
            chip1,
            far1,
            timing,
            bounds,
        ),
        6,
        24,
        scratch=(
            VMEM(fields, F32),
            VMEM(fields, F32),
            VMEM((2, *slabs), F32),
            VMEM((5, *layer), F32),
            VMEM((3, *layer), F32),
            VMEM(fields, F32),
            VMEM((3, *layer), F32),
            VMEM((2, *layer), F32),
            VMEM((2, *layer), F32),
            VMEM((2, *layer), F32),
            VMEM(layer, F32),
            dma((6,)),
            dma((2,)),
            dma((2, 2)),
            dma((2, 4)),
        ),
        in_hbm=(1, 4, 5, 6, 7),
        anywhere=(8,),
    )
    return call(
        last,
        (sent(*fields), sent(*fields), sent(*slabs)),
        (forward, h2, e2, grad, cb, share, far2, e_part, h_part, grad_part),
        2.5,
        16,
        scratch=(
            VMEM((3, *layer), F32),
            VMEM((2, *layer), F32),
            VMEM(layer, F32),
            dma((PARTS, 3)),
        ),
        in_hbm=(7, 8, 9),
        aliases={7: 0, 8: 1, 9: 2},
    )


def solution(mesh):
    placed = (
        P(None, "gz", "groups", None),
        P(None, "gz", "groups", None),
        P(None, "gz", "groups", None),
        P("gz", "groups", None),
        P("gz", "groups", None),
        P("gz", "groups"),
        P("gz", "groups"),
        P("groups", "gz"),
        P("groups", None),
        P("groups", None),
    )
    return jax.shard_map(
        local,
        mesh=mesh,
        in_specs=placed,
        out_specs=(
            P(None, "gz", "groups", None),
            P(None, "gz", "groups", None),
            P("gz", "groups", None),
        ),
        check_vma=False,
    )
```
